32 devices in a mesh: gx: 8 (over y, x, core), gy: 4 (over z).
Axes of the slice: x: 2, y: 2, z: 4, core: 2. Of those that a mesh axis runs over, the one named last changes fastest.
Arguments:
- soil_velocity: float32 [3, 32, 128, 512], P(None, None, 'gx', 'gy'), may hold values from -6 to 6
- soil_stress: float32 [6, 32, 128, 512], P(None, None, 'gx', 'gy'), may hold values from -6 to 6
- buoyancy: float32 [32, 128, 512], P(None, 'gx', 'gy'), may hold values from 0.5 to 1
- lame_first: float32 [32, 128, 512], P(None, 'gx', 'gy'), may hold values from 0.2 to 0.8
- shear_modulus: float32 [32, 128, 512], P(None, 'gx', 'gy'), may hold values from 0.1 to 0.6
- stiffness: bfloat16 [2048, 256, 256], P(('gx', 'gy')), may hold values from -1 to 5
- storey_drift: float32 [2048, 256], P(('gx', 'gy')), may hold values from -6 to 6
- drift_rate: float32 [2048, 256], P(('gx', 'gy')), may hold values from -6 to 6
- coupling: float32 [2048, 256], P(('gx', 'gy')), may hold values from 0.05 to 0.5
- contact: float32 [2048, 64], P(('gx', 'gy')), may hold values from 0.1 to 10
- dof_counts: int32 [2048], P(('gx', 'gy')), may hold values from 3 to 255, as said below
- owner_tile: int32 [2048, 1], P(('gx', 'gy')), may hold values from 0 to 31; in each aligned block of 64 rows (0 to 63, 64 to 127, ...) at most 2 rows name the same one
- corner_cell: int32 [2048], P(('gx', 'gy')), may hold values from 0 to 1088
Outputs:
- final_velocity: float32 [3, 32, 128, 512], P(None, None, 'gx', 'gy')
- final_drift: float32 [2048, 256], P(('gx', 'gy'))
- final_rate: float32 [2048, 256], P(('gx', 'gy'))
The draws below stay inside these ranges and needn't reach their ends.
Inputs may be any that keep to these rules, and one draw needn't show every extreme that they name: `dof_counts`: a multiple of 3; the first building of every device holds the most. `owner_tile`: the index of the tile's device along gx then gy; among the 64 buildings of one device no tile appears more than 2 times, and some tile appears exactly 2 times in some device's buildings; every tile holds some building. `corner_cell`: encodes the footprint's first cell within the owner tile as x * 121 + y, so that the whole footprint lies in that tile.
All inputs are finite; a program needn't handle non-finite values.
Results may differ from the reference program's by a relative error of at most 0.002.
Values sent between devices are 32-bit elements; how exact they have to be, the bound alone decides.
No kernel may reach another device: no remote copies, remote signals or barrier semaphores. Data moves between devices by JAX's collectives and lax.ppermute only.
A program may use at most 128 MiB of HBM per device.

```python
import math
import jax
import jax.numpy as jnp
import numpy as np
from jax import lax

LAYERS = 32
CX = 16
CY = 128
FOOT = 8
DOF = 256
BLD_DEV = 64
CAP = 2
NX = 128
NY = 512
BUILDINGS = 2048
DEVICES = 32


def draw_stiffness(key, part):
    diag_key, spread_key = jax.random.split(jax.random.fold_in(key, 17))
    diagonal = jax.random.uniform(diag_key, (BUILDINGS, DOF), jnp.float32, 1.0, 4.0)
    off_diag = jnp.clip(jax.random.normal(spread_key, (BUILDINGS, DOF, DOF), jnp.float32) * (0.5 / math.sqrt(DOF)), -0.5, 0.5)
    identity = jnp.arange(DOF)[:, None] == jnp.arange(DOF)[None, :]
    return jnp.where(identity[None], diagonal[:, :, None], off_diag).astype(jnp.bfloat16)


def draw_dof_counts(key, part):
    storeys = jax.random.randint(jax.random.fold_in(key, 23), (BUILDINGS,), 1, DOF // 3 + 1)
    leading = jnp.arange(BUILDINGS) % BLD_DEV == 0
    return (3 * jnp.where(leading, DOF // 3, storeys)).astype(jnp.int32)


def set_ends(values, rng, low, largest):
    shape = values.shape
    spot = [jax.random.randint(jax.random.fold_in(rng, axis), (), 0, shape[axis]) for axis in range(len(shape))]
    values = values.at[tuple(spot)].set(low)
    longest = shape.index(max(shape))
    spot[longest] = (spot[longest] + 1) % shape[longest]
    return values.at[tuple(spot)].set(largest)


def level_of(stream_key, shape, shards, least, high):
    def one(position, shards_of):
        heights = jax.random.uniform(jax.random.fold_in(jax.random.fold_in(stream_key, 6), position), (shards_of,), jnp.float32, least / len(shards), high / len(shards))
        return jnp.repeat(jnp.exp(heights), shape[position] // shards_of).reshape((-1,) + (1,) * (len(shape) - position - 1))

    factor_of = one(*shards[0])
    for cut in shards[1:]:
        factor_of = factor_of * one(*cut)
    return factor_of


def assign_block(key, own, number, rows, count, top, most, slope):
    ranking = jax.random.permutation(key, count)
    packed, ordinary = portions_of(count, rows * top, most, slope, True), portions_of(count, rows * top, most, slope, False)
    places = jnp.arange(count)

    def named(sizes, rotation):
        used = int((sizes > 0).sum())
        fixed = max(1, used // 4)
        moved = fixed + (places - fixed + rotation * (used - fixed)) % max(1, count - fixed)
        return jnp.zeros((count,), jnp.int32).at[ranking[jnp.where(places < fixed, places, moved)]].set(jnp.asarray(sizes, jnp.int32))

    sizes = jnp.where(number % 4 == 0, named(packed, number // 4), named(ordinary, number - number // 4 - 1))
    mixed = jax.random.permutation(jax.random.fold_in(own, 3), count)
    source_of, taker = mixed[0:count // 2 * 2:2], mixed[1:count // 2 * 2:2]
    slack = jnp.minimum(sizes[source_of] - 1, most - sizes[taker]) // 2
    slack = jnp.where((source_of == ranking[0]) | (taker == ranking[0]) | (sizes[taker] == 0), 0, jnp.maximum(slack, 0))
    moved = jax.random.randint(jax.random.fold_in(own, 4), (count // 2,), 0, 1 << 20) % (slack + 1)
    sizes = sizes.at[source_of].add(-moved).at[taker].add(moved)
    members = jnp.searchsorted(jnp.cumsum(sizes), jnp.arange(rows * top), side="right").astype(jnp.int32)
    grid = members.reshape(top, rows).T
    grid = grid[jax.random.permutation(jax.random.fold_in(own, 1), rows)]
    rotation = jax.random.randint(jax.random.fold_in(own, 2), (rows, 1), 0, top)
    return jnp.take_along_axis(grid, (jnp.arange(top)[None, :] + rotation) % top, axis=1)


def portions_of(count, total, limit, lean, full):
    portions = [(1 << 20) // math.isqrt(rank ** lean) + 1 for rank in range(1, count + 1)]
    largest = limit if full else min(limit, max(-(-total // count), total * portions[0] // sum(portions)))
    least = 1 if total - largest >= count - 1 else 0
    counts, rest = [largest] + [least] * (count - 1), total - largest - least * (count - 1)
    while rest > 0:
        candidates = [i for i in range(1, count) if counts[i] < largest] or [i for i in range(1, count) if counts[i] < limit]
        mass, left = sum([portions[i] for i in candidates]), rest
        for i in candidates:
            extra = min(limit - counts[i], max(1, left * portions[i] // mass), rest)
            counts[i] = counts[i] + extra
            rest = rest - extra
    return np.array(counts)


def gaussian(stream_key, extent, scale, most, pieces=(), kind=jnp.bfloat16):
    array = jax.random.normal(stream_key, extent, jnp.float32) * scale
    if len(pieces) > 0:
        array = level_of(stream_key, extent, pieces, -0.22, 0.18) * array
    return jnp.clip(array, min=-most, max=most).astype(kind)


def setup_inputs(seed: int = 0) -> dict:
    splits = jax.random.split(jax.random.key(seed), 14)
    soil_velocity = gaussian(splits[0], (3, LAYERS, NX, NY), 1.0, 6.0, ((2, 8), (3, 4)), jnp.float32)
    soil_stress = gaussian(splits[1], (6, LAYERS, NX, NY), 1.0, 6.0, ((2, 8), (3, 4)), jnp.float32)
    buoyancy = jnp.clip(jnp.exp(math.log(1.0) - 0.6931472 * jax.random.uniform(splits[2], (LAYERS, NX, NY), jnp.float32) ** level_of(splits[2], (LAYERS, NX, NY), ((1, 8), (2, 4)), -0.2, 0.2)), 0.5, 1.0)
    lame_first = jnp.clip(jnp.exp(math.log(0.8) - 1.3862944 * jax.random.uniform(splits[3], (LAYERS, NX, NY), jnp.float32) ** level_of(splits[3], (LAYERS, NX, NY), ((1, 8), (2, 4)), -0.2, 0.2)), 0.2, 0.8)
    shear_modulus = jnp.clip(jnp.exp(math.log(0.6) - 1.7917595 * jax.random.uniform(splits[4], (LAYERS, NX, NY), jnp.float32) ** level_of(splits[4], (LAYERS, NX, NY), ((1, 8), (2, 4)), -0.2, 0.2)), 0.1, 0.6)
    stiffness = draw_stiffness(jax.random.fold_in(splits[13], 71), 0)
    storey_drift = gaussian(splits[6], (BUILDINGS, DOF), 1.0, 6.0, ((0, 32),), jnp.float32)
    drift_rate = gaussian(splits[7], (BUILDINGS, DOF), 1.0, 6.0, ((0, 32),), jnp.float32)
    coupling = jnp.clip(jnp.exp(math.log(0.5) - 2.3025851 * jax.random.uniform(splits[8], (BUILDINGS, DOF), jnp.float32) ** level_of(splits[8], (BUILDINGS, DOF), ((0, 32),), -0.2, 0.2)), 0.05, 0.5)
    contact = jnp.clip(jnp.exp(math.log(10.0) - 4.6051702 * jax.random.uniform(splits[9], (BUILDINGS, FOOT * FOOT), jnp.float32) ** level_of(splits[9], (BUILDINGS, FOOT * FOOT), ((0, 32),), -0.2, 0.2)), 0.1, 10.0)
    dof_counts = draw_dof_counts(jax.random.fold_in(splits[13], 71), 0)
    owner_tile_keys = jax.random.split(jax.random.fold_in(splits[11], 1), BUILDINGS // BLD_DEV)
    owner_tile_turns = jax.random.permutation(jax.random.fold_in(splits[11], 3), BUILDINGS // BLD_DEV)
    owner_tile = jax.vmap(lambda own, number: assign_block(jax.random.fold_in(splits[11], 2), own, number, BLD_DEV, DEVICES, 1, CAP, 2))(owner_tile_keys, owner_tile_turns).reshape((BUILDINGS, 1))
    corner_cell = set_ends(jax.random.randint(splits[12], (BUILDINGS,), 0, (CX - FOOT + 1) * (CY - FOOT + 1)), jax.random.fold_in(splits[12], 1), 0, ((CX - FOOT + 1) * (CY - FOOT + 1)) - 1).astype(jnp.int32)
    return dict(soil_velocity=soil_velocity, soil_stress=soil_stress, buoyancy=buoyancy, lame_first=lame_first, shear_modulus=shear_modulus, stiffness=stiffness, storey_drift=storey_drift, drift_rate=drift_rate, coupling=coupling, contact=contact, dof_counts=dof_counts, owner_tile=owner_tile, corner_cell=corner_cell)


inner_coef = 9.0 / 8.0
outer_coef = 1.0 / 24.0
time_step = 0.3


def trim_axis(source, direction, amount):
    return lax.slice_in_dim(source, amount, source.shape[direction] - amount, axis=direction)


def derive(source, direction, forward):
    length = source.shape[direction] - 4

    def window(offset):
        return lax.slice_in_dim(source, offset, offset + length, axis=direction)

    if forward:
        return inner_coef * (window(3) - window(2)) - outer_coef * (window(4) - window(1))
    return inner_coef * (window(2) - window(1)) - outer_coef * (window(3) - window(0))


def gradient(source, direction, forward):
    result = derive(source, direction, forward)
    for other_axis in range(3):
        if other_axis != direction:
            result = trim_axis(result, other_axis, 2)
    return result


def neighbour(source, inside_x, inside_y, step_z, step_x, step_y):
    extent_x = source.shape[1]
    extent_y = source.shape[2]
    itself = source[:, 1:extent_x - 1, 1:extent_y - 1]
    shifted = source[:, 1 + step_x:extent_x - 1 + step_x, 1 + step_y:extent_y - 1 + step_y]
    usable = inside_x[1 + step_x:extent_x - 1 + step_x][None, :, None] & inside_y[1 + step_y:extent_y - 1 + step_y][None, None, :]
    if step_z:
        shifted = jnp.concatenate([shifted[1:], shifted[-1:]], axis=0)
        layer_ok = jnp.arange(source.shape[0]) < source.shape[0] - 1
        usable = usable & layer_ok[:, None, None]
    return jnp.where(usable, shifted, itself)


def mean_of(source, inside_x, inside_y, shifts):
    summed = neighbour(source, inside_x, inside_y, 0, 0, 0)
    for triple in shifts:
        summed = summed + neighbour(source, inside_x, inside_y, triple[0], triple[1], triple[2])
    return summed * (1.0 / (len(shifts) + 1))


def averages(buoy_field, lame_field, shear_field, inside_x, inside_y):
    buoy_avg = [mean_of(buoy_field, inside_x, inside_y, [(0, 1, 0)]),
                mean_of(buoy_field, inside_x, inside_y, [(0, 0, 1)]),
                mean_of(buoy_field, inside_x, inside_y, [(1, 0, 0)])]
    shear_avg = [mean_of(shear_field, inside_x, inside_y, [(0, 1, 0), (0, 0, 1), (0, 1, 1)]),
                 mean_of(shear_field, inside_x, inside_y, [(0, 1, 0), (1, 0, 0), (1, 1, 0)]),
                 mean_of(shear_field, inside_x, inside_y, [(0, 0, 1), (1, 0, 0), (1, 0, 1)])]
    return buoy_avg, lame_field[:, 1:-1, 1:-1], shear_field[:, 1:-1, 1:-1], shear_avg


def stress_update(speeds, stresses, lame_cell, shear_cell, shear_avg):
    stretch_x = gradient(speeds[0], 1, False)
    stretch_y = gradient(speeds[1], 2, False)
    stretch_z = gradient(speeds[2], 0, False)
    summed = stretch_x + stretch_y + stretch_z
    doubled = 2.0 * shear_cell
    return [
        stresses[0] + time_step * (lame_cell * summed + doubled * stretch_x),
        stresses[1] + time_step * (lame_cell * summed + doubled * stretch_y),
        stresses[2] + time_step * (lame_cell * summed + doubled * stretch_z),
        stresses[3] + time_step * shear_avg[0] * (gradient(speeds[0], 2, True) + gradient(speeds[1], 1, True)),
        stresses[4] + time_step * shear_avg[1] * (gradient(speeds[0], 0, True) + gradient(speeds[2], 1, True)),
        stresses[5] + time_step * shear_avg[2] * (gradient(speeds[1], 0, True) + gradient(speeds[2], 2, True)),
    ]


def velocity_update(speeds, stresses, buoy_avg):
    accel_x = gradient(stresses[0], 1, True) + gradient(stresses[3], 2, False) + gradient(stresses[4], 0, False)
    accel_y = gradient(stresses[3], 1, False) + gradient(stresses[1], 2, True) + gradient(stresses[5], 0, False)
    accel_z = gradient(stresses[4], 1, False) + gradient(stresses[5], 2, False) + gradient(stresses[2], 0, True)
    return [speeds[0] + time_step * buoy_avg[0] * accel_x,
            speeds[1] + time_step * buoy_avg[1] * accel_y,
            speeds[2] + time_step * buoy_avg[2] * accel_z]


def pad_cells(source, width_z, width_xy):
    return jnp.pad(source, ((width_z, width_z), (width_xy, width_xy), (width_xy, width_xy)))


def reference(soil_velocity, soil_stress, buoyancy, lame_first, shear_modulus, stiffness, storey_drift, drift_rate, coupling, contact, dof_counts, owner_tile, corner_cell):
    inside_x = jnp.pad(jnp.ones((NX,), dtype=jnp.bool_), 1)
    inside_y = jnp.pad(jnp.ones((NY,), dtype=jnp.bool_), 1)
    buoy_avg, lame_cell, shear_cell, shear_avg = averages(pad_cells(buoyancy, 0, 1), pad_cells(lame_first, 0, 1), pad_cells(shear_modulus, 0, 1), inside_x, inside_y)
    speeds = [soil_velocity[index] for index in range(3)]
    stresses = [soil_stress[index] for index in range(6)]
    dof_mask = jnp.arange(DOF)[None, :] < dof_counts[:, None]
    select = (jnp.arange(DOF)[:, None] % 3 == jnp.arange(3)[None, :]).astype(jnp.float32)
    drifts = jnp.where(dof_mask, storey_drift, 0.0)
    rates = jnp.where(dof_mask, drift_rate, 0.0)
    owners = owner_tile[:, 0]
    corner_span = CY - FOOT + 1
    tiles_y = NY // CY
    start_x = (owners // tiles_y) * CX + corner_cell // corner_span
    start_y = (owners % tiles_y) * CY + corner_cell % corner_span
    offsets = jnp.arange(FOOT)
    cell_index = ((start_x[:, None, None] + offsets[None, :, None]) * NY + start_y[:, None, None] + offsets[None, None, :]).reshape(BUILDINGS, FOOT * FOOT)
    weights = contact / jnp.sum(contact, axis=1, keepdims=True)
    for time_index in range(2):
        surface = jnp.stack([speeds[0][0], speeds[1][0], speeds[2][0]]).reshape(3, NX * NY)
        values = surface[:, cell_index]
        base_motion = jnp.sum(values * weights[None], axis=2).T
        relative = jnp.where(dof_mask, rates - jnp.dot(base_motion, select.T, precision=lax.Precision.HIGHEST), 0.0)
        rounded = drifts.astype(jnp.bfloat16)
        restoring = jnp.einsum("bij,bj->bi", stiffness.astype(jnp.float32), rounded.astype(jnp.float32))
        rates = jnp.where(dof_mask, rates - time_step * restoring - time_step * coupling * relative, 0.0)
        drifts = jnp.where(dof_mask, drifts + time_step * rates, 0.0)
        reaction = jnp.dot(coupling * relative, select, precision=lax.Precision.HIGHEST)
        cell_push = (time_step * FOOT) * reaction.T[:, :, None] * weights[None]
        forcing = jnp.zeros((3, NX * NY), jnp.float32).at[:, cell_index.reshape(-1)].add(cell_push.reshape(3, -1)).reshape(3, NX, NY)
        padded = [pad_cells(component_field, 2, 2) for component_field in speeds]
        stresses = stress_update(padded, stresses, lame_cell, shear_cell, shear_avg)
        stress_padded = [pad_cells(component_field, 2, 2) for component_field in stresses]
        speeds = velocity_update(speeds, stress_padded, buoy_avg)
        speeds = [speeds[index].at[0].add(forcing[index]) for index in range(3)]
    return jnp.stack(speeds), drifts, rates
```

```python
import jax
import jax.numpy as jnp
from jax import lax
from jax.experimental import pallas as pl
from jax.experimental.pallas import tpu as pltpu
from jax.sharding import PartitionSpec as P

FOOT = 8
CAP = 2
PAD = 8

near = 9.0 / 8.0
far = 1.0 / 24.0
time_step = 0.3
exact = lax.Precision.HIGHEST
f32 = jnp.float32

AT_X, AT_Y, AT_RATE, AT_COUPLING, AT_NEXT, AT_SQUARE = 64, 65, 66, 69, 72, 75


def call(kernel, name, outs, args, scratch=()):
    size = sum(a.size * a.dtype.itemsize for a in args) + sum(o.size * o.dtype.itemsize for o in outs)
    return pl.pallas_call(
        kernel,
        name=name,
        out_shape=outs,
        scratch_shapes=list(scratch),
        cost_estimate=pl.CostEstimate(flops=size, bytes_accessed=size, transcendentals=0),
        compiler_params=pltpu.CompilerParams(vmem_limit_bytes=32 * 2**20),
    )(*args)


def shape(*dims):
    return jax.ShapeDtypeStruct(dims, f32)


def ring(block, axis, step):
    size = lax.axis_size(axis)
    return lax.ppermute(block, axis, [(i, (i + step) % size) for i in range(size)])


def diagonal(block):
    nx, ny = lax.axis_size("gx"), lax.axis_size("gy")
    route = [
        (((i + 1) % nx) * ny + (j + 1) % ny, i * ny + j) for i in range(nx) for j in range(ny)
    ]
    return lax.ppermute(block, ("gx", "gy"), route)


def lanes_of(value):
    return lax.broadcasted_iota(jnp.int32, value.shape, len(value.shape) - 1)


def roll(value, amount):
    return pltpu.roll(value, amount % value.shape[-1], len(value.shape) - 1)


def packed(pieces):
    result = None
    for slab, first, count, amount in pieces:
        moved = roll(slab, amount) if amount else slab
        if result is None:
            result = moved
        else:
            lane = lanes_of(slab)
            result = jnp.where((lane >= first) & (lane < first + count), moved, result)
    return result


def send_columns(pack_ref, out_ref):
    rows, width = out_ref.shape
    for block in range(width // 128):
        part = pack_ref[block * 128 : (block + 1) * 128, :]
        out_ref[:, block * 128 : (block + 1) * 128] = part.T[:rows]


def receive_columns(south_ref, north_ref, from_south, south_ok, north_ok, out_ref):
    rows, width = south_ref.shape
    for block in range(width // 128):
        cut = slice(block * 128, (block + 1) * 128)
        south = jnp.where(south_ok, south_ref[:, cut], 0.0)
        north = jnp.where(north_ok, north_ref[:, cut], 0.0)
        row = lax.broadcasted_iota(jnp.int32, south.shape, 0)
        taken = row == from_south[0]
        for other in from_south[1:]:
            taken = taken | (row == other)
        part = jnp.where(taken, south, north)
        whole = jnp.concatenate([part, jnp.zeros((128 - rows, 128), f32)], axis=0)
        out_ref[cut, :] = whole.T


def slopes(f, ghost, forward):
    lane = lanes_of(f)
    last = f.shape[-1] - 1
    up1 = roll(jnp.where(lane == 0, ghost, f), -1)
    down1 = roll(jnp.where(lane == last, ghost, f), 1)
    if forward:
        up2 = roll(jnp.where(lane <= 1, ghost, f), -2)
        return near * (up1 - f) - far * (up2 - down1)
    down2 = roll(jnp.where(lane >= last - 1, ghost, f), 2)
    return near * (f - down1) - far * (up1 - down2)


def across(ext, c, x, forward, layers):
    def at(d):
        return ext[c, x + 2 + d, PAD : PAD + layers, :]

    if forward:
        return near * (at(1) - at(0)) - far * (at(2) - at(-1))
    return near * (at(0) - at(-1)) - far * (at(1) - at(-2))


def down(ext, c, x, forward, layers):
    def at(d):
        return ext[c, x + 2, PAD + d : PAD + layers + d, :]

    if forward:
        return near * (at(1) - at(0)) - far * (at(2) - at(-1))
    return near * (at(0) - at(-1)) - far * (at(1) - at(-2))


def place():
    gx, gy = lax.axis_index("gx"), lax.axis_index("gy")
    nx, ny = lax.axis_size("gx"), lax.axis_size("gy")
    return gx > 0, gx < nx - 1, gy > 0, gy < ny - 1


def fill(ext, c, source, src, size_x, layers):
    for x in range(size_x):
        ext[c, x + 2, 0:PAD, :] = jnp.zeros((PAD, 128), f32)
        ext[c, x + 2, PAD : PAD + layers, :] = source[src, x * layers : (x + 1) * layers, :]
        ext[c, x + 2, PAD + layers : PAD + layers + PAD, :] = jnp.zeros((PAD, 128), f32)


def first_kernel(layers, v_ref, b_ref, m_ref, vt_ref, up_ref, dn_ref, col_ref, pack):
    size_x = v_ref.shape[1] // layers

    for x in range(size_x):
        cut = pl.ds(x * layers, layers)
        slab = [v_ref[c, pl.ds(x, layers, stride=size_x), :] for c in range(3)]
        buoy = b_ref[pl.ds(x, layers, stride=size_x), :]
        shear = m_ref[pl.ds(x, layers, stride=size_x), :]
        for c in range(3):
            vt_ref[c, cut, :] = slab[c]
        pack[cut, :] = packed(
            [
                (slab[0], 0, 3, 1),
                (slab[1], 3, 3, 5),
                (slab[2], 6, 3, 7),
                (buoy, 9, 1, 9),
                (shear, 10, 1, 10),
            ]
        )
        if x == 0:
            dn_ref[0] = slab[0]
            dn_ref[1] = slab[1]
            dn_ref[3] = slab[2]
            dn_ref[5] = buoy
            dn_ref[6] = shear
        if x == 1:
            dn_ref[2] = slab[1]
            dn_ref[4] = slab[2]
        if x == size_x - 2:
            up_ref[0] = slab[0]
        if x == size_x - 1:
            for c in range(3):
                up_ref[1 + c] = slab[c]
    send_columns(pack, col_ref)


def material_kernel(
    layers, b_ref, l_ref, m_ref, east_ref, north_ref, diag_ref, out_ref, bs, ms, tb, tm, cols
):
    size_x = b_ref.shape[0] // layers
    _, east_ok, _, north_ok = place()
    receive_columns(north_ref, north_ref, (0,), north_ok, north_ok, cols)
    inner = slice(PAD, PAD + layers)
    for x in range(size_x):
        bs[x, inner, :] = b_ref[pl.ds(x, layers, stride=size_x), :]
        ms[x, inner, :] = m_ref[pl.ds(x, layers, stride=size_x), :]
        part = cols[x * layers : (x + 1) * layers, :]
        tb[x, inner, :] = roll(part, -9)
        tm[x, inner, :] = roll(part, -10)
    bs[size_x, inner, :] = east_ref[5]
    ms[size_x, inner, :] = east_ref[6]
    tm[size_x, inner, :] = diag_ref[...]
    zero = jnp.zeros((PAD, 128), f32)
    for x in range(size_x + 1):
        bs[x, PAD + layers : PAD + layers + PAD, :] = zero
        ms[x, PAD + layers : PAD + layers + PAD, :] = zero
        tm[x, PAD + layers : PAD + layers + PAD, :] = zero
    below = slice(PAD + 1, PAD + layers + 1)

    def step(x, carry):
        cut = pl.ds(pl.multiple_of(x * layers, layers), layers)
        b, m = bs[x, inner, :], ms[x, inner, :]
        lane = lanes_of(b)
        layer = lax.broadcasted_iota(jnp.int32, b.shape, 0)
        in_x = (x < size_x - 1) | east_ok
        in_y = (lane < 127) | north_ok
        in_z = layer < layers - 1

        def north(value, ghost):
            return roll(jnp.where(lane == 0, ghost, value), -1)

        b_e = jnp.where(in_x, bs[x + 1, inner, :], b)
        b_n = jnp.where(in_y, north(b, tb[x, inner, :]), b)
        b_z = jnp.where(in_z, bs[x, below, :], b)
        m_e = jnp.where(in_x, ms[x + 1, inner, :], m)
        m_n = jnp.where(in_y, north(m, tm[x, inner, :]), m)
        m_z = jnp.where(in_z, ms[x, below, :], m)
        m_en = jnp.where(in_y & in_x, north(ms[x + 1, inner, :], tm[x + 1, inner, :]), m)
        m_ez = jnp.where(in_z & in_x, ms[x + 1, below, :], m)
        m_nz = jnp.where(in_z & in_y, north(ms[x, below, :], tm[x, below, :]), m)
        out_ref[0, cut, :] = time_step * l_ref[pl.ds(x, layers, stride=size_x), :]
        out_ref[1, cut, :] = (2.0 * time_step) * m
        out_ref[2, cut, :] = (0.25 * time_step) * (m + m_e + m_n + m_en)
        out_ref[3, cut, :] = (0.25 * time_step) * (m + m_e + m_z + m_ez)
        out_ref[4, cut, :] = (0.25 * time_step) * (m + m_n + m_z + m_nz)
        out_ref[5, cut, :] = (0.5 * time_step) * (b + b_e)
        out_ref[6, cut, :] = (0.5 * time_step) * (b + b_n)
        out_ref[7, cut, :] = (0.5 * time_step) * (b + b_z)
        return carry

    lax.fori_loop(0, size_x, step, 0)


def stress_kernel(
    layers,
    first,
    v_ref,
    s_ref,
    mat_ref,
    west_ref,
    east_ref,
    south_ref,
    north_ref,
    out_ref,
    up_ref,
    dn_ref,
    col_ref,
    ext,
    cols,
    pack,
):
    size_x = v_ref.shape[1] // layers
    west_ok, east_ok, south_ok, north_ok = place()
    receive_columns(south_ref, north_ref, (0, 3, 4, 6), south_ok, north_ok, cols)
    for c in range(3):
        fill(ext, c, v_ref, c, size_x, layers)
    inner = slice(PAD, PAD + layers)
    for row, c, x in ((0, 0, 0), (1, 0, 1), (2, 1, 1), (3, 2, 1)):
        ext[c, x, inner, :] = jnp.where(west_ok, west_ref[row], 0.0)
    for row, c, x in ((0, 0, 0), (1, 1, 0), (2, 1, 1), (3, 2, 0), (4, 2, 1)):
        ext[c, size_x + 2 + x, inner, :] = jnp.where(east_ok, east_ref[row], 0.0)

    def step(x, carry):
        cut = pl.ds(pl.multiple_of(x * layers, layers), layers)
        ghost = cols[cut, :]
        vx, vy, vz = [ext[c, x + 2, inner, :] for c in range(3)]
        gx, gy, gz = roll(ghost, -1), roll(ghost, -5), roll(ghost, -7)

        def old(c):
            if first:
                return s_ref[c, pl.ds(x, layers, stride=size_x), :]
            return s_ref[c, cut, :]

        dx = across(ext, 0, x, False, layers)
        dy = slopes(vy, gy, False)
        dz = down(ext, 2, x, False, layers)
        both = mat_ref[0, cut, :] * (dx + dy + dz)
        twice = mat_ref[1, cut, :]
        xx = old(0) + (both + twice * dx)
        yy = old(1) + (both + twice * dy)
        zz = old(2) + (both + twice * dz)
        xy = old(3) + mat_ref[2, cut, :] * (
            slopes(vx, gx, True) + across(ext, 1, x, True, layers)
        )
        xz = old(4) + mat_ref[3, cut, :] * (
            down(ext, 0, x, True, layers) + across(ext, 2, x, True, layers)
        )
        yz = old(5) + mat_ref[4, cut, :] * (
            down(ext, 1, x, True, layers) + slopes(vz, gz, True)
        )
        for c, value in enumerate((xx, yy, zz, xy, xz, yz)):
            out_ref[c, cut, :] = value
        pack[cut, :] = packed([(yy, 0, 3, 1), (xy, 3, 3, 5), (yz, 6, 3, 8)])
        return carry

    lax.fori_loop(0, size_x, step, 0)
    send_columns(pack, col_ref)

    def slab(c, x):
        return out_ref[c, x * layers : (x + 1) * layers, :]

    for row, (c, x) in enumerate(((0, 1), (3, 2), (3, 1), (4, 2), (4, 1))):
        up_ref[row] = slab(c, size_x - x)
    for row, (c, x) in enumerate(((0, 0), (0, 1), (3, 0), (4, 0))):
        dn_ref[row] = slab(c, x)


def velocity_kernel(
    layers,
    last,
    v_ref,
    s_ref,
    mat_ref,
    west_ref,
    east_ref,
    south_ref,
    north_ref,
    push_ref,
    *refs,
):
    if last:
        out_ref, ext, cols = refs
    else:
        out_ref, up_ref, dn_ref, col_ref, ext, cols, pack = refs
    size_x = v_ref.shape[1] // layers
    west_ok, east_ok, south_ok, north_ok = place()
    receive_columns(south_ref, north_ref, (0, 3, 4, 6, 7), south_ok, north_ok, cols)
    for c, src in enumerate((0, 3, 4, 5, 2)):
        fill(ext, c, s_ref, src, size_x, layers)
    inner = slice(PAD, PAD + layers)
    for row, c, x in ((0, 0, 1), (1, 1, 0), (2, 1, 1), (3, 2, 0), (4, 2, 1)):
        ext[c, x, inner, :] = jnp.where(west_ok, west_ref[row], 0.0)
    for row, c, x in ((0, 0, 0), (1, 0, 1), (2, 1, 0), (3, 2, 0)):
        ext[c, size_x + 2 + x, inner, :] = jnp.where(east_ok, east_ref[row], 0.0)

    def step(x, carry):
        cut = pl.ds(pl.multiple_of(x * layers, layers), layers)
        ghost = cols[cut, :]
        yy, xy, yz = s_ref[1, cut, :], ext[1, x + 2, inner, :], ext[3, x + 2, inner, :]
        gyy, gxy, gyz = roll(ghost, -1), roll(ghost, -5), roll(ghost, -8)
        ax = across(ext, 0, x, True, layers) + slopes(xy, gxy, False) + down(ext, 2, x, False, layers)
        ay = across(ext, 1, x, False, layers) + slopes(yy, gyy, True) + down(ext, 3, x, False, layers)
        az = across(ext, 2, x, False, layers) + slopes(yz, gyz, False) + down(ext, 4, x, True, layers)
        layer = lax.broadcasted_iota(jnp.int32, yy.shape, 0)
        fresh = []
        for c, accel in enumerate((ax, ay, az)):
            pushed = jnp.where(layer == 0, push_ref[c, pl.ds(x, 1), :], 0.0)
            fresh.append(v_ref[c, cut, :] + mat_ref[5 + c, cut, :] * accel + pushed)
        if last:
            for c in range(3):
                out_ref[c, pl.ds(x, layers, stride=size_x), :] = fresh[c]
        else:
            for c in range(3):
                out_ref[c, cut, :] = fresh[c]
            pack[cut, :] = packed([(fresh[0], 0, 3, 1), (fresh[1], 3, 3, 5), (fresh[2], 6, 3, 7)])
        return carry

    lax.fori_loop(0, size_x, step, 0)
    if last:
        return
    send_columns(pack, col_ref)

    def slab(c, x):
        return out_ref[c, x * layers : (x + 1) * layers, :]

    for row, (c, x) in enumerate(((0, 2), (0, 1), (1, 1), (2, 1))):
        up_ref[row] = slab(c, size_x - x)
    for row, (c, x) in enumerate(((0, 0), (1, 0), (1, 1), (2, 0), (2, 1))):
        dn_ref[row] = slab(c, x)


def third(value, e):
    d = lanes_of(value).astype(f32)
    return d - 3.0 * jnp.floor((d + 0.5) * (1.0 / 3.0)) == e


def column(row):
    n = row.shape[1]
    same = lax.broadcasted_iota(jnp.int32, (n, n), 0) == lax.broadcasted_iota(jnp.int32, (n, n), 1)
    return jnp.sum(jnp.where(same, row, 0.0), axis=1, keepdims=True)


def table_kernel(
    span,
    pull_ref,
    drift_ref,
    rate_ref,
    coupling_ref,
    contact_ref,
    counts_ref,
    owner_ref,
    corner_ref,
    out_ref,
    slot_ref,
    base_ref,
):
    number, width = rate_ref.shape
    slots = out_ref.shape[0]
    counts = column(counts_ref[...].astype(f32))
    mask = lax.broadcasted_iota(jnp.int32, (number, width), 1).astype(f32) < counts
    rate = jnp.where(mask, rate_ref[...], 0.0)
    coupling = jnp.where(mask, coupling_ref[...], 0.0)
    base = jnp.where(
        mask, rate - time_step * pull_ref[...] - time_step * coupling * rate, 0.0
    )
    base_ref[...] = base
    contact = contact_ref[...]
    weights = contact / jnp.sum(contact, axis=1, keepdims=True)
    corner = column(corner_ref[...].astype(f32))
    start_x = jnp.floor((corner + 0.5) * (1.0 / span))
    start_y = corner - start_x * span
    row = jnp.concatenate([weights, jnp.zeros((number, 128 - weights.shape[1]), f32)], axis=1)
    lane = lanes_of(row)
    row = jnp.where(lane == AT_X, start_x, row)
    row = jnp.where(lane == AT_Y, start_y, row)
    sums = (
        (AT_RATE, coupling * rate),
        (AT_COUPLING, coupling),
        (AT_NEXT, coupling * base),
        (AT_SQUARE, time_step * coupling * coupling),
    )
    for at, value in sums:
        for e in range(3):
            total = jnp.sum(jnp.where(third(value, e), value, 0.0), axis=1, keepdims=True)
            row = jnp.where(lane == at + e, total, row)
    owner = owner_ref[...].astype(f32)
    owner_col = column(owner)
    same = owner_col == owner
    i = lax.broadcasted_iota(jnp.int32, same.shape, 0)
    j = lax.broadcasted_iota(jnp.int32, same.shape, 1)
    slot_row = owner * CAP + jnp.sum(jnp.where(same & (i < j), 1.0, 0.0), axis=0, keepdims=True)
    slot_col = owner_col * CAP + jnp.sum(jnp.where(same & (j < i), 1.0, 0.0), axis=1, keepdims=True)
    to_slot = lax.broadcasted_iota(jnp.int32, (slots, number), 0).astype(f32) == slot_row
    of_slot = lax.broadcasted_iota(jnp.int32, (number, slots), 1).astype(f32) == slot_col
    slot_ref[...] = jnp.where(of_slot, 1.0, 0.0)
    out_ref[...] = jnp.dot(
        jnp.where(to_slot, 1.0, 0.0), row, precision=exact, preferred_element_type=f32
    )


def motion(maps_ref, v_ref, layers):
    size_x, slots, size_y = maps_ref.shape
    total = [jnp.zeros((slots, size_y), f32) for _ in range(3)]
    for x in range(size_x):
        part = maps_ref[x]
        for c in range(3):
            total[c] = total[c] + part * v_ref[c, x * layers : x * layers + 1, :]
    return [jnp.sum(t, axis=1, keepdims=True) for t in total]


def spread(maps_ref, reaction, out_ref):
    size_x = maps_ref.shape[0]
    for x in range(size_x):
        part = maps_ref[x]
        for c in range(3):
            out_ref[c, x : x + 1, :] = jnp.sum(part * reaction[c], axis=0, keepdims=True)


def surface_kernel(layers, table_ref, v_ref, maps_ref, moved_ref, push_ref):
    size_x = maps_ref.shape[0]
    table = table_ref[...]
    lane = lanes_of(table)
    off_y = lane - table[:, AT_Y : AT_Y + 1].astype(jnp.int32)
    start_x = table[:, AT_X : AT_X + 1]
    within = (off_y >= 0) & (off_y < FOOT)
    inside = jnp.where(within, off_y, 0)
    lines = []
    for a in range(FOOT):
        picked = jnp.take_along_axis(table, inside + a * FOOT, axis=1)
        lines.append(jnp.where(within, picked, 0.0))
    for x in range(size_x):
        value = jnp.zeros(table.shape, f32)
        for a in range(FOOT):
            value = jnp.where(start_x == float(x - a), lines[a], value)
        maps_ref[x] = value
    moved = motion(maps_ref, v_ref, layers)
    reaction = []
    rows = jnp.zeros(table.shape, f32)
    for c in range(3):
        rest, slope = (table[:, at + c : at + c + 1] for at in (AT_RATE, AT_COUPLING))
        reaction.append(time_step * FOOT * (rest - slope * moved[c]))
        rows = jnp.where(lane == c, moved[c], rows)
    moved_ref[...] = rows
    spread(maps_ref, reaction, push_ref)


def surface_again_kernel(layers, table_ref, v_ref, maps_ref, before_ref, moved_ref, push_ref):
    table, before = table_ref[...], before_ref[...]
    lane = lanes_of(table)
    moved = motion(maps_ref, v_ref, layers)
    reaction = []
    rows = before
    for c in range(3):
        rest, square, slope = (
            table[:, at + c : at + c + 1] for at in (AT_NEXT, AT_SQUARE, AT_COUPLING)
        )
        rest = rest + square * before[:, c : c + 1]
        reaction.append(time_step * FOOT * (rest - slope * moved[c]))
        rows = jnp.where(lane == 3 + c, moved[c], rows)
    moved_ref[...] = rows
    spread(maps_ref, reaction, push_ref)


def spread_thirds(moved, at, value):
    result = jnp.zeros(value.shape, f32)
    for e in range(3):
        result = jnp.where(third(value, e), moved[:, at + e : at + e + 1], result)
    return result


def halfway_kernel(
    moved_ref, slot_ref, base_ref, drift_ref, coupling_ref, counts_ref, rate_out, drift_out, m_out
):
    moved = jnp.dot(slot_ref[...], moved_ref[...], precision=exact, preferred_element_type=f32)
    m_out[...] = moved
    coupling = coupling_ref[...]
    counts = column(counts_ref[...].astype(f32))
    mask = lanes_of(coupling).astype(f32) < counts
    rate = base_ref[...] + time_step * coupling * spread_thirds(moved, 0, coupling)
    rate = jnp.where(mask, rate, 0.0)
    rate_out[...] = rate
    drift_out[...] = jnp.where(mask, drift_ref[...] + time_step * rate, 0.0)


def end_kernel(
    moved_ref, rate_ref, drift_ref, pull_ref, coupling_ref, counts_ref, drift_out, rate_out
):
    coupling = coupling_ref[...]
    counts = column(counts_ref[...].astype(f32))
    mask = lanes_of(coupling).astype(f32) < counts
    rate = rate_ref[...]
    relative = rate - spread_thirds(moved_ref[...], 3, coupling)
    rate = rate - time_step * pull_ref[...] - time_step * coupling * relative
    rate = jnp.where(mask, rate, 0.0)
    rate_out[...] = rate
    drift_out[...] = jnp.where(mask, drift_ref[...] + time_step * rate, 0.0)


def trade(rows):
    devices = lax.axis_size("gx") * lax.axis_size("gy")
    blocks = rows.reshape(devices, CAP, rows.shape[1])
    blocks = lax.all_to_all(blocks, ("gx", "gy"), split_axis=0, concat_axis=0, tiled=True)
    return blocks.reshape(rows.shape)


def pull_of(stiffness, drift):
    return jnp.einsum(
        "bij,bj->bi", stiffness, drift.astype(jnp.bfloat16), preferred_element_type=f32
    )


def body(
    soil_velocity,
    soil_stress,
    buoyancy,
    lame_first,
    shear_modulus,
    stiffness,
    storey_drift,
    drift_rate,
    coupling,
    contact,
    dof_counts,
    owner_tile,
    corner_cell,
):
    layers, size_x, size_y = buoyancy.shape
    cells = layers * size_x
    number, width = storey_drift.shape
    slots = lax.axis_size("gx") * lax.axis_size("gy") * CAP
    span = size_y - FOOT + 1
    v = soil_velocity.reshape(3, cells, size_y)
    s = soil_stress.reshape(6, cells, size_y)
    buoy, lame, shear = (a.reshape(cells, size_y) for a in (buoyancy, lame_first, shear_modulus))
    counts, owner, corner = (a.reshape(1, number) for a in (dof_counts, owner_tile, corner_cell))

    def bind(kernel, *fixed):
        def bound(*refs):
            kernel(*fixed, *refs)

        return bound

    def vm(*dims):
        return pltpu.VMEM(dims, f32)

    field = vm(cells, size_y)
    tall = layers + 2 * PAD
    vt, up, dn, col = call(
        bind(first_kernel, layers),
        "edges",
        (shape(3, cells, size_y), shape(4, layers, size_y), shape(7, layers, size_y), shape(16, cells)),
        (v, buoy, shear),
        [field],
    )

    def exchange(up, dn, col):
        west = ring(up, "gx", 1)
        east = ring(dn, "gx", -1)
        south = ring(col, "gy", 1)
        north = ring(col, "gy", -1)
        return west, east, south, north

    halo = exchange(up, dn, col)
    corner_rows = diagonal(dn[6])
    counted = jnp.arange(width)[None, :] < dof_counts[:, None]
    pull = pull_of(stiffness, jnp.where(counted, storey_drift, 0.0))
    table, of_slot, base = call(
        bind(table_kernel, span),
        "table",
        (shape(slots, 128), shape(number, slots), shape(number, width)),
        (pull, storey_drift, drift_rate, coupling, contact, counts, owner, corner),
    )
    table = trade(table)
    (material,) = call(
        bind(material_kernel, layers),
        "material",
        (shape(8, cells, size_y),),
        (buoy, lame, shear, halo[1], halo[3], corner_rows),
        [vm(size_x + 1, tall, size_y) for _ in range(4)] + [field],
    )

    def stress_step(first, v, s, halo):
        return call(
            bind(stress_kernel, layers, first),
            "stress",
            (
                shape(6, cells, size_y),
                shape(5, layers, size_y),
                shape(4, layers, size_y),
                shape(16, cells),
            ),
            (v, s, material, *halo),
            [vm(3, size_x + 4, tall, size_y), field, field],
        )

    def velocity_step(last, v, s, halo, push):
        outs = [shape(3, cells, size_y)]
        scratch = [vm(5, size_x + 4, tall, size_y), field]
        if not last:
            outs += [shape(4, layers, size_y), shape(5, layers, size_y), shape(16, cells)]
            scratch += [field]
        return call(
            bind(velocity_kernel, layers, last),
            "velocity",
            tuple(outs),
            (v, s, material, *halo, push),
            scratch,
        )

    st, up, dn, col = stress_step(True, vt, s, halo)
    halo = exchange(up, dn, col)
    maps, moved, push = call(
        bind(surface_kernel, layers),
        "surface",
        (shape(size_x, slots, size_y), shape(slots, 128), shape(3, size_x, size_y)),
        (table, vt),
    )
    vt, up, dn, col = velocity_step(False, vt, st, halo, push)
    halo = exchange(up, dn, col)
    moved, push = call(
        bind(surface_again_kernel, layers),
        "surface_again",
        (shape(slots, 128), shape(3, size_x, size_y)),
        (table, vt, maps, moved),
    )
    moved = trade(moved)
    st, up, dn, col = stress_step(False, vt, st, halo)
    halo = exchange(up, dn, col)
    rate, drift, moved = call(
        halfway_kernel,
        "halfway",
        (shape(number, width), shape(number, width), shape(number, 128)),
        (moved, of_slot, base, storey_drift, coupling, counts),
    )
    pull = pull_of(stiffness, drift)
    drift, rate = call(
        end_kernel,
        "end",
        (shape(number, width), shape(number, width)),
        (moved, rate, drift, pull, coupling, counts),
    )
    (v,) = velocity_step(True, vt, st, halo, push)
    return v.reshape(soil_velocity.shape), drift, rate


def solution(mesh):
    both = ("gx", "gy")
    soil = P(None, None, "gx", "gy")
    cell = P(None, "gx", "gy")
    placed = (
        soil,
        soil,
        cell,
        cell,
        cell,
        P(both, None, None),
        P(both, None),
        P(both, None),
        P(both, None),
        P(both, None),
        P(both),
        P(both, None),
        P(both),
    )
    return jax.shard_map(
        body,
        mesh=mesh,
        in_specs=placed,
        out_specs=(soil, P(both, None), P(both, None)),
        check_vma=False,
    )
```

```python
import jax
import jax.numpy as jnp
from jax import lax
from jax.experimental import pallas as pl
from jax.experimental.pallas import tpu as pltpu
from jax.sharding import PartitionSpec as P

FOOT = 8
CAP = 2
PAD = 8
STRIP = 8

near = 9.0 / 8.0
far = 1.0 / 24.0
time_step = 0.3
exact = lax.Precision.HIGHEST
f32 = jnp.float32

AT_X, AT_Y, AT_RATE, AT_COUPLING, AT_SQUARE, AT_CORNER = 64, 65, 66, 69, 72, 75
FIRST, SECOND, AT_NEXT = 0, 3, 8


COSTS = {
    "first": 30_000_000,
    "load": 20_000_000,
    "material": 10_000_000,
    "stress": 25_000_000,
    "surface": 10_000_000,
    "pull": 30_000_000,
    "velocity": 25_000_000,
    "motion_again": 10_000_000,
    "finish": 60_000_000,
}


class Far:
    def __init__(self, value):
        self.value = value


def call(kernel, name, outs, args, scratch=(), far_outs=()):
    cost = COSTS[name]
    specs, values = [], []
    for a in args:
        far = isinstance(a, Far)
        a = a.value if far else a
        values.append(pltpu.with_memory_space_constraint(a, pltpu.HBM if far else pltpu.VMEM))
        specs.append(pl.BlockSpec(memory_space=pl.ANY if far else pltpu.VMEM))
    return pl.pallas_call(
        kernel,
        name=name,
        out_shape=outs,
        in_specs=specs,
        out_specs=tuple(
            pl.BlockSpec(memory_space=pl.ANY if i in far_outs else pltpu.VMEM)
            for i in range(len(outs))
        ),
        scratch_shapes=list(scratch),
        cost_estimate=pl.CostEstimate(flops=cost, bytes_accessed=cost, transcendentals=0),
        compiler_params=pltpu.CompilerParams(vmem_limit_bytes=16 * 2**20),
    )(*values)


def shape(*dims):
    return jax.ShapeDtypeStruct(dims, f32)


def near_by(*dims, dtype=f32):
    return pltpu.VMEM(dims, dtype)


def fetch(sources, targets, sems):
    copies = [
        pltpu.make_async_copy(source, target, sems.at[i])
        for i, (source, target) in enumerate(zip(sources, targets))
    ]
    for copy in copies:
        copy.start()
    return copies


def ring(block, axis, step):
    size = lax.axis_size(axis)
    return lax.ppermute(block, axis, [(i, (i + step) % size) for i in range(size)])


def lanes_of(value):
    return lax.broadcasted_iota(jnp.int32, value.shape, len(value.shape) - 1)


def roll(value, amount):
    return pltpu.roll(value, amount % value.shape[-1], len(value.shape) - 1)


def packed(pieces):
    result = None
    for slab, first, count, amount in pieces:
        moved = roll(slab, amount) if amount else slab
        if result is None:
            result = moved
        else:
            lane = lanes_of(slab)
            result = jnp.where((lane >= first) & (lane < first + count), moved, result)
    return result


def send_columns(pack_ref, out_ref):
    rows, width = out_ref.shape
    for block in range(width // 128):
        part = pack_ref[block * 128 : (block + 1) * 128, :]
        out_ref[:, block * 128 : (block + 1) * 128] = part.T[:rows]


def receive_columns(south_ref, north_ref, from_south, south_ok, north_ok, out_ref):
    rows, width = south_ref.shape
    for block in range(width // 128):
        cut = slice(block * 128, (block + 1) * 128)
        south = jnp.where(south_ok, south_ref[:, cut], 0.0)
        north = jnp.where(north_ok, north_ref[:, cut], 0.0)
        row = lax.broadcasted_iota(jnp.int32, south.shape, 0)
        taken = row == from_south[0]
        for other in from_south[1:]:
            taken = taken | (row == other)
        part = jnp.where(taken, south, north)
        whole = jnp.concatenate([part, jnp.zeros((128 - rows, 128), f32)], axis=0)
        out_ref[cut, :] = whole.T


def slopes(f, ghost, forward):
    lane = lanes_of(f)
    last = f.shape[-1] - 1
    up1 = roll(jnp.where(lane == 0, ghost, f), -1)
    down1 = roll(jnp.where(lane == last, ghost, f), 1)
    if forward:
        up2 = roll(jnp.where(lane <= 1, ghost, f), -2)
        return near * (up1 - f) - far * (up2 - down1)
    down2 = roll(jnp.where(lane >= last - 1, ghost, f), 2)
    return near * (f - down1) - far * (up1 - down2)


def across(ext, c, x, forward, layers):
    def at(d):
        return ext[c, x + 2 + d, PAD : PAD + layers, :]

    if forward:
        return near * (at(1) - at(0)) - far * (at(2) - at(-1))
    return near * (at(0) - at(-1)) - far * (at(1) - at(-2))


def down(ext, c, x, forward, layers):
    def at(d):
        return ext[c, x + 2, PAD + d : PAD + layers + d, :]

    if forward:
        return near * (at(1) - at(0)) - far * (at(2) - at(-1))
    return near * (at(0) - at(-1)) - far * (at(1) - at(-2))


def place():
    gx, gy = lax.axis_index("gx"), lax.axis_index("gy")
    nx, ny = lax.axis_size("gx"), lax.axis_size("gy")
    return gx > 0, gx < nx - 1, gy > 0, gy < ny - 1


def fill(ext, c, source, src, size_x, layers):
    for x in range(size_x):
        ext[c, x + 2, 0:PAD, :] = jnp.zeros((PAD, 128), f32)
        ext[c, x + 2, PAD : PAD + layers, :] = source[src, x * layers : (x + 1) * layers, :]
        ext[c, x + 2, PAD + layers : PAD + layers + PAD, :] = jnp.zeros((PAD, 128), f32)


def edges(layers, v_ref, b_ref, m_ref, vt_ref, bt_ref, mt_ref, up_ref, dn_ref, col_ref, pack):
    size_x = v_ref.shape[1] // layers
    for x in range(size_x):
        cut = pl.ds(x * layers, layers)
        slab = [v_ref[c, pl.ds(x, layers, stride=size_x), :] for c in range(3)]
        buoy = b_ref[pl.ds(x, layers, stride=size_x), :]
        shear = m_ref[pl.ds(x, layers, stride=size_x), :]
        for c in range(3):
            vt_ref[c, cut, :] = slab[c]
        bt_ref[cut, :] = buoy
        mt_ref[cut, :] = shear
        pack[cut, :] = packed(
            [
                (slab[0], 0, 3, 1),
                (slab[1], 3, 3, 5),
                (slab[2], 6, 3, 7),
                (buoy, 9, 1, 9),
                (shear, 10, 1, 10),
            ]
        )
        if x == 0:
            dn_ref[0] = slab[0]
            dn_ref[1] = slab[1]
            dn_ref[3] = slab[2]
            dn_ref[5] = buoy
            dn_ref[6] = shear
        if x == 1:
            dn_ref[2] = slab[1]
            dn_ref[4] = slab[2]
        if x == size_x - 2:
            up_ref[0] = slab[0]
        if x == size_x - 1:
            for c in range(3):
                up_ref[1 + c] = slab[c]
    send_columns(pack, col_ref)


def load_kernel(layers, s_hbm, l_hbm, st_ref, lt_ref, s_ref, l_ref, sems):
    size_x = l_ref.shape[0] // layers
    sources = [s_hbm.at[c] for c in range(6)] + [l_hbm]
    targets = [s_ref.at[c] for c in range(6)] + [l_ref]
    copies = fetch(sources, targets, sems)
    for c, copy in enumerate(copies):
        copy.wait()
        for x in range(size_x):
            cut = pl.ds(x * layers, layers)
            if c < 6:
                st_ref[c, cut, :] = s_ref[c, pl.ds(x, layers, stride=size_x), :]
            else:
                lt_ref[cut, :] = l_ref[pl.ds(x, layers, stride=size_x), :]


def material_kernel(
    layers, b_ref, l_ref, m_ref, east_ref, north_ref, table_ref, out_ref, bs, ms, tb, tm, cols
):
    size_x = b_ref.shape[0] // layers
    _, east_ok, _, north_ok = place()
    nx, ny = lax.axis_size("gx"), lax.axis_size("gy")
    beyond = lax.rem(lax.axis_index("gx") + 1, nx) * ny + lax.rem(lax.axis_index("gy") + 1, ny)
    receive_columns(north_ref, north_ref, (0,), north_ok, north_ok, cols)
    inner = slice(PAD, PAD + layers)
    for x in range(size_x):
        cut = slice(x * layers, (x + 1) * layers)
        bs[x, inner, :] = b_ref[cut, :]
        ms[x, inner, :] = m_ref[cut, :]
        part = cols[cut, :]
        tb[x, inner, :] = roll(part, -9)
        tm[x, inner, :] = roll(part, -10)
    bs[size_x, inner, :] = east_ref[5]
    ms[size_x, inner, :] = east_ref[6]
    line = jnp.broadcast_to(table_ref[pl.ds(beyond * CAP, 1), :], (layers, 128))
    own = lanes_of(line) - AT_CORNER == lax.broadcasted_iota(jnp.int32, line.shape, 0)
    corner = jnp.sum(jnp.where(own, line, 0.0), axis=1, keepdims=True)
    tm[size_x, inner, :] = jnp.broadcast_to(corner, line.shape)
    zero = jnp.zeros((PAD, 128), f32)
    for x in range(size_x + 1):
        bs[x, PAD + layers : PAD + layers + PAD, :] = zero
        ms[x, PAD + layers : PAD + layers + PAD, :] = zero
        tm[x, PAD + layers : PAD + layers + PAD, :] = zero
    below = slice(PAD + 1, PAD + layers + 1)

    def step(x, carry):
        cut = pl.ds(pl.multiple_of(x * layers, layers), layers)
        b, m = bs[x, inner, :], ms[x, inner, :]
        lane = lanes_of(b)
        layer = lax.broadcasted_iota(jnp.int32, b.shape, 0)
        in_x = (x < size_x - 1) | east_ok
        in_y = (lane < 127) | north_ok
        in_z = layer < layers - 1

        def north(value, ghost):
            return roll(jnp.where(lane == 0, ghost, value), -1)

        b_e = jnp.where(in_x, bs[x + 1, inner, :], b)
        b_n = jnp.where(in_y, north(b, tb[x, inner, :]), b)
        b_z = jnp.where(in_z, bs[x, below, :], b)
        m_e = jnp.where(in_x, ms[x + 1, inner, :], m)
        m_n = jnp.where(in_y, north(m, tm[x, inner, :]), m)
        m_z = jnp.where(in_z, ms[x, below, :], m)
        m_en = jnp.where(in_y & in_x, north(ms[x + 1, inner, :], tm[x + 1, inner, :]), m)
        m_ez = jnp.where(in_z & in_x, ms[x + 1, below, :], m)
        m_nz = jnp.where(in_z & in_y, north(ms[x, below, :], tm[x, below, :]), m)
        out_ref[0, cut, :] = time_step * l_ref[cut, :]
        out_ref[1, cut, :] = (2.0 * time_step) * m
        out_ref[2, cut, :] = (0.25 * time_step) * (m + m_e + m_n + m_en)
        out_ref[3, cut, :] = (0.25 * time_step) * (m + m_e + m_z + m_ez)
        out_ref[4, cut, :] = (0.25 * time_step) * (m + m_n + m_z + m_nz)
        out_ref[5, cut, :] = (0.5 * time_step) * (b + b_e)
        out_ref[6, cut, :] = (0.5 * time_step) * (b + b_n)
        out_ref[7, cut, :] = (0.5 * time_step) * (b + b_z)
        return carry

    lax.fori_loop(0, size_x, step, 0, unroll=4)


def stress_kernel(
    layers,
    first,
    v_ref,
    s_ref,
    mat_ref,
    west_ref,
    east_ref,
    south_ref,
    north_ref,
    out_ref,
    up_ref,
    dn_ref,
    col_ref,
    *refs,
):
    if first:
        kept_hbm, ext, cols, pack, sems = refs
        keep = pltpu.make_async_copy(mat_ref, kept_hbm, sems.at[0])
        keep.start()
    else:
        ext, cols, pack = refs
    size_x = v_ref.shape[1] // layers
    west_ok, east_ok, south_ok, north_ok = place()
    receive_columns(south_ref, north_ref, (0, 3, 4, 6), south_ok, north_ok, cols)
    for c in range(3):
        fill(ext, c, v_ref, c, size_x, layers)
    inner = slice(PAD, PAD + layers)
    for row, c, x in ((0, 0, 0), (1, 0, 1), (2, 1, 1), (3, 2, 1)):
        ext[c, x, inner, :] = jnp.where(west_ok, west_ref[row], 0.0)
    for row, c, x in ((0, 0, 0), (1, 1, 0), (2, 1, 1), (3, 2, 0), (4, 2, 1)):
        ext[c, size_x + 2 + x, inner, :] = jnp.where(east_ok, east_ref[row], 0.0)

    def step(x, carry):
        cut = pl.ds(pl.multiple_of(x * layers, layers), layers)
        ghost = cols[cut, :]
        vx, vy, vz = [ext[c, x + 2, inner, :] for c in range(3)]
        gx, gy, gz = roll(ghost, -1), roll(ghost, -5), roll(ghost, -7)

        def old(c):
            return s_ref[c, cut, :]

        dx = across(ext, 0, x, False, layers)
        dy = slopes(vy, gy, False)
        dz = down(ext, 2, x, False, layers)
        both = mat_ref[0, cut, :] * (dx + dy + dz)
        twice = mat_ref[1, cut, :]
        xx = old(0) + (both + twice * dx)
        yy = old(1) + (both + twice * dy)
        zz = old(2) + (both + twice * dz)
        xy = old(3) + mat_ref[2, cut, :] * (
            slopes(vx, gx, True) + across(ext, 1, x, True, layers)
        )
        xz = old(4) + mat_ref[3, cut, :] * (
            down(ext, 0, x, True, layers) + across(ext, 2, x, True, layers)
        )
        yz = old(5) + mat_ref[4, cut, :] * (
            down(ext, 1, x, True, layers) + slopes(vz, gz, True)
        )
        for c, value in enumerate((xx, yy, zz, xy, xz, yz)):
            out_ref[c, cut, :] = value
        pack[cut, :] = packed([(yy, 0, 3, 1), (xy, 3, 3, 5), (yz, 6, 3, 8)])
        return carry

    lax.fori_loop(0, size_x, step, 0, unroll=4)
    send_columns(pack, col_ref)

    def slab(c, x):
        return out_ref[c, x * layers : (x + 1) * layers, :]

    for row, (c, x) in enumerate(((0, 1), (3, 2), (3, 1), (4, 2), (4, 1))):
        up_ref[row] = slab(c, size_x - x)
    for row, (c, x) in enumerate(((0, 0), (0, 1), (3, 0), (4, 0))):
        dn_ref[row] = slab(c, x)
    if first:
        keep.wait()


def velocity_kernel(
    layers,
    last,
    v_ref,
    s_ref,
    mat_ref,
    west_ref,
    east_ref,
    south_ref,
    north_ref,
    push_ref,
    *refs,
):
    if last:
        out_hbm, out_ref, ext, cols, sems = refs
    else:
        out_ref, up_ref, dn_ref, col_ref, ext, cols, pack = refs
    size_x = v_ref.shape[1] // layers
    parts = size_x // STRIP
    west_ok, east_ok, south_ok, north_ok = place()
    receive_columns(south_ref, north_ref, (0, 3, 4, 6, 7), south_ok, north_ok, cols)
    for c, src in enumerate((0, 3, 4, 5, 2)):
        fill(ext, c, s_ref, src, size_x, layers)
    inner = slice(PAD, PAD + layers)
    for row, c, x in ((0, 0, 1), (1, 1, 0), (2, 1, 1), (3, 2, 0), (4, 2, 1)):
        ext[c, x, inner, :] = jnp.where(west_ok, west_ref[row], 0.0)
    for row, c, x in ((0, 0, 0), (1, 0, 1), (2, 1, 0), (3, 2, 0)):
        ext[c, size_x + 2 + x, inner, :] = jnp.where(east_ok, east_ref[row], 0.0)

    def step(x, carry):
        cut = pl.ds(pl.multiple_of(x * layers, layers), layers)
        ghost = cols[cut, :]
        yy, xy, yz = s_ref[1, cut, :], ext[1, x + 2, inner, :], ext[3, x + 2, inner, :]
        gyy, gxy, gyz = roll(ghost, -1), roll(ghost, -5), roll(ghost, -8)
        ax = across(ext, 0, x, True, layers) + slopes(xy, gxy, False) + down(ext, 2, x, False, layers)
        ay = across(ext, 1, x, False, layers) + slopes(yy, gyy, True) + down(ext, 3, x, False, layers)
        az = across(ext, 2, x, False, layers) + slopes(yz, gyz, False) + down(ext, 4, x, True, layers)
        layer = lax.broadcasted_iota(jnp.int32, yy.shape, 0)
        fresh = []
        for c, accel in enumerate((ax, ay, az)):
            pushed = jnp.where(layer == 0, push_ref[c, pl.ds(x, 1), :], 0.0)
            fresh.append(v_ref[c, cut, :] + mat_ref[5 + c, cut, :] * accel + pushed)
        if last:
            for c in range(3):
                out_ref[x // STRIP, c, :, lax.rem(x, STRIP), :] = fresh[c]
        else:
            for c in range(3):
                out_ref[c, cut, :] = fresh[c]
            pack[cut, :] = packed([(fresh[0], 0, 3, 1), (fresh[1], 3, 3, 5), (fresh[2], 6, 3, 7)])
        return carry

    leaving = []
    for part in range(parts):
        lax.fori_loop(part * STRIP, (part + 1) * STRIP, step, 0, unroll=4)
        if last:
            leaving += fetch(
                [out_ref.at[part]], [out_hbm.at[:, :, part]], sems.at[pl.ds(part, 1)]
            )
    for copy in leaving:
        copy.wait()
    if last:
        return
    send_columns(pack, col_ref)

    def slab(c, x):
        return out_ref[c, x * layers : (x + 1) * layers, :]

    for row, (c, x) in enumerate(((0, 2), (0, 1), (1, 1), (2, 1))):
        up_ref[row] = slab(c, size_x - x)
    for row, (c, x) in enumerate(((0, 0), (1, 0), (1, 1), (2, 0), (2, 1))):
        dn_ref[row] = slab(c, x)


def third(value, e):
    d = lanes_of(value).astype(f32)
    return d - 3.0 * jnp.floor((d + 0.5) * (1.0 / 3.0)) == e


def column(row):
    n = row.shape[1]
    same = lax.broadcasted_iota(jnp.int32, (n, n), 0) == lax.broadcasted_iota(jnp.int32, (n, n), 1)
    return jnp.sum(jnp.where(same, row, 0.0), axis=1, keepdims=True)


def slot_table(owner_ref, slots):
    number = owner_ref.shape[1]
    owner = owner_ref[...].astype(f32)
    owner_col = column(owner)
    same = owner_col == owner
    i = lax.broadcasted_iota(jnp.int32, same.shape, 0)
    j = lax.broadcasted_iota(jnp.int32, same.shape, 1)
    slot_row = owner * CAP + jnp.sum(jnp.where(same & (i < j), 1.0, 0.0), axis=0, keepdims=True)
    slot_col = owner_col * CAP + jnp.sum(jnp.where(same & (j < i), 1.0, 0.0), axis=1, keepdims=True)
    to_slot = lax.broadcasted_iota(jnp.int32, (slots, number), 0).astype(f32) == slot_row
    of_slot = lax.broadcasted_iota(jnp.int32, (number, slots), 1).astype(f32) == slot_col
    return jnp.where(to_slot, 1.0, 0.0), jnp.where(of_slot, 1.0, 0.0)


def counted(counts_ref, shape):
    return lax.broadcasted_iota(jnp.int32, shape, 1).astype(f32) < column(
        counts_ref[...].astype(f32)
    )


def table(
    span,
    rate_ref,
    coupling_ref,
    contact_ref,
    counts_ref,
    owner_ref,
    corner_ref,
    out_ref,
):
    number, width = rate_ref.shape
    slots = out_ref.shape[0]
    mask = counted(counts_ref, (number, width))
    rate = jnp.where(mask, rate_ref[...], 0.0)
    coupling = jnp.where(mask, coupling_ref[...], 0.0)
    contact = contact_ref[...]
    weights = contact / jnp.sum(contact, axis=1, keepdims=True)
    corner = column(corner_ref[...].astype(f32))
    start_x = jnp.floor((corner + 0.5) * (1.0 / span))
    start_y = corner - start_x * span
    row = jnp.concatenate([weights, jnp.zeros((number, 128 - weights.shape[1]), f32)], axis=1)
    lane = lanes_of(row)
    row = jnp.where(lane == AT_X, start_x, row)
    row = jnp.where(lane == AT_Y, start_y, row)
    sums = (
        (AT_RATE, coupling * rate),
        (AT_COUPLING, coupling),
        (AT_SQUARE, time_step * coupling * coupling),
    )
    row = sums_by_third(row, sums)
    to_slot, _ = slot_table(owner_ref, slots)
    out_ref[...] = jnp.dot(to_slot, row, precision=exact, preferred_element_type=f32)


def first_kernel(layers, span, *refs):
    far, outs, scratch = refs[:9], refs[9:16], refs[16:]
    near, pack, sems = scratch[:9], scratch[9], scratch[10]
    copies = fetch(far, near, sems)
    for copy in copies[3:]:
        copy.wait()
    table(span, *near[3:], outs[6])
    for copy in copies[:3]:
        copy.wait()
    edges(layers, *near[:3], *outs[:6], pack)
    first = outs[2][pl.ds(0, layers), 0:1]
    spot = lax.broadcasted_iota(jnp.int32, (layers, 128), 1) - AT_CORNER
    own = spot == lax.broadcasted_iota(jnp.int32, (layers, 128), 0)
    outs[6][...] += jnp.sum(jnp.where(own, first, 0.0), axis=0, keepdims=True)


def sums_by_third(row, sums):
    lane = lanes_of(row)
    for at, value in sums:
        for e in range(3):
            total = jnp.sum(jnp.where(third(value, e), value, 0.0), axis=1, keepdims=True)
            row = jnp.where(lane == at + e, total, row)
    return row


def products(stiff_ref, drift_ref, out_ref, begin, end):
    group = 16
    for g in range(begin // group * group, end, group):
        rounded = drift_ref[g : g + group, :].astype(jnp.bfloat16)
        row = lax.broadcasted_iota(jnp.int32, rounded.shape, 0)
        low, high = max(g, begin), min(g + group, end)
        total = out_ref[g : g + group, :]
        for b in range(low, high):
            part = lax.dot_general(
                rounded, stiff_ref[b], (((1,), (1,)), ((), ())), preferred_element_type=f32
            )
            total = jnp.where(row == b - g, part, total)
        out_ref[g : g + group, :] = total


def pull_kernel(
    stiff_ref,
    raw_ref,
    rate_ref,
    coupling_ref,
    counts_ref,
    owner_ref,
    base_ref,
    drift_out,
    next_ref,
    pull,
):
    number = drift_out.shape[0]
    mask = counted(counts_ref, drift_out.shape)
    drift_out[...] = jnp.where(mask, raw_ref[...], 0.0)
    pull[...] = jnp.zeros(pull.shape, f32)
    products(stiff_ref, drift_out, pull, 0, number)
    rate = jnp.where(mask, rate_ref[...], 0.0)
    coupling = jnp.where(mask, coupling_ref[...], 0.0)
    base = rate - time_step * pull[...] - time_step * coupling * rate
    base = jnp.where(mask, base, 0.0)
    base_ref[...] = base
    row = sums_by_third(jnp.zeros((number, 128), f32), ((AT_NEXT, coupling * base),))
    to_slot, _ = slot_table(owner_ref, next_ref.shape[0])
    next_ref[...] = jnp.dot(to_slot, row, precision=exact, preferred_element_type=f32)


def motion(maps_ref, v_ref, layers):
    size_x, slots, size_y = maps_ref.shape
    total = [jnp.zeros((slots, size_y), f32) for _ in range(3)]
    for x in range(size_x):
        part = maps_ref[x]
        for c in range(3):
            total[c] = total[c] + part * v_ref[c, x * layers : x * layers + 1, :]
    return [jnp.sum(t, axis=1, keepdims=True) for t in total]


def spread(at, reaction, out_ref):
    for x in range(out_ref.shape[1]):
        part = at(x)
        for c in range(3):
            out_ref[c, x : x + 1, :] = jnp.sum(part * reaction[c], axis=0, keepdims=True)


def footprints(table):
    lane = lanes_of(table)
    off_y = lane - table[:, AT_Y : AT_Y + 1].astype(jnp.int32)
    start_x = jnp.broadcast_to(table[:, AT_X : AT_X + 1], table.shape)
    within = (off_y >= 0) & (off_y < FOOT)
    inside = jnp.where(within, off_y, 0)
    lines = []
    for a in range(FOOT):
        picked = jnp.take_along_axis(table, inside + a * FOOT, axis=1)
        lines.append(jnp.where(within, picked, 0.0))

    def at(x):
        value = jnp.zeros(table.shape, f32)
        for a in range(FOOT):
            value = jnp.where(start_x == float(x - a), lines[a], value)
        return value

    return at


def surface_kernel(layers, table_ref, v_ref, maps_ref, moved_ref, push_ref):
    table = table_ref[...]
    lane = lanes_of(table)
    at = footprints(table)
    for x in range(maps_ref.shape[0]):
        maps_ref[x] = at(x)
    moved = motion(maps_ref, v_ref, layers)
    reaction = []
    rows = jnp.zeros(table.shape, f32)
    for c in range(3):
        rest, slope = (table[:, at + c : at + c + 1] for at in (AT_RATE, AT_COUPLING))
        reaction.append(time_step * FOOT * (rest - slope * moved[c]))
        rows = jnp.where(lane == FIRST + c, moved[c], rows)
    moved_ref[...] = rows
    spread(lambda x: maps_ref[x], reaction, push_ref)


def spread_thirds(moved, at, value):
    result = jnp.zeros(value.shape, f32)
    for e in range(3):
        result = jnp.where(third(value, e), moved[:, at + e : at + e + 1], result)
    return result


def motion_again_kernel(layers, v_ref, maps_ref, before_ref, next_ref, out_ref):
    moved = motion(maps_ref, v_ref, layers)
    rows = before_ref[...] + next_ref[...]
    lane = lanes_of(rows)
    for c in range(3):
        rows = jnp.where(lane == SECOND + c, moved[c], rows)
    out_ref[...] = rows


def finish_kernel(
    sent_ref,
    back_ref,
    table_ref,
    base_ref,
    drift_ref,
    coupling_ref,
    counts_ref,
    owner_ref,
    stiff_hbm,
    push_ref,
    drift_out,
    rate_out,
    half,
    pull,
    stiff_ref,
    sems,
):
    chunks = sems.shape[0]
    size = half.shape[0] // chunks
    strips = [pl.ds(c * size, size) for c in range(chunks)]
    copies = fetch([stiff_hbm.at[c] for c in strips], [stiff_ref.at[c] for c in strips], sems)
    table, sent, back = table_ref[...], sent_ref[...], back_ref[...]
    reaction = []
    for c in range(3):
        rest = back[:, AT_NEXT + c : AT_NEXT + c + 1]
        rest = rest + table[:, AT_SQUARE + c : AT_SQUARE + c + 1] * sent[:, FIRST + c : FIRST + c + 1]
        slope = table[:, AT_COUPLING + c : AT_COUPLING + c + 1]
        reaction.append(time_step * FOOT * (rest - slope * sent[:, SECOND + c : SECOND + c + 1]))
    spread(footprints(table), reaction, push_ref)
    _, of_slot = slot_table(owner_ref, back.shape[0])
    moved = jnp.dot(of_slot, back, precision=exact, preferred_element_type=f32)
    coupling = coupling_ref[...]
    mask = counted(counts_ref, coupling.shape)
    rate = base_ref[...] + time_step * coupling * spread_thirds(moved, FIRST, coupling)
    rate = jnp.where(mask, rate, 0.0)
    drift = jnp.where(mask, drift_ref[...] + time_step * rate, 0.0)
    half[...] = drift
    pull[...] = jnp.zeros(pull.shape, f32)
    for c in range(chunks):
        copies[c].wait()
        products(stiff_ref, half, pull, c * size, (c + 1) * size)
    relative = rate - spread_thirds(moved, SECOND, coupling)
    rate = rate - time_step * pull[...] - time_step * coupling * relative
    rate = jnp.where(mask, rate, 0.0)
    rate_out[...] = rate
    drift_out[...] = jnp.where(mask, drift + time_step * rate, 0.0)


def trade(rows):
    devices = lax.axis_size("gx") * lax.axis_size("gy")
    blocks = rows.reshape(devices, CAP, rows.shape[1])
    blocks = lax.all_to_all(blocks, ("gx", "gy"), split_axis=0, concat_axis=0, tiled=True)
    return blocks.reshape(rows.shape)


def body(
    soil_velocity,
    soil_stress,
    buoyancy,
    lame_first,
    shear_modulus,
    stiffness,
    storey_drift,
    drift_rate,
    coupling,
    contact,
    dof_counts,
    owner_tile,
    corner_cell,
):
    layers, size_x, size_y = buoyancy.shape
    cells = layers * size_x
    number, width = storey_drift.shape
    slots = lax.axis_size("gx") * lax.axis_size("gy") * CAP
    span = size_y - FOOT + 1
    v = soil_velocity.reshape(3, cells, size_y)
    s = soil_stress.reshape(6, cells, size_y)
    buoy, lame, shear = (a.reshape(cells, size_y) for a in (buoyancy, lame_first, shear_modulus))
    counts, owner, corner = (a.reshape(1, number) for a in (dof_counts, owner_tile, corner_cell))

    def bind(kernel, *fixed):
        def bound(*refs):
            kernel(*fixed, *refs)

        return bound

    def vm(*dims):
        return pltpu.VMEM(dims, f32)

    field = vm(cells, size_y)
    tall = layers + 2 * PAD
    plane = near_by(number, width)
    dma = pltpu.SemaphoreType.DMA
    far = (v, buoy, shear, drift_rate, coupling, contact, counts, owner, corner)
    outs = call(
        bind(first_kernel, layers, span),
        "first",
        (
            near_by(3, cells, size_y),
            near_by(cells, size_y),
            near_by(cells, size_y),
            near_by(4, layers, size_y),
            near_by(7, layers, size_y),
            near_by(16, cells),
            near_by(slots, 128),
        ),
        [Far(a) for a in far],
        [pltpu.VMEM(a.shape, a.dtype) for a in far] + [field, dma((len(far),))],
    )
    vt, bt, mt, up, dn, col, rows = outs

    def exchange(up, dn, col):
        west = ring(up, "gx", 1)
        east = ring(dn, "gx", -1)
        south = ring(col, "gy", 1)
        north = ring(col, "gy", -1)
        return west, east, south, north

    halo = exchange(up, dn, col)
    rows = trade(rows)
    parts = size_x // STRIP
    st, lt = call(
        bind(load_kernel, layers),
        "load",
        (near_by(6, cells, size_y), near_by(cells, size_y)),
        (Far(s), Far(lame)),
        [vm(6, cells, size_y), field, dma((7,))],
    )
    (material,) = call(
        bind(material_kernel, layers),
        "material",
        (near_by(8, cells, size_y),),
        (bt, lt, mt, halo[1], halo[3], rows),
        [vm(size_x + 1, tall, size_y) for _ in range(4)] + [field],
    )

    def stress_step(first, v, s, material, halo):
        outs = [
            near_by(6, cells, size_y),
            near_by(5, layers, size_y),
            near_by(4, layers, size_y),
            near_by(16, cells),
        ]
        scratch = [vm(3, size_x + 4, tall, size_y), field, field]
        if first:
            outs += [pltpu.HBM((8, cells, size_y), f32)]
            scratch += [dma((1,))]
        return call(
            bind(stress_kernel, layers, first),
            "stress",
            tuple(outs),
            (v, s, material, *halo),
            scratch,
            far_outs=(4,),
        )

    def velocity_step(last, v, s, material, halo, push):
        scratch = [vm(5, size_x + 4, tall, size_y), field]
        if last:
            outs = [pltpu.HBM((3, layers, parts, STRIP, size_y), f32)]
            scratch = [vm(parts, 3, layers, STRIP, size_y)] + scratch + [dma((parts,))]
        else:
            outs = [near_by(3, cells, size_y)]
            outs += [near_by(4, layers, size_y), near_by(5, layers, size_y), near_by(16, cells)]
            scratch += [field]
        return call(
            bind(velocity_kernel, layers, last),
            "velocity",
            tuple(outs),
            (v, s, material, *halo, push),
            scratch,
            far_outs=(0,) if last else (),
        )

    st, up, dn, col, kept = stress_step(True, vt, st, material, halo)
    halo = exchange(up, dn, col)
    maps, moved, push = call(
        bind(surface_kernel, layers),
        "surface",
        (near_by(size_x, slots, size_y), near_by(slots, 128), near_by(3, size_x, size_y)),
        (rows, vt),
    )
    base, drift, following = call(
        pull_kernel,
        "pull",
        (plane, plane, near_by(slots, 128)),
        (stiffness, storey_drift, drift_rate, coupling, counts, owner),
        [vm(number, width)],
    )
    push, following = lax.optimization_barrier((push, following))
    vt, up, dn, col = velocity_step(False, vt, st, material, halo, push)
    halo = exchange(up, dn, col)
    (sent,) = call(
        bind(motion_again_kernel, layers),
        "motion_again",
        (near_by(slots, 128),),
        (vt, maps, moved, following),
    )
    vt, sent = lax.optimization_barrier((vt, sent))
    back = trade(sent)
    st, up, dn, col = stress_step(False, vt, st, kept, halo)
    halo = exchange(up, dn, col)
    sent, st = lax.optimization_barrier((sent, st))
    chunks = 8 if number % 8 == 0 else 1
    push, drift, rate = call(
        finish_kernel,
        "finish",
        (near_by(3, size_x, size_y), shape(number, width), shape(number, width)),
        (sent, back, rows, base, drift, coupling, counts, owner, Far(stiffness)),
        [
            vm(number, width),
            vm(number, width),
            pltpu.VMEM(stiffness.shape, stiffness.dtype),
            dma((chunks,)),
        ],
    )
    (v,) = velocity_step(True, vt, st, kept, halo, push)
    return v.reshape(soil_velocity.shape), drift, rate


def solution(mesh):
    both = ("gx", "gy")
    soil = P(None, None, "gx", "gy")
    cell = P(None, "gx", "gy")
    placed = (
        soil,
        soil,
        cell,
        cell,
        cell,
        P(both, None, None),
        P(both, None),
        P(both, None),
        P(both, None),
        P(both, None),
        P(both),
        P(both, None),
        P(both),
    )
    return jax.shard_map(
        body,
        mesh=mesh,
        in_specs=placed,
        out_specs=(soil, P(both, None), P(both, None)),
        check_vma=False,
    )
```

```python
import jax
import jax.numpy as jnp
from jax import lax
from jax.experimental import pallas as pl
from jax.experimental.pallas import tpu as pltpu
from jax.sharding import PartitionSpec as P

FOOT = 8
CAP = 2
PAD = 8
STRIP = 4
TILE = 8

near = 9.0 / 8.0
far = 1.0 / 24.0
time_step = 0.3
exact = lax.Precision.HIGHEST
f32 = jnp.float32

AT_X, AT_Y, AT_RATE, AT_COUPLING, AT_SQUARE, AT_CORNER = 64, 65, 66, 69, 72, 75
FIRST, SECOND, AT_NEXT = 0, 3, 8


COSTS = {
    "first": 30_000_000,
    "begin": 40_000_000,
    "stress": 25_000_000,
    "surface": 10_000_000,
    "pull": 30_000_000,
    "velocity": 25_000_000,
    "motion_again": 10_000_000,
    "finish": 60_000_000,
}


class Far:
    def __init__(self, value):
        self.value = value


def call(kernel, name, outs, args, scratch=(), far_outs=()):
    cost = COSTS[name]
    specs, values = [], []
    for a in args:
        far = isinstance(a, Far)
        a = a.value if far else a
        values.append(pltpu.with_memory_space_constraint(a, pltpu.HBM if far else pltpu.VMEM))
        specs.append(pl.BlockSpec(memory_space=pl.ANY if far else pltpu.VMEM))
    return pl.pallas_call(
        kernel,
        name=name,
        out_shape=outs,
        in_specs=specs,
        out_specs=tuple(
            pl.BlockSpec(memory_space=pl.ANY if i in far_outs else pltpu.VMEM)
            for i in range(len(outs))
        ),
        scratch_shapes=list(scratch),
        cost_estimate=pl.CostEstimate(flops=1000*cost, bytes_accessed=cost, transcendentals=0),
        compiler_params=pltpu.CompilerParams(vmem_limit_bytes=16 * 2**20),
    )(*values)


def shape(*dims):
    return jax.ShapeDtypeStruct(dims, f32)


def near_by(*dims, dtype=f32):
    return pltpu.VMEM(dims, dtype)


def fetch(sources, targets, sems):
    copies = [
        pltpu.make_async_copy(source, target, sems.at[i])
        for i, (source, target) in enumerate(zip(sources, targets))
    ]
    for copy in copies:
        copy.start()
    return copies


def swap(block, axis, odd):
    size = lax.axis_size(axis)
    pairs = [(i % size, (i + 1) % size) for i in range(odd, size + odd, 2)]
    return lax.ppermute(block, axis, pairs + [(b, a) for a, b in pairs])


def even(axis):
    return lax.rem(lax.axis_index(axis), 2) == 0


def two_ways(up, down, even_ref, odd_ref):
    lead = even("gx")
    blank = jnp.zeros(even_ref.shape[1:], f32)
    for row in range(even_ref.shape[0]):
        a = up[row] if row < len(up) else blank
        b = down[row] if row < len(down) else blank
        even_ref[row] = jnp.where(lead, a, b)
        odd_ref[row] = jnp.where(lead, b, a)


def below_above(axis, even_ref, odd_ref):
    lead = even(axis)

    def below(index):
        return jnp.where(lead, odd_ref[index], even_ref[index])

    def above(index):
        return jnp.where(lead, even_ref[index], odd_ref[index])

    return below, above


def lanes_of(value):
    return lax.broadcasted_iota(jnp.int32, value.shape, len(value.shape) - 1)


def roll(value, amount):
    return pltpu.roll(value, amount % value.shape[-1], len(value.shape) - 1)


def packed(pieces):
    result = None
    for slab, first, count, amount in pieces:
        moved = roll(slab, amount) if amount else slab
        if result is None:
            result = moved
        else:
            lane = lanes_of(slab)
            result = jnp.where((lane >= first) & (lane < first + count), moved, result)
    return result


def send_columns(pack_ref, out_ref):
    rows, width = out_ref.shape
    for block in range(width // 128):
        part = pack_ref[block * 128 : (block + 1) * 128, :]
        out_ref[:, block * 128 : (block + 1) * 128] = part.T[:rows]


def receive_columns(even_ref, odd_ref, from_south, south_ok, north_ok, out_ref):
    rows, width = even_ref.shape
    below, above = below_above("gy", even_ref, odd_ref)
    for block in range(width // 128):
        cut = slice(block * 128, (block + 1) * 128)
        south = jnp.where(south_ok, below((slice(None), cut)), 0.0)
        north = jnp.where(north_ok, above((slice(None), cut)), 0.0)
        row = lax.broadcasted_iota(jnp.int32, south.shape, 0)
        taken = row == from_south[0]
        for other in from_south[1:]:
            taken = taken | (row == other)
        part = jnp.where(taken, south, north)
        whole = jnp.concatenate([part, jnp.zeros((128 - rows, 128), f32)], axis=0)
        out_ref[cut, :] = whole.T


def slopes(f, ghost, forward):
    lane = lanes_of(f)
    last = f.shape[-1] - 1
    up1 = roll(jnp.where(lane == 0, ghost, f), -1)
    down1 = roll(jnp.where(lane == last, ghost, f), 1)
    if forward:
        up2 = roll(jnp.where(lane <= 1, ghost, f), -2)
        return near * (up1 - f) - far * (up2 - down1)
    down2 = roll(jnp.where(lane >= last - 1, ghost, f), 2)
    return near * (f - down1) - far * (up1 - down2)


def across(ext, c, x, forward, layers):
    def at(d):
        return ext[c, x + 2 + d, PAD : PAD + layers, :]

    if forward:
        return near * (at(1) - at(0)) - far * (at(2) - at(-1))
    return near * (at(0) - at(-1)) - far * (at(1) - at(-2))


def down(ext, c, x, forward, layers):
    def at(d):
        return ext[c, x + 2, PAD + d : PAD + layers + d, :]

    if forward:
        return near * (at(1) - at(0)) - far * (at(2) - at(-1))
    return near * (at(0) - at(-1)) - far * (at(1) - at(-2))


def place():
    gx, gy = lax.axis_index("gx"), lax.axis_index("gy")
    nx, ny = lax.axis_size("gx"), lax.axis_size("gy")
    return gx > 0, gx < nx - 1, gy > 0, gy < ny - 1


def fill(ext, c, source, src, size_x, layers):
    for x in range(size_x):
        ext[c, x + 2, 0:PAD, :] = jnp.zeros((PAD, 128), f32)
        ext[c, x + 2, PAD : PAD + layers, :] = source[src, x * layers : (x + 1) * layers, :]
        ext[c, x + 2, PAD + layers : PAD + layers + PAD, :] = jnp.zeros((PAD, 128), f32)


def edges(layers, arrived, vt_ref, bt_ref, mt_ref, even_ref, odd_ref, col_ref, pack):
    size_x = vt_ref.shape[1] // layers

    def slab(ref, x):
        return ref[x * layers : (x + 1) * layers, :]

    for x in range(size_x):
        arrived(x)
        pack[x * layers : (x + 1) * layers, :] = packed(
            [
                (slab(vt_ref.at[0], x), 0, 3, 1),
                (slab(vt_ref.at[1], x), 3, 3, 5),
                (slab(vt_ref.at[2], x), 6, 3, 7),
                (slab(bt_ref, x), 9, 1, 9),
                (slab(mt_ref, x), 10, 1, 10),
            ]
        )
    last = size_x - 1
    up = [slab(vt_ref.at[c], x) for c, x in ((0, last - 1), (0, last), (1, last), (2, last))]
    down = [slab(vt_ref.at[c], x) for c, x in ((0, 0), (1, 0), (1, 1), (2, 0), (2, 1))]
    two_ways(up, down + [slab(bt_ref, 0), slab(mt_ref, 0)], even_ref, odd_ref)
    send_columns(pack, col_ref)


def materials(layers, b_ref, l_ref, m_ref, above, cols, table_ref, mat_ref, buoy_ref, bs, ms, tb, tm):
    size_x = b_ref.shape[0] // layers
    _, east_ok, _, north_ok = place()
    nx, ny = lax.axis_size("gx"), lax.axis_size("gy")
    beyond = lax.rem(lax.axis_index("gx") + 1, nx) * ny + lax.rem(lax.axis_index("gy") + 1, ny)
    inner = slice(PAD, PAD + layers)
    for x in range(size_x):
        cut = slice(x * layers, (x + 1) * layers)
        bs[x, inner, :] = b_ref[cut, :]
        ms[x, inner, :] = m_ref[cut, :]
        part = cols[cut, :]
        tb[x, inner, :] = roll(part, -9)
        tm[x, inner, :] = roll(part, -10)
    bs[size_x, inner, :] = above(5)
    ms[size_x, inner, :] = above(6)
    line = jnp.broadcast_to(table_ref[pl.ds(beyond * CAP, 1), :], (layers, 128))
    own = lanes_of(line) - AT_CORNER == lax.broadcasted_iota(jnp.int32, line.shape, 0)
    corner = jnp.sum(jnp.where(own, line, 0.0), axis=1, keepdims=True)
    tm[size_x, inner, :] = jnp.broadcast_to(corner, line.shape)
    zero = jnp.zeros((PAD, 128), f32)
    for x in range(size_x + 1):
        bs[x, PAD + layers : PAD + layers + PAD, :] = zero
        ms[x, PAD + layers : PAD + layers + PAD, :] = zero
        tm[x, PAD + layers : PAD + layers + PAD, :] = zero
    below = slice(PAD + 1, PAD + layers + 1)

    def step(x, carry):
        cut = pl.ds(pl.multiple_of(x * layers, layers), layers)
        b, m = bs[x, inner, :], ms[x, inner, :]
        lane = lanes_of(b)
        layer = lax.broadcasted_iota(jnp.int32, b.shape, 0)
        in_x = (x < size_x - 1) | east_ok
        in_y = (lane < 127) | north_ok
        in_z = layer < layers - 1

        def north(value, ghost):
            return roll(jnp.where(lane == 0, ghost, value), -1)

        b_e = jnp.where(in_x, bs[x + 1, inner, :], b)
        b_n = jnp.where(in_y, north(b, tb[x, inner, :]), b)
        b_z = jnp.where(in_z, bs[x, below, :], b)
        m_e = jnp.where(in_x, ms[x + 1, inner, :], m)
        m_n = jnp.where(in_y, north(m, tm[x, inner, :]), m)
        m_z = jnp.where(in_z, ms[x, below, :], m)
        m_en = jnp.where(in_y & in_x, north(ms[x + 1, inner, :], tm[x + 1, inner, :]), m)
        m_ez = jnp.where(in_z & in_x, ms[x + 1, below, :], m)
        m_nz = jnp.where(in_z & in_y, north(ms[x, below, :], tm[x, below, :]), m)
        mat_ref[0, cut, :] = time_step * l_ref[x]
        mat_ref[1, cut, :] = (2.0 * time_step) * m
        mat_ref[2, cut, :] = (0.25 * time_step) * (m + m_e + m_n + m_en)
        mat_ref[3, cut, :] = (0.25 * time_step) * (m + m_e + m_z + m_ez)
        mat_ref[4, cut, :] = (0.25 * time_step) * (m + m_n + m_z + m_nz)
        buoy_ref[0, cut, :] = (0.5 * time_step) * (b + b_e)
        buoy_ref[1, cut, :] = (0.5 * time_step) * (b + b_n)
        buoy_ref[2, cut, :] = (0.5 * time_step) * (b + b_z)
        return carry

    lax.fori_loop(0, size_x, step, 0, unroll=4)


def extend(ext, rows, at, ok, layers):
    for row, c, x in rows:
        ext[c, x, PAD : PAD + layers, :] = jnp.where(ok, at(row), 0.0)


def stresses(layers, v_ref, old, ready, mat_ref, below, above, cols, out_ref, refs, ext, pack):
    even_ref, odd_ref, col_ref = refs
    size_x = v_ref.shape[1] // layers
    west_ok, east_ok, _, _ = place()
    for c in range(3):
        fill(ext, c, v_ref, c, size_x, layers)
    inner = slice(PAD, PAD + layers)
    extend(ext, ((0, 0, 0), (1, 0, 1), (2, 1, 1), (3, 2, 1)), below, west_ok, layers)
    over = size_x + 2
    rows = ((0, 0, over), (1, 1, over), (2, 1, over + 1), (3, 2, over), (4, 2, over + 1))
    extend(ext, rows, above, east_ok, layers)

    def step(x, carry):
        cut = pl.ds(pl.multiple_of(x * layers, layers), layers)
        ghost = cols[cut, :]
        vx, vy, vz = [ext[c, x + 2, inner, :] for c in range(3)]
        gx, gy, gz = roll(ghost, -1), roll(ghost, -5), roll(ghost, -7)
        dx = across(ext, 0, x, False, layers)
        dy = slopes(vy, gy, False)
        dz = down(ext, 2, x, False, layers)
        both = mat_ref[0, cut, :] * (dx + dy + dz)
        twice = mat_ref[1, cut, :]
        xx = old(0, x, cut) + (both + twice * dx)
        yy = old(1, x, cut) + (both + twice * dy)
        zz = old(2, x, cut) + (both + twice * dz)
        xy = old(3, x, cut) + mat_ref[2, cut, :] * (
            slopes(vx, gx, True) + across(ext, 1, x, True, layers)
        )
        xz = old(4, x, cut) + mat_ref[3, cut, :] * (
            down(ext, 0, x, True, layers) + across(ext, 2, x, True, layers)
        )
        yz = old(5, x, cut) + mat_ref[4, cut, :] * (
            down(ext, 1, x, True, layers) + slopes(vz, gz, True)
        )
        for c, value in enumerate((xx, yy, zz, xy, xz, yz)):
            out_ref[c, cut, :] = value
        pack[cut, :] = packed([(yy, 0, 3, 1), (xy, 3, 3, 5), (yz, 6, 3, 8)])
        return carry

    for strip in range(size_x // STRIP):
        ready(strip)
        lax.fori_loop(strip * STRIP, (strip + 1) * STRIP, step, 0, unroll=4)
    send_columns(pack, col_ref)

    def slab(c, x):
        return out_ref[c, x * layers : (x + 1) * layers, :]

    up = [slab(c, size_x - x) for c, x in ((0, 1), (3, 2), (3, 1), (4, 2), (4, 1))]
    two_ways(up, [slab(c, x) for c, x in ((0, 0), (0, 1), (3, 0), (4, 0))], even_ref, odd_ref)


def begin_kernel(
    layers,
    v_ref,
    b_ref,
    m_ref,
    s_hbm,
    l_hbm,
    stiff_hbm,
    x_even,
    x_odd,
    y_even,
    y_odd,
    table_ref,
    out_ref,
    even_ref,
    odd_ref,
    col_ref,
    buoy_ref,
    stiff_ref,
    mat_hbm,
    buoy_hbm,
    s_ref,
    l_ref,
    mat_ref,
    bs,
    ms,
    tb,
    tm,
    ext,
    cols,
    pack,
    sems,
):
    size_x = v_ref.shape[1] // layers
    own = range(size_x)
    sources = [l_hbm.at[:, x] for x in own] + [s_hbm.at[:, :, x] for x in own]
    targets = [l_ref.at[x] for x in own] + [s_ref.at[:, x] for x in own]
    half = stiff_ref.shape[0]
    copies = fetch(
        sources + [stiff_hbm.at[pl.ds(0, half)]], targets + [stiff_ref.at[...]], sems
    )
    _, _, south_ok, north_ok = place()
    below, above = below_above("gx", x_even, x_odd)
    receive_columns(y_even, y_odd, (0, 3, 4, 6), south_ok, north_ok, cols)
    for x in own:
        copies[x].wait()
    materials(layers, b_ref, l_ref, m_ref, above, cols, table_ref, mat_ref, buoy_ref, bs, ms, tb, tm)
    leaving = fetch([mat_ref, buoy_ref], [mat_hbm, buoy_hbm], sems.at[pl.ds(2 * size_x + 1, 2)])

    def ready(strip):
        for x in range(strip * STRIP, (strip + 1) * STRIP):
            copies[size_x + x].wait()

    def old(c, x, cut):
        return s_ref[c, x]

    refs = (even_ref, odd_ref, col_ref)
    stresses(layers, v_ref, old, ready, mat_ref, below, above, cols, out_ref, refs, ext, pack)
    for copy in leaving + copies[2 * size_x :]:
        copy.wait()


def stress_kernel(
    layers,
    v_ref,
    s_hbm,
    mat_hbm,
    x_even,
    x_odd,
    y_even,
    y_odd,
    out_ref,
    even_ref,
    odd_ref,
    col_ref,
    s_ref,
    mat_ref,
    ext,
    cols,
    pack,
    sems,
):
    strips = v_ref.shape[1] // layers // STRIP
    cuts = [pl.ds(strip * STRIP * layers, STRIP * layers) for strip in range(strips)]
    sources, targets = [], []
    for cut in cuts:
        sources += [s_hbm.at[:, cut], mat_hbm.at[:, cut]]
        targets += [s_ref.at[:, cut], mat_ref.at[:, cut]]
    copies = fetch(sources, targets, sems)
    _, _, south_ok, north_ok = place()
    below, above = below_above("gx", x_even, x_odd)
    receive_columns(y_even, y_odd, (0, 3, 4, 6), south_ok, north_ok, cols)

    def ready(strip):
        copies[2 * strip].wait()
        copies[2 * strip + 1].wait()

    def old(c, x, cut):
        return s_ref[c, cut, :]

    refs = (even_ref, odd_ref, col_ref)
    stresses(layers, v_ref, old, ready, mat_ref, below, above, cols, out_ref, refs, ext, pack)


def velocity_kernel(
    layers, last, v_ref, s_ref, buoy_ref, x_even, x_odd, y_even, y_odd, push_ref, *refs
):
    if last:
        out_hbm, out_ref, ext, cols, sems = refs
    else:
        out_ref, even_ref, odd_ref, col_ref, kept_hbm, ext, cols, pack, sems = refs
        keep = pltpu.make_async_copy(s_ref, kept_hbm, sems.at[0])
        keep.start()
    size_x = v_ref.shape[1] // layers
    west_ok, east_ok, south_ok, north_ok = place()
    below, above = below_above("gx", x_even, x_odd)
    receive_columns(y_even, y_odd, (0, 3, 4, 6, 7), south_ok, north_ok, cols)
    for c, src in enumerate((0, 3, 4, 5, 2)):
        fill(ext, c, s_ref, src, size_x, layers)
    inner = slice(PAD, PAD + layers)
    rows = ((0, 0, 1), (1, 1, 0), (2, 1, 1), (3, 2, 0), (4, 2, 1))
    extend(ext, rows, below, west_ok, layers)
    over = size_x + 2
    extend(ext, ((0, 0, over), (1, 0, over + 1), (2, 1, over), (3, 2, over)), above, east_ok, layers)

    def step(x, carry):
        cut = pl.ds(pl.multiple_of(x * layers, layers), layers)
        ghost = cols[cut, :]
        yy, xy, yz = s_ref[1, cut, :], ext[1, x + 2, inner, :], ext[3, x + 2, inner, :]
        gyy, gxy, gyz = roll(ghost, -1), roll(ghost, -5), roll(ghost, -8)
        ax = across(ext, 0, x, True, layers) + slopes(xy, gxy, False) + down(ext, 2, x, False, layers)
        ay = across(ext, 1, x, False, layers) + slopes(yy, gyy, True) + down(ext, 3, x, False, layers)
        az = across(ext, 2, x, False, layers) + slopes(yz, gyz, False) + down(ext, 4, x, True, layers)
        layer = lax.broadcasted_iota(jnp.int32, yy.shape, 0)
        fresh = []
        for c, accel in enumerate((ax, ay, az)):
            pushed = jnp.where(layer == 0, push_ref[c, pl.ds(x, 1), :], 0.0)
            fresh.append(v_ref[c, cut, :] + buoy_ref[c, cut, :] * accel + pushed)
        if last:
            for c in range(3):
                out_ref[x // TILE, c, :, lax.rem(x, TILE), :] = fresh[c]
        else:
            for c in range(3):
                out_ref[c, cut, :] = fresh[c]
            pack[cut, :] = packed([(fresh[0], 0, 3, 1), (fresh[1], 3, 3, 5), (fresh[2], 6, 3, 7)])
        return carry

    if last:
        leaving = []
        for tile in range(size_x // TILE):
            lax.fori_loop(tile * TILE, (tile + 1) * TILE, step, 0, unroll=4)
            leaving += fetch(
                [out_ref.at[tile]], [out_hbm.at[:, :, tile]], sems.at[pl.ds(tile, 1)]
            )
        for copy in leaving:
            copy.wait()
        return
    lax.fori_loop(0, size_x, step, 0, unroll=4)
    send_columns(pack, col_ref)

    def slab(c, x):
        return out_ref[c, x * layers : (x + 1) * layers, :]

    up = [slab(c, size_x - x) for c, x in ((0, 2), (0, 1), (1, 1), (2, 1))]
    down_rows = [slab(c, x) for c, x in ((0, 0), (1, 0), (1, 1), (2, 0), (2, 1))]
    two_ways(up, down_rows, even_ref, odd_ref)
    keep.wait()


def third(value, e):
    d = lanes_of(value).astype(f32)
    return d - 3.0 * jnp.floor((d + 0.5) * (1.0 / 3.0)) == e


def column(row):
    n = row.shape[1]
    same = lax.broadcasted_iota(jnp.int32, (n, n), 0) == lax.broadcasted_iota(jnp.int32, (n, n), 1)
    return jnp.sum(jnp.where(same, row, 0.0), axis=1, keepdims=True)


def slot_table(owner_ref, slots):
    number = owner_ref.shape[1]
    owner = owner_ref[...].astype(f32)
    owner_col = column(owner)
    same = owner_col == owner
    i = lax.broadcasted_iota(jnp.int32, same.shape, 0)
    j = lax.broadcasted_iota(jnp.int32, same.shape, 1)
    slot_row = owner * CAP + jnp.sum(jnp.where(same & (i < j), 1.0, 0.0), axis=0, keepdims=True)
    slot_col = owner_col * CAP + jnp.sum(jnp.where(same & (j < i), 1.0, 0.0), axis=1, keepdims=True)
    to_slot = lax.broadcasted_iota(jnp.int32, (slots, number), 0).astype(f32) == slot_row
    of_slot = lax.broadcasted_iota(jnp.int32, (number, slots), 1).astype(f32) == slot_col
    return jnp.where(to_slot, 1.0, 0.0), jnp.where(of_slot, 1.0, 0.0)


def counted(counts_ref, shape):
    return lax.broadcasted_iota(jnp.int32, shape, 1).astype(f32) < column(
        counts_ref[...].astype(f32)
    )


def table(
    span,
    rate_ref,
    coupling_ref,
    contact_ref,
    counts_ref,
    owner_ref,
    corner_ref,
    out_ref,
):
    number, width = rate_ref.shape
    slots = out_ref.shape[0]
    mask = counted(counts_ref, (number, width))
    rate = jnp.where(mask, rate_ref[...], 0.0)
    coupling = jnp.where(mask, coupling_ref[...], 0.0)
    contact = contact_ref[...]
    weights = contact / jnp.sum(contact, axis=1, keepdims=True)
    corner = column(corner_ref[...].astype(f32))
    start_x = jnp.floor((corner + 0.5) * (1.0 / span))
    start_y = corner - start_x * span
    row = jnp.concatenate([weights, jnp.zeros((number, 128 - weights.shape[1]), f32)], axis=1)
    lane = lanes_of(row)
    row = jnp.where(lane == AT_X, start_x, row)
    row = jnp.where(lane == AT_Y, start_y, row)
    sums = (
        (AT_RATE, coupling * rate),
        (AT_COUPLING, coupling),
        (AT_SQUARE, time_step * coupling * coupling),
    )
    row = sums_by_third(row, sums)
    to_slot, _ = slot_table(owner_ref, slots)
    out_ref[...] = jnp.dot(to_slot, row, precision=exact, preferred_element_type=f32)


def first_kernel(layers, span, *refs):
    far, outs, scratch = refs[:9], refs[9:16], refs[16:]
    small, pack, sems = scratch[:6], scratch[6], scratch[7]
    vt, bt, mt = outs[:3]
    size_x = vt.shape[1] // layers
    cuts = [pl.ds(x * layers, layers) for x in range(size_x)]
    sources, targets = list(far[3:]), list(small)
    for x, cut in enumerate(cuts):
        sources += [far[0].at[:, :, x], far[1].at[:, x], far[2].at[:, x]]
        targets += [vt.at[:, cut], bt.at[cut], mt.at[cut]]
    copies = fetch(sources, targets, sems)
    for copy in copies[:6]:
        copy.wait()
    table(span, *small, outs[6])

    def arrived(x):
        for copy in copies[6 + 3 * x : 9 + 3 * x]:
            copy.wait()

    edges(layers, arrived, *outs[:6], pack)
    first = mt[pl.ds(0, layers), 0:1]
    spot = lax.broadcasted_iota(jnp.int32, (layers, 128), 1) - AT_CORNER
    own = spot == lax.broadcasted_iota(jnp.int32, (layers, 128), 0)
    outs[6][...] += jnp.sum(jnp.where(own, first, 0.0), axis=0, keepdims=True)


def sums_by_third(row, sums):
    lane = lanes_of(row)
    for at, value in sums:
        for e in range(3):
            total = jnp.sum(jnp.where(third(value, e), value, 0.0), axis=1, keepdims=True)
            row = jnp.where(lane == at + e, total, row)
    return row


def fetch_strips(stiff_hbm, begin, stiff_ref, sems):
    size = stiff_ref.shape[0] // sems.shape[0]
    strips = range(sems.shape[0])
    return fetch(
        [stiff_hbm.at[pl.ds(begin + c * size, size)] for c in strips],
        [stiff_ref.at[pl.ds(c * size, size)] for c in strips],
        sems,
    )


def products(stiff_ref, at, drift_ref, out_ref, begin, end):
    group = 16
    for g in range(begin // group * group, end, group):
        rounded = drift_ref[g : g + group, :].astype(jnp.bfloat16)
        row = lax.broadcasted_iota(jnp.int32, rounded.shape, 0)
        low, high = max(g, begin), min(g + group, end)
        total = out_ref[g : g + group, :]
        for b in range(low, high):
            part = lax.dot_general(
                rounded, stiff_ref[b - at], (((1,), (1,)), ((), ())), preferred_element_type=f32
            )
            total = jnp.where(row == b - g, part, total)
        out_ref[g : g + group, :] = total


def pull_kernel(
    stiff_ref,
    stiff_hbm,
    raw_ref,
    rate_ref,
    coupling_ref,
    counts_ref,
    owner_ref,
    base_ref,
    drift_out,
    next_ref,
    pull,
    rest_ref,
    sems,
):
    number, half = drift_out.shape[0], stiff_ref.shape[0]
    copies = fetch_strips(stiff_hbm, half, rest_ref, sems)
    mask = counted(counts_ref, drift_out.shape)
    drift_out[...] = jnp.where(mask, raw_ref[...], 0.0)
    pull[...] = jnp.zeros(pull.shape, f32)
    products(stiff_ref, 0, drift_out, pull, 0, half)
    size = (number - half) // len(copies)
    for c, copy in enumerate(copies):
        copy.wait()
        products(rest_ref, half, drift_out, pull, half + c * size, half + (c + 1) * size)
    rate = jnp.where(mask, rate_ref[...], 0.0)
    coupling = jnp.where(mask, coupling_ref[...], 0.0)
    base = rate - time_step * pull[...] - time_step * coupling * rate
    base = jnp.where(mask, base, 0.0)
    base_ref[...] = base
    row = sums_by_third(jnp.zeros((number, 128), f32), ((AT_NEXT, coupling * base),))
    to_slot, _ = slot_table(owner_ref, next_ref.shape[0])
    next_ref[...] = jnp.dot(to_slot, row, precision=exact, preferred_element_type=f32)


def motion(maps_ref, v_ref, layers):
    size_x, slots, size_y = maps_ref.shape
    total = [jnp.zeros((slots, size_y), f32) for _ in range(3)]
    for x in range(size_x):
        part = maps_ref[x]
        for c in range(3):
            total[c] = total[c] + part * v_ref[c, x * layers : x * layers + 1, :]
    return [jnp.sum(t, axis=1, keepdims=True) for t in total]


def spread(at, reaction, out_ref):
    for x in range(out_ref.shape[1]):
        part = at(x)
        for c in range(3):
            out_ref[c, x : x + 1, :] = jnp.sum(part * reaction[c], axis=0, keepdims=True)


def footprints(table):
    lane = lanes_of(table)
    off_y = lane - table[:, AT_Y : AT_Y + 1].astype(jnp.int32)
    start_x = jnp.broadcast_to(table[:, AT_X : AT_X + 1], table.shape)
    within = (off_y >= 0) & (off_y < FOOT)
    inside = jnp.where(within, off_y, 0)
    lines = []
    for a in range(FOOT):
        picked = jnp.take_along_axis(table, inside + a * FOOT, axis=1)
        lines.append(jnp.where(within, picked, 0.0))

    def at(x):
        value = jnp.zeros(table.shape, f32)
        for a in range(FOOT):
            value = jnp.where(start_x == float(x - a), lines[a], value)
        return value

    return at


def surface_kernel(layers, table_ref, v_ref, maps_ref, moved_ref, push_ref):
    table = table_ref[...]
    lane = lanes_of(table)
    at = footprints(table)
    for x in range(maps_ref.shape[0]):
        maps_ref[x] = at(x)
    moved = motion(maps_ref, v_ref, layers)
    reaction = []
    rows = jnp.zeros(table.shape, f32)
    for c in range(3):
        rest, slope = (table[:, at + c : at + c + 1] for at in (AT_RATE, AT_COUPLING))
        reaction.append(time_step * FOOT * (rest - slope * moved[c]))
        rows = jnp.where(lane == FIRST + c, moved[c], rows)
    moved_ref[...] = rows
    spread(lambda x: maps_ref[x], reaction, push_ref)


def spread_thirds(moved, at, value):
    result = jnp.zeros(value.shape, f32)
    for e in range(3):
        result = jnp.where(third(value, e), moved[:, at + e : at + e + 1], result)
    return result


def motion_again_kernel(layers, v_ref, maps_ref, before_ref, next_ref, out_ref):
    moved = motion(maps_ref, v_ref, layers)
    rows = before_ref[...] + next_ref[...]
    lane = lanes_of(rows)
    for c in range(3):
        rows = jnp.where(lane == SECOND + c, moved[c], rows)
    out_ref[...] = rows


def finish_kernel(
    sent_ref,
    back_ref,
    table_ref,
    base_ref,
    drift_ref,
    coupling_ref,
    counts_ref,
    owner_ref,
    stiff_hbm,
    push_ref,
    drift_out,
    rate_out,
    half,
    pull,
    stiff_ref,
    sems,
):
    copies = fetch_strips(stiff_hbm, 0, stiff_ref, sems)
    table, sent, back = table_ref[...], sent_ref[...], back_ref[...]
    reaction = []
    for c in range(3):
        rest = back[:, AT_NEXT + c : AT_NEXT + c + 1]
        rest = rest + table[:, AT_SQUARE + c : AT_SQUARE + c + 1] * sent[:, FIRST + c : FIRST + c + 1]
        slope = table[:, AT_COUPLING + c : AT_COUPLING + c + 1]
        reaction.append(time_step * FOOT * (rest - slope * sent[:, SECOND + c : SECOND + c + 1]))
    spread(footprints(table), reaction, push_ref)
    _, of_slot = slot_table(owner_ref, back.shape[0])
    moved = jnp.dot(of_slot, back, precision=exact, preferred_element_type=f32)
    coupling = coupling_ref[...]
    mask = counted(counts_ref, coupling.shape)
    rate = base_ref[...] + time_step * coupling * spread_thirds(moved, FIRST, coupling)
    rate = jnp.where(mask, rate, 0.0)
    drift = jnp.where(mask, drift_ref[...] + time_step * rate, 0.0)
    half[...] = drift
    pull[...] = jnp.zeros(pull.shape, f32)
    size = half.shape[0] // len(copies)
    for c, copy in enumerate(copies):
        copy.wait()
        products(stiff_ref, 0, half, pull, c * size, (c + 1) * size)
    relative = rate - spread_thirds(moved, SECOND, coupling)
    rate = rate - time_step * pull[...] - time_step * coupling * relative
    rate = jnp.where(mask, rate, 0.0)
    rate_out[...] = rate
    drift_out[...] = jnp.where(mask, drift + time_step * rate, 0.0)


def trade(rows):
    devices = lax.axis_size("gx") * lax.axis_size("gy")
    blocks = rows.reshape(devices, CAP, rows.shape[1])
    blocks = lax.all_to_all(blocks, ("gx", "gy"), split_axis=0, concat_axis=0, tiled=True)
    return blocks.reshape(rows.shape)


def body(
    soil_velocity,
    soil_stress,
    buoyancy,
    lame_first,
    shear_modulus,
    stiffness,
    storey_drift,
    drift_rate,
    coupling,
    contact,
    dof_counts,
    owner_tile,
    corner_cell,
):
    layers, size_x, size_y = buoyancy.shape
    cells = layers * size_x
    number, width = storey_drift.shape
    slots = lax.axis_size("gx") * lax.axis_size("gy") * CAP
    span = size_y - FOOT + 1
    counts, owner, corner = (a.reshape(1, number) for a in (dof_counts, owner_tile, corner_cell))

    def bind(kernel, *fixed):
        def bound(*refs):
            kernel(*fixed, *refs)

        return bound

    def vm(*dims):
        return pltpu.VMEM(dims, f32)

    field = vm(cells, size_y)
    tall = layers + 2 * PAD
    plane = near_by(number, width)
    dma = pltpu.SemaphoreType.DMA
    far = (soil_velocity, buoyancy, shear_modulus, drift_rate, coupling, contact, counts, owner, corner)
    outs = call(
        bind(first_kernel, layers, span),
        "first",
        (
            near_by(3, cells, size_y),
            near_by(cells, size_y),
            near_by(cells, size_y),
            near_by(7, layers, size_y),
            near_by(7, layers, size_y),
            near_by(16, cells),
            near_by(slots, 128),
        ),
        [Far(a) for a in far],
        [pltpu.VMEM(a.shape, a.dtype) for a in far[3:]] + [field, dma((6 + 3 * size_x,))],
    )
    vt, bt, mt, one, two, col, rows = outs

    def exchange(one, two, col):
        return swap(one, "gx", 0), swap(two, "gx", 1), swap(col, "gy", 0), swap(col, "gy", 1)

    halo = exchange(one, two, col)
    rows = trade(rows)
    half = number // 2
    payload = (near_by(5, layers, size_y), near_by(5, layers, size_y), near_by(16, cells))
    ext = vm(3, size_x + 4, tall, size_y)
    stack = vm(size_x + 1, tall, size_y)
    st, one, two, col, buoys, stiff, mat_kept, buoy_kept = call(
        bind(begin_kernel, layers),
        "begin",
        (
            near_by(6, cells, size_y),
            *payload,
            near_by(3, cells, size_y),
            near_by(half, width, width, dtype=stiffness.dtype),
            pltpu.HBM((5, cells, size_y), f32),
            pltpu.HBM((3, cells, size_y), f32),
        ),
        (vt, bt, mt, Far(soil_stress), Far(lame_first), Far(stiffness), *halo, rows),
        [
            vm(6, size_x, layers, size_y),
            vm(size_x, layers, size_y),
            vm(5, cells, size_y),
            stack,
            stack,
            stack,
            stack,
            ext,
            field,
            field,
            dma((2 * size_x + 3,)),
        ],
        far_outs=(6, 7),
    )

    def velocity_step(last, v, s, buoys, halo, push):
        scratch = [vm(5, size_x + 4, tall, size_y), field]
        tiles = size_x // TILE
        if last:
            outs = [pltpu.HBM((3, layers, tiles, TILE, size_y), f32)]
            scratch = [vm(tiles, 3, layers, TILE, size_y)] + scratch + [dma((tiles,))]
        else:
            outs = [near_by(3, cells, size_y), *payload, pltpu.HBM((6, cells, size_y), f32)]
            scratch += [field, dma((1,))]
        return call(
            bind(velocity_kernel, layers, last),
            "velocity",
            tuple(outs),
            (v, s, buoys, *halo, push),
            scratch,
            far_outs=(0,) if last else (4,),
        )

    halo = exchange(one, two, col)
    maps, moved, push = call(
        bind(surface_kernel, layers),
        "surface",
        (near_by(size_x, slots, size_y), near_by(slots, 128), near_by(3, size_x, size_y)),
        (rows, vt),
    )
    chunks = 4 if number % 8 == 0 else 1
    base, drift, following = call(
        pull_kernel,
        "pull",
        (plane, plane, near_by(slots, 128)),
        (stiff, Far(stiffness), storey_drift, drift_rate, coupling, counts, owner),
        [
            vm(number, width),
            pltpu.VMEM((number - half, width, width), stiffness.dtype),
            dma((chunks,)),
        ],
    )
    push, following = lax.optimization_barrier((push, following))
    vt, one, two, col, kept = velocity_step(False, vt, st, buoys, halo, push)
    halo = exchange(one, two, col)
    (sent,) = call(
        bind(motion_again_kernel, layers),
        "motion_again",
        (near_by(slots, 128),),
        (vt, maps, moved, following),
    )
    vt, sent = lax.optimization_barrier((vt, sent))
    back = trade(sent)
    strips = size_x // STRIP
    st, one, two, col = call(
        bind(stress_kernel, layers),
        "stress",
        (near_by(6, cells, size_y), *payload),
        (vt, Far(kept), Far(mat_kept), *halo),
        [
            vm(6, cells, size_y),
            vm(5, cells, size_y),
            ext,
            field,
            field,
            dma((2 * strips,)),
        ],
    )
    halo = exchange(one, two, col)
    sent, st = lax.optimization_barrier((sent, st))
    push, drift, rate = call(
        finish_kernel,
        "finish",
        (near_by(3, size_x, size_y), shape(number, width), shape(number, width)),
        (sent, back, rows, base, drift, coupling, counts, owner, Far(stiffness)),
        [
            vm(number, width),
            vm(number, width),
            pltpu.VMEM(stiffness.shape, stiffness.dtype),
            dma((2 * chunks,)),
        ],
    )
    (v,) = velocity_step(True, vt, st, buoy_kept, halo, push)
    return v.reshape(soil_velocity.shape), drift, rate


def solution(mesh):
    both = ("gx", "gy")
    soil = P(None, None, "gx", "gy")
    cell = P(None, "gx", "gy")
    placed = (
        soil,
        soil,
        cell,
        cell,
        cell,
        P(both, None, None),
        P(both, None),
        P(both, None),
        P(both, None),
        P(both, None),
        P(both),
        P(both, None),
        P(both),
    )
    return jax.shard_map(
        body,
        mesh=mesh,
        in_specs=placed,
        out_specs=(soil, P(both, None), P(both, None)),
        check_vma=False,
    )
```

```python
import jax
import jax.numpy as jnp
from jax import lax
from jax.experimental import pallas as pl
from jax.experimental.pallas import tpu as pltpu
from jax.sharding import PartitionSpec as P

FOOT = 8
CAP = 2
PAD = 8
STRIP = 4
TILE = 8

near = 9.0 / 8.0
far = 1.0 / 24.0
time_step = 0.3
exact = lax.Precision.HIGHEST
f32 = jnp.float32

AT_X, AT_Y, AT_RATE, AT_COUPLING, AT_SQUARE, AT_CORNER = 64, 65, 66, 69, 72, 75
FIRST, SECOND, AT_NEXT = 0, 3, 8


COSTS = {
    "first": 30_000_000,
    "table": 60_000_000,
    "load": 20_000_000,
    "begin": 40_000_000,
    "stress": 25_000_000,
    "surface": 10_000_000,
    "pull": 30_000_000,
    "velocity": 25_000_000,
    "motion_again": 10_000_000,
    "prepare": 60_000_000,
    "finish": 60_000_000,
}


class Far:
    def __init__(self, value):
        self.value = value


def call(kernel, name, outs, args, scratch=(), far_outs=()):
    cost = COSTS[name]
    specs, values = [], []
    for a in args:
        far = isinstance(a, Far)
        a = a.value if far else a
        values.append(pltpu.with_memory_space_constraint(a, pltpu.HBM if far else pltpu.VMEM))
        specs.append(pl.BlockSpec(memory_space=pl.ANY if far else pltpu.VMEM))
    return pl.pallas_call(
        kernel,
        name=name,
        out_shape=outs,
        in_specs=specs,
        out_specs=tuple(
            pl.BlockSpec(memory_space=pl.ANY if i in far_outs else pltpu.VMEM)
            for i in range(len(outs))
        ),
        scratch_shapes=list(scratch),
        cost_estimate=pl.CostEstimate(flops=1000*cost, bytes_accessed=cost, transcendentals=0),
        compiler_params=pltpu.CompilerParams(vmem_limit_bytes=16 * 2**20),
    )(*values)


def shape(*dims):
    return jax.ShapeDtypeStruct(dims, f32)


def near_by(*dims, dtype=f32):
    return pltpu.VMEM(dims, dtype)


def fetch(sources, targets, sems):
    copies = [
        pltpu.make_async_copy(source, target, sems.at[i])
        for i, (source, target) in enumerate(zip(sources, targets))
    ]
    for copy in copies:
        copy.start()
    return copies


def swap(block, axis, odd):
    size = lax.axis_size(axis)
    pairs = [(i % size, (i + 1) % size) for i in range(odd, size + odd, 2)]
    return lax.ppermute(block, axis, pairs + [(b, a) for a, b in pairs])


def even(axis):
    return lax.rem(lax.axis_index(axis), 2) == 0


def two_ways(up, down, even_ref, odd_ref):
    lead = even("gx")
    blank = jnp.zeros(even_ref.shape[1:], f32)
    for row in range(even_ref.shape[0]):
        a = up[row] if row < len(up) else blank
        b = down[row] if row < len(down) else blank
        even_ref[row] = jnp.where(lead, a, b)
        odd_ref[row] = jnp.where(lead, b, a)


def below_above(axis, even_ref, odd_ref):
    lead = even(axis)

    def below(index):
        return jnp.where(lead, odd_ref[index], even_ref[index])

    def above(index):
        return jnp.where(lead, even_ref[index], odd_ref[index])

    return below, above


def lanes_of(value):
    return lax.broadcasted_iota(jnp.int32, value.shape, len(value.shape) - 1)


def roll(value, amount):
    return pltpu.roll(value, amount % value.shape[-1], len(value.shape) - 1)


def packed(pieces):
    result = None
    for slab, first, count, amount in pieces:
        moved = roll(slab, amount) if amount else slab
        if result is None:
            result = moved
        else:
            lane = lanes_of(slab)
            result = jnp.where((lane >= first) & (lane < first + count), moved, result)
    return result


def send_columns(pack_ref, out_ref):
    rows, width = out_ref.shape
    for block in range(width // 128):
        part = pack_ref[block * 128 : (block + 1) * 128, :]
        out_ref[:, block * 128 : (block + 1) * 128] = part.T[:rows]


def receive_columns(even_ref, odd_ref, from_south, south_ok, north_ok, out_ref):
    rows, width = even_ref.shape
    below, above = below_above("gy", even_ref, odd_ref)
    for block in range(width // 128):
        cut = slice(block * 128, (block + 1) * 128)
        south = jnp.where(south_ok, below((slice(None), cut)), 0.0)
        north = jnp.where(north_ok, above((slice(None), cut)), 0.0)
        row = lax.broadcasted_iota(jnp.int32, south.shape, 0)
        taken = row == from_south[0]
        for other in from_south[1:]:
            taken = taken | (row == other)
        part = jnp.where(taken, south, north)
        whole = jnp.concatenate([part, jnp.zeros((128 - rows, 128), f32)], axis=0)
        out_ref[cut, :] = whole.T


def slopes(f, ghost, forward):
    lane = lanes_of(f)
    last = f.shape[-1] - 1
    up1 = roll(jnp.where(lane == 0, ghost, f), -1)
    down1 = roll(jnp.where(lane == last, ghost, f), 1)
    if forward:
        up2 = roll(jnp.where(lane <= 1, ghost, f), -2)
        return near * (up1 - f) - far * (up2 - down1)
    down2 = roll(jnp.where(lane >= last - 1, ghost, f), 2)
    return near * (f - down1) - far * (up1 - down2)


def across(ext, c, x, forward, layers):
    def at(d):
        return ext[c, x + 2 + d, PAD : PAD + layers, :]

    if forward:
        return near * (at(1) - at(0)) - far * (at(2) - at(-1))
    return near * (at(0) - at(-1)) - far * (at(1) - at(-2))


def down(ext, c, x, forward, layers):
    def at(d):
        return ext[c, x + 2, PAD + d : PAD + layers + d, :]

    if forward:
        return near * (at(1) - at(0)) - far * (at(2) - at(-1))
    return near * (at(0) - at(-1)) - far * (at(1) - at(-2))


def place():
    gx, gy = lax.axis_index("gx"), lax.axis_index("gy")
    nx, ny = lax.axis_size("gx"), lax.axis_size("gy")
    return gx > 0, gx < nx - 1, gy > 0, gy < ny - 1


def fill(ext, c, source, src, size_x, layers):
    for x in range(size_x):
        ext[c, x + 2, 0:PAD, :] = jnp.zeros((PAD, 128), f32)
        ext[c, x + 2, PAD : PAD + layers, :] = source[src, x * layers : (x + 1) * layers, :]
        ext[c, x + 2, PAD + layers : PAD + layers + PAD, :] = jnp.zeros((PAD, 128), f32)


def edges(layers, v_ref, b_ref, m_ref, vt_ref, bt_ref, mt_ref, even_ref, odd_ref, col_ref, pack):
    size_x = vt_ref.shape[1] // layers

    def slab(ref, x):
        return ref[x * layers : (x + 1) * layers, :]

    for x in range(size_x):
        cut = pl.ds(x * layers, layers)
        turned = pl.ds(x, layers, stride=size_x)
        v = [v_ref[c, turned, :] for c in range(3)]
        buoy, shear = b_ref[turned, :], m_ref[turned, :]
        for c in range(3):
            vt_ref[c, cut, :] = v[c]
        bt_ref[cut, :] = buoy
        mt_ref[cut, :] = shear
        pack[cut, :] = packed(
            [(v[0], 0, 3, 1), (v[1], 3, 3, 5), (v[2], 6, 3, 7), (buoy, 9, 1, 9), (shear, 10, 1, 10)]
        )
    last = size_x - 1
    up = [slab(vt_ref.at[c], x) for c, x in ((0, last - 1), (0, last), (1, last), (2, last))]
    down = [slab(vt_ref.at[c], x) for c, x in ((0, 0), (1, 0), (1, 1), (2, 0), (2, 1))]
    two_ways(up, down + [slab(bt_ref, 0), slab(mt_ref, 0)], even_ref, odd_ref)
    send_columns(pack, col_ref)


def load_kernel(layers, after_ref, s_hbm, l_hbm, st_ref, lt_ref, s_ref, l_ref, sems):
    del after_ref
    size_x = l_ref.shape[0] // layers
    copies = fetch(
        [l_hbm] + [s_hbm.at[c] for c in range(6)], [l_ref] + [s_ref.at[c] for c in range(6)], sems
    )
    for c, copy in enumerate(copies):
        copy.wait()
        for x in range(size_x):
            cut, turned = pl.ds(x * layers, layers), pl.ds(x, layers, stride=size_x)
            if c == 0:
                lt_ref[cut, :] = l_ref[turned, :]
            else:
                st_ref[c - 1, cut, :] = s_ref[c - 1, turned, :]


def materials(layers, b_ref, l_ref, m_ref, above, cols, table_ref, mat_ref, buoy_ref, bs, ms, tb, tm):
    size_x = b_ref.shape[0] // layers
    _, east_ok, _, north_ok = place()
    nx, ny = lax.axis_size("gx"), lax.axis_size("gy")
    beyond = lax.rem(lax.axis_index("gx") + 1, nx) * ny + lax.rem(lax.axis_index("gy") + 1, ny)
    inner = slice(PAD, PAD + layers)
    for x in range(size_x):
        cut = slice(x * layers, (x + 1) * layers)
        bs[x, inner, :] = b_ref[cut, :]
        ms[x, inner, :] = m_ref[cut, :]
        part = cols[cut, :]
        tb[x, inner, :] = roll(part, -9)
        tm[x, inner, :] = roll(part, -10)
    bs[size_x, inner, :] = above(5)
    ms[size_x, inner, :] = above(6)
    line = jnp.broadcast_to(table_ref[pl.ds(beyond * CAP, 1), :], (layers, 128))
    own = lanes_of(line) - AT_CORNER == lax.broadcasted_iota(jnp.int32, line.shape, 0)
    corner = jnp.sum(jnp.where(own, line, 0.0), axis=1, keepdims=True)
    tm[size_x, inner, :] = jnp.broadcast_to(corner, line.shape)
    zero = jnp.zeros((PAD, 128), f32)
    for x in range(size_x + 1):
        bs[x, PAD + layers : PAD + layers + PAD, :] = zero
        ms[x, PAD + layers : PAD + layers + PAD, :] = zero
        tm[x, PAD + layers : PAD + layers + PAD, :] = zero
    below = slice(PAD + 1, PAD + layers + 1)

    def step(x, carry):
        cut = pl.ds(pl.multiple_of(x * layers, layers), layers)
        b, m = bs[x, inner, :], ms[x, inner, :]
        lane = lanes_of(b)
        layer = lax.broadcasted_iota(jnp.int32, b.shape, 0)
        in_x = (x < size_x - 1) | east_ok
        in_y = (lane < 127) | north_ok
        in_z = layer < layers - 1

        def north(value, ghost):
            return roll(jnp.where(lane == 0, ghost, value), -1)

        b_e = jnp.where(in_x, bs[x + 1, inner, :], b)
        b_n = jnp.where(in_y, north(b, tb[x, inner, :]), b)
        b_z = jnp.where(in_z, bs[x, below, :], b)
        m_e = jnp.where(in_x, ms[x + 1, inner, :], m)
        m_n = jnp.where(in_y, north(m, tm[x, inner, :]), m)
        m_z = jnp.where(in_z, ms[x, below, :], m)
        m_en = jnp.where(in_y & in_x, north(ms[x + 1, inner, :], tm[x + 1, inner, :]), m)
        m_ez = jnp.where(in_z & in_x, ms[x + 1, below, :], m)
        m_nz = jnp.where(in_z & in_y, north(ms[x, below, :], tm[x, below, :]), m)
        mat_ref[0, cut, :] = time_step * l_ref[cut, :]
        mat_ref[1, cut, :] = (2.0 * time_step) * m
        mat_ref[2, cut, :] = (0.25 * time_step) * (m + m_e + m_n + m_en)
        mat_ref[3, cut, :] = (0.25 * time_step) * (m + m_e + m_z + m_ez)
        mat_ref[4, cut, :] = (0.25 * time_step) * (m + m_n + m_z + m_nz)
        buoy_ref[0, cut, :] = (0.5 * time_step) * (b + b_e)
        buoy_ref[1, cut, :] = (0.5 * time_step) * (b + b_n)
        buoy_ref[2, cut, :] = (0.5 * time_step) * (b + b_z)
        return carry

    lax.fori_loop(0, size_x, step, 0, unroll=4)


def extend(ext, rows, at, ok, layers):
    for row, c, x in rows:
        ext[c, x, PAD : PAD + layers, :] = jnp.where(ok, at(row), 0.0)


def stresses(layers, v_ref, old, ready, mat_ref, below, above, cols, out_ref, refs, ext, pack):
    even_ref, odd_ref, col_ref = refs
    size_x = v_ref.shape[1] // layers
    west_ok, east_ok, _, _ = place()
    for c in range(3):
        fill(ext, c, v_ref, c, size_x, layers)
    inner = slice(PAD, PAD + layers)
    extend(ext, ((0, 0, 0), (1, 0, 1), (2, 1, 1), (3, 2, 1)), below, west_ok, layers)
    over = size_x + 2
    rows = ((0, 0, over), (1, 1, over), (2, 1, over + 1), (3, 2, over), (4, 2, over + 1))
    extend(ext, rows, above, east_ok, layers)

    def step(x, carry):
        cut = pl.ds(pl.multiple_of(x * layers, layers), layers)
        ghost = cols[cut, :]
        vx, vy, vz = [ext[c, x + 2, inner, :] for c in range(3)]
        gx, gy, gz = roll(ghost, -1), roll(ghost, -5), roll(ghost, -7)
        dx = across(ext, 0, x, False, layers)
        dy = slopes(vy, gy, False)
        dz = down(ext, 2, x, False, layers)
        both = mat_ref[0, cut, :] * (dx + dy + dz)
        twice = mat_ref[1, cut, :]
        xx = old(0, x, cut) + (both + twice * dx)
        yy = old(1, x, cut) + (both + twice * dy)
        zz = old(2, x, cut) + (both + twice * dz)
        xy = old(3, x, cut) + mat_ref[2, cut, :] * (
            slopes(vx, gx, True) + across(ext, 1, x, True, layers)
        )
        xz = old(4, x, cut) + mat_ref[3, cut, :] * (
            down(ext, 0, x, True, layers) + across(ext, 2, x, True, layers)
        )
        yz = old(5, x, cut) + mat_ref[4, cut, :] * (
            down(ext, 1, x, True, layers) + slopes(vz, gz, True)
        )
        for c, value in enumerate((xx, yy, zz, xy, xz, yz)):
            out_ref[c, cut, :] = value
        pack[cut, :] = packed([(yy, 0, 3, 1), (xy, 3, 3, 5), (yz, 6, 3, 8)])
        return carry

    for strip in range(size_x // STRIP):
        ready(strip)
        lax.fori_loop(strip * STRIP, (strip + 1) * STRIP, step, 0, unroll=4)
    send_columns(pack, col_ref)

    def slab(c, x):
        return out_ref[c, x * layers : (x + 1) * layers, :]

    up = [slab(c, size_x - x) for c, x in ((0, 1), (3, 2), (3, 1), (4, 2), (4, 1))]
    two_ways(up, [slab(c, x) for c, x in ((0, 0), (0, 1), (3, 0), (4, 0))], even_ref, odd_ref)


def begin_kernel(
    layers,
    v_ref,
    b_ref,
    m_ref,
    s_ref,
    l_ref,
    stiff_hbm,
    x_even,
    x_odd,
    y_even,
    y_odd,
    table_ref,
    out_ref,
    even_ref,
    odd_ref,
    col_ref,
    mat_ref,
    buoy_ref,
    stiff_ref,
    bs,
    ms,
    tb,
    tm,
    ext,
    cols,
    pack,
    sems,
):
    half = stiff_ref.shape[0]
    half = stiff_ref.shape[0]
    copies = fetch([stiff_hbm.at[pl.ds(0, half)]], [stiff_ref], sems)
    _, _, south_ok, north_ok = place()
    below, above = below_above("gx", x_even, x_odd)
    receive_columns(y_even, y_odd, (0, 3, 4, 6), south_ok, north_ok, cols)
    materials(layers, b_ref, l_ref, m_ref, above, cols, table_ref, mat_ref, buoy_ref, bs, ms, tb, tm)

    def ready(strip):
        pass

    def old(c, x, cut):
        return s_ref[c, cut, :]

    refs = (even_ref, odd_ref, col_ref)
    stresses(layers, v_ref, old, ready, mat_ref, below, above, cols, out_ref, refs, ext, pack)
    copies[0].wait()


def stress_kernel(
    layers,
    v_ref,
    s_hbm,
    mat_hbm,
    x_even,
    x_odd,
    y_even,
    y_odd,
    out_ref,
    even_ref,
    odd_ref,
    col_ref,
    s_ref,
    mat_ref,
    ext,
    cols,
    pack,
    sems,
):
    strips = v_ref.shape[1] // layers // STRIP
    cuts = [pl.ds(strip * STRIP * layers, STRIP * layers) for strip in range(strips)]
    sources, targets = [], []
    for cut in cuts:
        sources += [s_hbm.at[:, cut], mat_hbm.at[:, cut]]
        targets += [s_ref.at[:, cut], mat_ref.at[:, cut]]
    copies = fetch(sources, targets, sems)
    _, _, south_ok, north_ok = place()
    below, above = below_above("gx", x_even, x_odd)
    receive_columns(y_even, y_odd, (0, 3, 4, 6), south_ok, north_ok, cols)

    def ready(strip):
        copies[2 * strip].wait()
        copies[2 * strip + 1].wait()

    def old(c, x, cut):
        return s_ref[c, cut, :]

    refs = (even_ref, odd_ref, col_ref)
    stresses(layers, v_ref, old, ready, mat_ref, below, above, cols, out_ref, refs, ext, pack)


def moving(layers, v_ref, s_ref, buoy_ref, halo, push_ref, ext, cols):
    x_even, x_odd, y_even, y_odd = halo
    size_x = v_ref.shape[1] // layers
    west_ok, east_ok, south_ok, north_ok = place()
    below, above = below_above("gx", x_even, x_odd)
    receive_columns(y_even, y_odd, (0, 3, 4, 6, 7), south_ok, north_ok, cols)
    for c, src in enumerate((0, 3, 4, 5, 2)):
        fill(ext, c, s_ref, src, size_x, layers)
    inner = slice(PAD, PAD + layers)
    rows = ((0, 0, 1), (1, 1, 0), (2, 1, 1), (3, 2, 0), (4, 2, 1))
    extend(ext, rows, below, west_ok, layers)
    over = size_x + 2
    extend(ext, ((0, 0, over), (1, 0, over + 1), (2, 1, over), (3, 2, over)), above, east_ok, layers)

    def fresh(x, cut):
        ghost = cols[cut, :]
        yy, xy, yz = s_ref[1, cut, :], ext[1, x + 2, inner, :], ext[3, x + 2, inner, :]
        gyy, gxy, gyz = roll(ghost, -1), roll(ghost, -5), roll(ghost, -8)
        ax = across(ext, 0, x, True, layers) + slopes(xy, gxy, False) + down(ext, 2, x, False, layers)
        ay = across(ext, 1, x, False, layers) + slopes(yy, gyy, True) + down(ext, 3, x, False, layers)
        az = across(ext, 2, x, False, layers) + slopes(yz, gyz, False) + down(ext, 4, x, True, layers)
        layer = lax.broadcasted_iota(jnp.int32, yy.shape, 0)
        result = []
        for c, accel in enumerate((ax, ay, az)):
            pushed = jnp.where(layer == 0, push_ref[c, pl.ds(x, 1), :], 0.0)
            result.append(v_ref[c, cut, :] + buoy_ref[c, cut, :] * accel + pushed)
        return result

    return fresh


def velocity_kernel(
    layers,
    v_ref,
    s_ref,
    buoy_ref,
    x_even,
    x_odd,
    y_even,
    y_odd,
    push_ref,
    out_ref,
    even_ref,
    odd_ref,
    col_ref,
    ext,
    cols,
    pack,
):
    size_x = v_ref.shape[1] // layers
    halo = (x_even, x_odd, y_even, y_odd)
    fresh = moving(layers, v_ref, s_ref, buoy_ref, halo, push_ref, ext, cols)

    def step(x, carry):
        cut = pl.ds(pl.multiple_of(x * layers, layers), layers)
        v = fresh(x, cut)
        for c in range(3):
            out_ref[c, cut, :] = v[c]
        pack[cut, :] = packed([(v[0], 0, 3, 1), (v[1], 3, 3, 5), (v[2], 6, 3, 7)])
        return carry

    lax.fori_loop(0, size_x, step, 0, unroll=4)
    send_columns(pack, col_ref)

    def slab(c, x):
        return out_ref[c, x * layers : (x + 1) * layers, :]

    up = [slab(c, size_x - x) for c, x in ((0, 2), (0, 1), (1, 1), (2, 1))]
    down_rows = [slab(c, x) for c, x in ((0, 0), (1, 0), (1, 1), (2, 0), (2, 1))]
    two_ways(up, down_rows, even_ref, odd_ref)


def third(value, e):
    d = lanes_of(value).astype(f32)
    return d - 3.0 * jnp.floor((d + 0.5) * (1.0 / 3.0)) == e


def column(row):
    n = row.shape[1]
    same = lax.broadcasted_iota(jnp.int32, (n, n), 0) == lax.broadcasted_iota(jnp.int32, (n, n), 1)
    return jnp.sum(jnp.where(same, row, 0.0), axis=1, keepdims=True)


def slot_table(owner_ref, slots):
    number = owner_ref.shape[1]
    owner = owner_ref[...].astype(f32)
    owner_col = column(owner)
    same = owner_col == owner
    i = lax.broadcasted_iota(jnp.int32, same.shape, 0)
    j = lax.broadcasted_iota(jnp.int32, same.shape, 1)
    slot_row = owner * CAP + jnp.sum(jnp.where(same & (i < j), 1.0, 0.0), axis=0, keepdims=True)
    slot_col = owner_col * CAP + jnp.sum(jnp.where(same & (j < i), 1.0, 0.0), axis=1, keepdims=True)
    to_slot = lax.broadcasted_iota(jnp.int32, (slots, number), 0).astype(f32) == slot_row
    of_slot = lax.broadcasted_iota(jnp.int32, (number, slots), 1).astype(f32) == slot_col
    return jnp.where(to_slot, 1.0, 0.0), jnp.where(of_slot, 1.0, 0.0)


def counted(counts_ref, shape):
    return lax.broadcasted_iota(jnp.int32, shape, 1).astype(f32) < column(
        counts_ref[...].astype(f32)
    )


def table(
    span,
    rate_ref,
    coupling_ref,
    contact_ref,
    counts_ref,
    owner_ref,
    corner_ref,
    out_ref,
):
    number, width = rate_ref.shape
    slots = out_ref.shape[0]
    mask = counted(counts_ref, (number, width))
    rate = jnp.where(mask, rate_ref[...], 0.0)
    coupling = jnp.where(mask, coupling_ref[...], 0.0)
    contact = contact_ref[...]
    weights = contact / jnp.sum(contact, axis=1, keepdims=True)
    corner = column(corner_ref[...].astype(f32))
    start_x = jnp.floor((corner + 0.5) * (1.0 / span))
    start_y = corner - start_x * span
    row = jnp.concatenate([weights, jnp.zeros((number, 128 - weights.shape[1]), f32)], axis=1)
    lane = lanes_of(row)
    row = jnp.where(lane == AT_X, start_x, row)
    row = jnp.where(lane == AT_Y, start_y, row)
    sums = (
        (AT_RATE, coupling * rate),
        (AT_COUPLING, coupling),
        (AT_SQUARE, time_step * coupling * coupling),
    )
    row = sums_by_third(row, sums)
    to_slot, _ = slot_table(owner_ref, slots)
    out_ref[...] = jnp.dot(to_slot, row, precision=exact, preferred_element_type=f32)


def first_kernel(layers, v_hbm, b_hbm, m_hbm, *refs):
    outs, near, pack, sems = refs[:6], refs[6:9], refs[9], refs[10]
    for copy in fetch((v_hbm, b_hbm, m_hbm), near, sems):
        copy.wait()
    edges(layers, *near, *outs, pack)


def table_kernel(span, layers, shear_ref, *refs):
    table(span, *refs)
    first = shear_ref[pl.ds(0, layers), 0:1]
    spot = lax.broadcasted_iota(jnp.int32, (layers, 128), 1) - AT_CORNER
    own = spot == lax.broadcasted_iota(jnp.int32, (layers, 128), 0)
    refs[-1][...] += jnp.sum(jnp.where(own, first, 0.0), axis=0, keepdims=True)


def sums_by_third(row, sums):
    lane = lanes_of(row)
    for at, value in sums:
        for e in range(3):
            total = jnp.sum(jnp.where(third(value, e), value, 0.0), axis=1, keepdims=True)
            row = jnp.where(lane == at + e, total, row)
    return row


def fetch_strips(stiff_hbm, begin, stiff_ref, sems):
    size = stiff_ref.shape[0] // sems.shape[0]
    strips = range(sems.shape[0])
    return fetch(
        [stiff_hbm.at[pl.ds(begin + c * size, size)] for c in strips],
        [stiff_ref.at[pl.ds(c * size, size)] for c in strips],
        sems,
    )


def products(stiff_ref, at, drift_ref, out_ref, begin, end):
    group = 16
    for g in range(begin // group * group, end, group):
        rounded = drift_ref[g : g + group, :].astype(jnp.bfloat16)
        row = lax.broadcasted_iota(jnp.int32, rounded.shape, 0)
        low, high = max(g, begin), min(g + group, end)
        total = out_ref[g : g + group, :]
        for b in range(low, high):
            part = lax.dot_general(
                rounded, stiff_ref[b - at], (((1,), (1,)), ((), ())), preferred_element_type=f32
            )
            total = jnp.where(row == b - g, part, total)
        out_ref[g : g + group, :] = total


def pull_kernel(
    stiff_ref,
    stiff_hbm,
    raw_ref,
    rate_ref,
    coupling_ref,
    counts_ref,
    owner_ref,
    base_ref,
    drift_out,
    next_ref,
    pull,
    rest_ref,
    sems,
):
    number, half = drift_out.shape[0], stiff_ref.shape[0]
    copies = fetch_strips(stiff_hbm, half, rest_ref, sems)
    mask = counted(counts_ref, drift_out.shape)
    drift_out[...] = jnp.where(mask, raw_ref[...], 0.0)
    pull[...] = jnp.zeros(pull.shape, f32)
    products(stiff_ref, 0, drift_out, pull, 0, half)
    size = (number - half) // len(copies)
    for c, copy in enumerate(copies):
        copy.wait()
        products(rest_ref, half, drift_out, pull, half + c * size, half + (c + 1) * size)
    rate = jnp.where(mask, rate_ref[...], 0.0)
    coupling = jnp.where(mask, coupling_ref[...], 0.0)
    base = rate - time_step * pull[...] - time_step * coupling * rate
    base = jnp.where(mask, base, 0.0)
    base_ref[...] = base
    row = sums_by_third(jnp.zeros((number, 128), f32), ((AT_NEXT, coupling * base),))
    to_slot, _ = slot_table(owner_ref, next_ref.shape[0])
    next_ref[...] = jnp.dot(to_slot, row, precision=exact, preferred_element_type=f32)


def motion(maps_ref, v_ref, layers):
    size_x, slots, size_y = maps_ref.shape
    total = [jnp.zeros((slots, size_y), f32) for _ in range(3)]
    for x in range(size_x):
        part = maps_ref[x]
        for c in range(3):
            total[c] = total[c] + part * v_ref[c, x * layers : x * layers + 1, :]
    return [jnp.sum(t, axis=1, keepdims=True) for t in total]


def spread(at, reaction, out_ref):
    for x in range(out_ref.shape[1]):
        part = at(x)
        for c in range(3):
            out_ref[c, x : x + 1, :] = jnp.sum(part * reaction[c], axis=0, keepdims=True)


def footprints(table):
    lane = lanes_of(table)
    off_y = lane - table[:, AT_Y : AT_Y + 1].astype(jnp.int32)
    start_x = jnp.broadcast_to(table[:, AT_X : AT_X + 1], table.shape)
    within = (off_y >= 0) & (off_y < FOOT)
    inside = jnp.where(within, off_y, 0)
    lines = []
    for a in range(FOOT):
        picked = jnp.take_along_axis(table, inside + a * FOOT, axis=1)
        lines.append(jnp.where(within, picked, 0.0))

    def at(x):
        value = jnp.zeros(table.shape, f32)
        for a in range(FOOT):
            value = jnp.where(start_x == float(x - a), lines[a], value)
        return value

    return at


def surface_kernel(layers, table_ref, v_ref, maps_ref, moved_ref, push_ref):
    table = table_ref[...]
    lane = lanes_of(table)
    at = footprints(table)
    for x in range(maps_ref.shape[0]):
        maps_ref[x] = at(x)
    moved = motion(maps_ref, v_ref, layers)
    reaction = []
    rows = jnp.zeros(table.shape, f32)
    for c in range(3):
        rest, slope = (table[:, at + c : at + c + 1] for at in (AT_RATE, AT_COUPLING))
        reaction.append(time_step * FOOT * (rest - slope * moved[c]))
        rows = jnp.where(lane == FIRST + c, moved[c], rows)
    moved_ref[...] = rows
    spread(lambda x: maps_ref[x], reaction, push_ref)


def spread_thirds(moved, at, value):
    result = jnp.zeros(value.shape, f32)
    for e in range(3):
        result = jnp.where(third(value, e), moved[:, at + e : at + e + 1], result)
    return result


def motion_again_kernel(layers, v_ref, maps_ref, before_ref, next_ref, out_ref):
    moved = motion(maps_ref, v_ref, layers)
    rows = before_ref[...] + next_ref[...]
    lane = lanes_of(rows)
    for c in range(3):
        rows = jnp.where(lane == SECOND + c, moved[c], rows)
    out_ref[...] = rows


def prepare_kernel(
    sent_ref,
    back_ref,
    table_ref,
    base_ref,
    drift_ref,
    coupling_ref,
    counts_ref,
    owner_ref,
    push_ref,
    drift_out,
    rate_out,
):
    table, sent, back = table_ref[...], sent_ref[...], back_ref[...]
    reaction = []
    for c in range(3):
        rest = back[:, AT_NEXT + c : AT_NEXT + c + 1]
        rest = rest + table[:, AT_SQUARE + c : AT_SQUARE + c + 1] * sent[:, FIRST + c : FIRST + c + 1]
        slope = table[:, AT_COUPLING + c : AT_COUPLING + c + 1]
        reaction.append(time_step * FOOT * (rest - slope * sent[:, SECOND + c : SECOND + c + 1]))
    spread(footprints(table), reaction, push_ref)
    _, of_slot = slot_table(owner_ref, back.shape[0])
    moved = jnp.dot(of_slot, back, precision=exact, preferred_element_type=f32)
    coupling = coupling_ref[...]
    mask = counted(counts_ref, coupling.shape)
    rate = base_ref[...] + time_step * coupling * spread_thirds(moved, FIRST, coupling)
    rate = jnp.where(mask, rate, 0.0)
    drift_out[...] = jnp.where(mask, drift_ref[...] + time_step * rate, 0.0)
    rate_out[...] = rate - time_step * coupling * (rate - spread_thirds(moved, SECOND, coupling))


def finish_kernel(
    layers,
    v_ref,
    s_ref,
    buoy_ref,
    x_even,
    x_odd,
    y_even,
    y_odd,
    push_ref,
    half,
    rate_ref,
    counts_ref,
    stiff_hbm,
    out_hbm,
    drift_out,
    rate_out,
    out_ref,
    ext,
    cols,
    pull,
    stiff_ref,
    sems,
    out_sems,
):
    fetch_strips(stiff_hbm, 0, stiff_ref, sems)
    size_x = v_ref.shape[1] // layers
    halo = (x_even, x_odd, y_even, y_odd)
    fresh = moving(layers, v_ref, s_ref, buoy_ref, halo, push_ref, ext, cols)
    strips = sems.shape[0]
    share = half.shape[0] // strips
    batch = size_x // strips

    def advance(strip):
        for i in range(batch):
            x = strip * batch + i
            v = fresh(x, pl.ds(pl.multiple_of(x * layers, layers), layers))
            for c in range(3):
                out_ref[x // TILE, c, :, lax.rem(x, TILE), :] = v[c]

    def multiply(strip):
        cut = pl.ds(pl.multiple_of(strip * share, share), share)
        pltpu.make_async_copy(stiff_hbm.at[cut], stiff_ref.at[cut], sems.at[strip]).wait()
        rounded = half[cut, :].astype(jnp.bfloat16)
        row = lax.broadcasted_iota(jnp.int32, rounded.shape, 0)
        total = jnp.zeros(rounded.shape, f32)
        for b in range(share):
            part = lax.dot_general(
                rounded,
                stiff_ref[strip * share + b],
                (((1,), (1,)), ((), ())),
                preferred_element_type=f32,
            )
            total = jnp.where(row == b, part, total)
        pull[cut, :] = total

    def leave(tile):
        return pltpu.make_async_copy(out_ref.at[tile], out_hbm.at[:, :, tile], out_sems.at[tile])

    def step(strip, carry):
        multiply(strip - 1)
        advance(strip)
        return carry

    tiles = size_x // TILE
    for tile in range(tiles):
        begin, end = tile * strips // tiles, (tile + 1) * strips // tiles
        if tile == 0:
            advance(0)
            begin = 1
        lax.fori_loop(begin, end, step, 0)
        leave(tile).start()
    multiply(strips - 1)
    mask = counted(counts_ref, half.shape)
    rate = jnp.where(mask, rate_ref[...] - time_step * pull[...], 0.0)
    rate_out[...] = rate
    drift_out[...] = jnp.where(mask, half[...] + time_step * rate, 0.0)
    for tile in range(tiles):
        leave(tile).wait()


def trade(rows):
    devices = lax.axis_size("gx") * lax.axis_size("gy")
    blocks = rows.reshape(devices, CAP, rows.shape[1])
    blocks = lax.all_to_all(blocks, ("gx", "gy"), split_axis=0, concat_axis=0, tiled=True)
    return blocks.reshape(rows.shape)


def body(
    soil_velocity,
    soil_stress,
    buoyancy,
    lame_first,
    shear_modulus,
    stiffness,
    storey_drift,
    drift_rate,
    coupling,
    contact,
    dof_counts,
    owner_tile,
    corner_cell,
):
    layers, size_x, size_y = buoyancy.shape
    cells = layers * size_x
    number, width = storey_drift.shape
    slots = lax.axis_size("gx") * lax.axis_size("gy") * CAP
    span = size_y - FOOT + 1
    counts, owner, corner = (a.reshape(1, number) for a in (dof_counts, owner_tile, corner_cell))

    def bind(kernel, *fixed):
        def bound(*refs):
            kernel(*fixed, *refs)

        return bound

    def vm(*dims):
        return pltpu.VMEM(dims, f32)

    field = vm(cells, size_y)
    tall = layers + 2 * PAD
    plane = near_by(number, width)
    dma = pltpu.SemaphoreType.DMA
    flat = [a.reshape(cells, size_y) for a in (buoyancy, shear_modulus, lame_first)]
    far = (soil_velocity.reshape(3, cells, size_y), *flat[:2])
    vt, bt, mt, one, two, col = call(
        bind(first_kernel, layers),
        "first",
        (
            near_by(3, cells, size_y),
            near_by(cells, size_y),
            near_by(cells, size_y),
            near_by(7, layers, size_y),
            near_by(7, layers, size_y),
            near_by(16, cells),
        ),
        [Far(a) for a in far],
        [pltpu.VMEM(a.shape, a.dtype) for a in far] + [field, dma((len(far),))],
    )
    (rows,) = call(
        bind(table_kernel, span, layers),
        "table",
        (near_by(slots, 128),),
        (mt, drift_rate, coupling, contact, counts, owner, corner),
    )

    def exchange(one, two, col):
        return swap(one, "gx", 0), swap(two, "gx", 1), swap(col, "gy", 0), swap(col, "gy", 1)

    halo = exchange(one, two, col)
    rows = trade(rows)
    st, lt = call(
        bind(load_kernel, layers),
        "load",
        (near_by(6, cells, size_y), near_by(cells, size_y)),
        (rows, Far(soil_stress.reshape(6, cells, size_y)), Far(flat[2])),
        [vm(6, cells, size_y), field, dma((7,))],
    )
    half = number // 2
    payload = (near_by(5, layers, size_y), near_by(5, layers, size_y), near_by(16, cells))
    ext = vm(3, size_x + 4, tall, size_y)
    stack = vm(size_x + 1, tall, size_y)
    st, one, two, col, means, buoys, stiff = call(
        bind(begin_kernel, layers),
        "begin",
        (
            near_by(6, cells, size_y),
            *payload,
            near_by(5, cells, size_y),
            near_by(3, cells, size_y),
            near_by(half, width, width, dtype=stiffness.dtype),
        ),
        (vt, bt, mt, st, lt, Far(stiffness), *halo, rows),
        [
            stack,
            stack,
            stack,
            stack,
            ext,
            field,
            field,
            dma((1,)),
        ],
    )

    halo = exchange(one, two, col)
    maps, moved, push = call(
        bind(surface_kernel, layers),
        "surface",
        (near_by(size_x, slots, size_y), near_by(slots, 128), near_by(3, size_x, size_y)),
        (rows, vt),
    )
    chunks = 4 if number % 8 == 0 else 1
    base, drift, following = call(
        pull_kernel,
        "pull",
        (plane, plane, near_by(slots, 128)),
        (stiff, Far(stiffness), storey_drift, drift_rate, coupling, counts, owner),
        [
            vm(number, width),
            pltpu.VMEM((number - half, width, width), stiffness.dtype),
            dma((chunks,)),
        ],
    )
    push, following = lax.optimization_barrier((push, following))
    bulk = vm(5, size_x + 4, tall, size_y)
    vt, one, two, col = call(
        bind(velocity_kernel, layers),
        "velocity",
        (near_by(3, cells, size_y), *payload),
        (vt, st, buoys, *halo, push),
        [bulk, field, field],
    )
    halo = exchange(one, two, col)
    (sent,) = call(
        bind(motion_again_kernel, layers),
        "motion_again",
        (near_by(slots, 128),),
        (vt, maps, moved, following),
    )
    vt, sent = lax.optimization_barrier((vt, sent))
    back = trade(sent)
    strips = size_x // STRIP
    st, one, two, col = call(
        bind(stress_kernel, layers),
        "stress",
        (near_by(6, cells, size_y), *payload),
        (vt, Far(st), Far(means), *halo),
        [
            vm(6, cells, size_y),
            vm(5, cells, size_y),
            ext,
            field,
            field,
            dma((2 * strips,)),
        ],
    )
    halo = exchange(one, two, col)
    sent, st = lax.optimization_barrier((sent, st))
    push, drift, rate = call(
        prepare_kernel,
        "prepare",
        (near_by(3, size_x, size_y), plane, plane),
        (sent, back, rows, base, drift, coupling, counts, owner),
    )
    tiles = size_x // TILE
    v, drift, rate = call(
        bind(finish_kernel, layers),
        "finish",
        (
            pltpu.HBM((3, layers, tiles, TILE, size_y), f32),
            shape(number, width),
            shape(number, width),
        ),
        (
            vt,
            st,
            buoys,
            *halo,
            push,
            drift,
            rate,
            counts,
            Far(stiffness),
        ),
        [
            vm(tiles, 3, layers, TILE, size_y),
            bulk,
            field,
            vm(number, width),
            pltpu.VMEM(stiffness.shape, stiffness.dtype),
            dma((chunks,)),
            dma((tiles,)),
        ],
        far_outs=(0,),
    )
    return v.reshape(soil_velocity.shape), drift, rate


def solution(mesh):
    both = ("gx", "gy")
    soil = P(None, None, "gx", "gy")
    cell = P(None, "gx", "gy")
    placed = (
        soil,
        soil,
        cell,
        cell,
        cell,
        P(both, None, None),
        P(both, None),
        P(both, None),
        P(both, None),
        P(both, None),
        P(both),
        P(both, None),
        P(both),
    )
    return jax.shard_map(
        body,
        mesh=mesh,
        in_specs=placed,
        out_specs=(soil, P(both, None), P(both, None)),
        check_vma=False,
    )
```

```python
import jax
import jax.numpy as jnp
from jax import lax
from jax.experimental import pallas as pl
from jax.experimental.pallas import tpu as pltpu
from jax.sharding import PartitionSpec as P

FOOT = 8
CAP = 2
PAD = 8
STRIP = 4
TILE = 8

near = 9.0 / 8.0
far = 1.0 / 24.0
time_step = 0.3
exact = lax.Precision.HIGHEST
f32 = jnp.float32

AT_X, AT_Y, AT_RATE, AT_COUPLING, AT_SQUARE, AT_CORNER = 64, 65, 66, 69, 72, 75
FIRST, SECOND, AT_NEXT = 0, 3, 8


COSTS = {
    "first": 30_000_000,
    "table": 60_000_000,
    "load": 20_000_000,
    "begin": 40_000_000,
    "stress": 25_000_000,
    "surface": 10_000_000,
    "pull": 30_000_000,
    "velocity": 25_000_000,
    "motion_again": 10_000_000,
    "prepare": 60_000_000,
    "finish": 60_000_000,
}


class Far:
    def __init__(self, value):
        self.value = value


def call(kernel, name, outs, args, scratch=(), far_outs=()):
    cost = COSTS[name]
    specs, values = [], []
    for a in args:
        far = isinstance(a, Far)
        a = a.value if far else a
        values.append(pltpu.with_memory_space_constraint(a, pltpu.HBM if far else pltpu.VMEM))
        specs.append(pl.BlockSpec(memory_space=pl.ANY if far else pltpu.VMEM))
    return pl.pallas_call(
        kernel,
        name=name,
        out_shape=outs,
        in_specs=specs,
        out_specs=tuple(
            pl.BlockSpec(memory_space=pl.ANY if i in far_outs else pltpu.VMEM)
            for i in range(len(outs))
        ),
        scratch_shapes=list(scratch),
        cost_estimate=pl.CostEstimate(flops=1000*cost, bytes_accessed=cost, transcendentals=0),
        compiler_params=pltpu.CompilerParams(vmem_limit_bytes=16 * 2**20),
    )(*values)


def shape(*dims):
    return jax.ShapeDtypeStruct(dims, f32)


def near_by(*dims, dtype=f32):
    return pltpu.VMEM(dims, dtype)


def fetch(sources, targets, sems):
    copies = [
        pltpu.make_async_copy(source, target, sems.at[i])
        for i, (source, target) in enumerate(zip(sources, targets))
    ]
    for copy in copies:
        copy.start()
    return copies


def swap(block, axis, odd):
    size = lax.axis_size(axis)
    pairs = [(i % size, (i + 1) % size) for i in range(odd, size + odd, 2)]
    return lax.ppermute(block, axis, pairs + [(b, a) for a, b in pairs])


def even(axis):
    return lax.rem(lax.axis_index(axis), 2) == 0


def two_ways(up, down, even_ref, odd_ref):
    lead = even("gx")
    blank = jnp.zeros(even_ref.shape[1:], f32)
    for row in range(even_ref.shape[0]):
        a = up[row] if row < len(up) else blank
        b = down[row] if row < len(down) else blank
        even_ref[row] = jnp.where(lead, a, b)
        odd_ref[row] = jnp.where(lead, b, a)


def below_above(axis, even_ref, odd_ref):
    lead = even(axis)

    def below(index):
        return jnp.where(lead, odd_ref[index], even_ref[index])

    def above(index):
        return jnp.where(lead, even_ref[index], odd_ref[index])

    return below, above


def lanes_of(value):
    return lax.broadcasted_iota(jnp.int32, value.shape, len(value.shape) - 1)


def roll(value, amount):
    return pltpu.roll(value, amount % value.shape[-1], len(value.shape) - 1)


def packed(pieces):
    result = None
    for slab, first, count, amount in pieces:
        moved = roll(slab, amount) if amount else slab
        if result is None:
            result = moved
        else:
            lane = lanes_of(slab)
            result = jnp.where((lane >= first) & (lane < first + count), moved, result)
    return result


def send_columns(pack_ref, out_ref):
    rows, width = out_ref.shape
    for block in range(width // 128):
        part = pack_ref[block * 128 : (block + 1) * 128, :]
        out_ref[:, block * 128 : (block + 1) * 128] = part.T[:rows]


def receive_columns(even_ref, odd_ref, from_south, south_ok, north_ok, out_ref):
    rows, width = even_ref.shape
    below, above = below_above("gy", even_ref, odd_ref)
    for block in range(width // 128):
        cut = slice(block * 128, (block + 1) * 128)
        south = jnp.where(south_ok, below((slice(None), cut)), 0.0)
        north = jnp.where(north_ok, above((slice(None), cut)), 0.0)
        row = lax.broadcasted_iota(jnp.int32, south.shape, 0)
        taken = row == from_south[0]
        for other in from_south[1:]:
            taken = taken | (row == other)
        part = jnp.where(taken, south, north)
        whole = jnp.concatenate([part, jnp.zeros((128 - rows, 128), f32)], axis=0)
        out_ref[cut, :] = whole.T


def bands(forward, amount):
    row = lax.broadcasted_iota(jnp.int32, (256, 128), 0)
    lane = row - 128
    beyond = jnp.where(lane < amount, lane - amount, 128 + lane - amount)
    shift = jnp.where(row < 128, row, beyond) - lax.broadcasted_iota(jnp.int32, (256, 128), 1)
    first, last = (amount - 1, amount + 1) if forward else (amount - 2, amount)
    valid = (row < 128) | ((lane >= first) & (lane <= last))
    value = jnp.zeros((256, 128), f32)
    at = 0 if forward else -1
    for step, entry in ((at + 1, 27.0), (at, -27.0), (at + 2, -1.0), (at - 1, 1.0)):
        value = jnp.where(shift == step, entry, value)
    return jnp.where(valid, value, 0.0).astype(jnp.bfloat16)


def parted(value):
    large = value.astype(jnp.bfloat16)
    return large, (value - large.astype(f32)).astype(jnp.bfloat16)


def slopes(fields, cols, out_ref):
    matrices = [bands(forward, amount) for _, forward, amount in fields]
    size = 256
    for begin in range(0, cols.shape[0], size):
        cut = slice(begin, begin + size)
        ghost = parted(cols[cut, :])
        for i, (read, _, _) in enumerate(fields):
            total = None
            for own, other in zip(parted(read(cut)), ghost):
                both = jnp.concatenate([own, other], axis=1)
                part = jnp.dot(both, matrices[i], preferred_element_type=f32)
                total = part if total is None else total + part
            out_ref[i, cut, :] = total * (1.0 / 24.0)


def across(ext, c, x, forward, layers):
    def at(d):
        return ext[c, x + 2 + d, PAD : PAD + layers, :]

    if forward:
        return near * (at(1) - at(0)) - far * (at(2) - at(-1))
    return near * (at(0) - at(-1)) - far * (at(1) - at(-2))


def down(ext, c, x, forward, layers):
    def at(d):
        return ext[c, x + 2, PAD + d : PAD + layers + d, :]

    if forward:
        return near * (at(1) - at(0)) - far * (at(2) - at(-1))
    return near * (at(0) - at(-1)) - far * (at(1) - at(-2))


def place():
    gx, gy = lax.axis_index("gx"), lax.axis_index("gy")
    nx, ny = lax.axis_size("gx"), lax.axis_size("gy")
    return gx > 0, gx < nx - 1, gy > 0, gy < ny - 1


def fill(ext, c, source, src, size_x, layers):
    for x in range(size_x):
        ext[c, x + 2, 0:PAD, :] = jnp.zeros((PAD, 128), f32)
        ext[c, x + 2, PAD : PAD + layers, :] = source[src, x * layers : (x + 1) * layers, :]
        ext[c, x + 2, PAD + layers : PAD + layers + PAD, :] = jnp.zeros((PAD, 128), f32)


def edges(layers, v_ref, b_ref, m_ref, vt_ref, bt_ref, mt_ref, even_ref, odd_ref, col_ref, pack):
    size_x = vt_ref.shape[1] // layers

    def slab(ref, x):
        return ref[x * layers : (x + 1) * layers, :]

    for x in range(size_x):
        cut = pl.ds(x * layers, layers)
        turned = pl.ds(x, layers, stride=size_x)
        v = [v_ref[c, turned, :] for c in range(3)]
        buoy, shear = b_ref[turned, :], m_ref[turned, :]
        for c in range(3):
            vt_ref[c, cut, :] = v[c]
        bt_ref[cut, :] = buoy
        mt_ref[cut, :] = shear
        pack[cut, :] = packed(
            [(v[0], 0, 3, 1), (v[1], 3, 3, 5), (v[2], 6, 3, 7), (buoy, 9, 1, 9), (shear, 10, 1, 10)]
        )
    last = size_x - 1
    up = [slab(vt_ref.at[c], x) for c, x in ((0, last - 1), (0, last), (1, last), (2, last))]
    down = [slab(vt_ref.at[c], x) for c, x in ((0, 0), (1, 0), (1, 1), (2, 0), (2, 1))]
    two_ways(up, down + [slab(bt_ref, 0), slab(mt_ref, 0)], even_ref, odd_ref)
    send_columns(pack, col_ref)


def load_kernel(layers, after_ref, s_hbm, l_hbm, st_ref, lt_ref, s_ref, l_ref, sems):
    del after_ref
    size_x = l_ref.shape[0] // layers
    copies = fetch(
        [l_hbm] + [s_hbm.at[c] for c in range(6)], [l_ref] + [s_ref.at[c] for c in range(6)], sems
    )
    for c, copy in enumerate(copies):
        copy.wait()
        for x in range(size_x):
            cut, turned = pl.ds(x * layers, layers), pl.ds(x, layers, stride=size_x)
            if c == 0:
                lt_ref[cut, :] = l_ref[turned, :]
            else:
                st_ref[c - 1, cut, :] = s_ref[c - 1, turned, :]


def materials(layers, b_ref, l_ref, m_ref, above, cols, table_ref, mat_ref, buoy_ref, bs, ms, tb, tm):
    size_x = b_ref.shape[0] // layers
    _, east_ok, _, north_ok = place()
    nx, ny = lax.axis_size("gx"), lax.axis_size("gy")
    beyond = lax.rem(lax.axis_index("gx") + 1, nx) * ny + lax.rem(lax.axis_index("gy") + 1, ny)
    inner = slice(PAD, PAD + layers)
    for x in range(size_x):
        cut = slice(x * layers, (x + 1) * layers)
        bs[x, inner, :] = b_ref[cut, :]
        ms[x, inner, :] = m_ref[cut, :]
        part = cols[cut, :]
        tb[x, inner, :] = roll(part, -9)
        tm[x, inner, :] = roll(part, -10)
    bs[size_x, inner, :] = above(5)
    ms[size_x, inner, :] = above(6)
    line = jnp.broadcast_to(table_ref[pl.ds(beyond * CAP, 1), :], (layers, 128))
    own = lanes_of(line) - AT_CORNER == lax.broadcasted_iota(jnp.int32, line.shape, 0)
    corner = jnp.sum(jnp.where(own, line, 0.0), axis=1, keepdims=True)
    tm[size_x, inner, :] = jnp.broadcast_to(corner, line.shape)
    zero = jnp.zeros((PAD, 128), f32)
    for x in range(size_x + 1):
        bs[x, PAD + layers : PAD + layers + PAD, :] = zero
        ms[x, PAD + layers : PAD + layers + PAD, :] = zero
        tm[x, PAD + layers : PAD + layers + PAD, :] = zero
    below = slice(PAD + 1, PAD + layers + 1)

    def step(x, carry):
        cut = pl.ds(pl.multiple_of(x * layers, layers), layers)
        b, m = bs[x, inner, :], ms[x, inner, :]
        lane = lanes_of(b)
        layer = lax.broadcasted_iota(jnp.int32, b.shape, 0)
        in_x = (x < size_x - 1) | east_ok
        in_y = (lane < 127) | north_ok
        in_z = layer < layers - 1

        def north(value, ghost):
            return roll(jnp.where(lane == 0, ghost, value), -1)

        b_e = jnp.where(in_x, bs[x + 1, inner, :], b)
        b_n = jnp.where(in_y, north(b, tb[x, inner, :]), b)
        b_z = jnp.where(in_z, bs[x, below, :], b)
        m_e = jnp.where(in_x, ms[x + 1, inner, :], m)
        m_n = jnp.where(in_y, north(m, tm[x, inner, :]), m)
        m_z = jnp.where(in_z, ms[x, below, :], m)
        m_en = jnp.where(in_y & in_x, north(ms[x + 1, inner, :], tm[x + 1, inner, :]), m)
        m_ez = jnp.where(in_z & in_x, ms[x + 1, below, :], m)
        m_nz = jnp.where(in_z & in_y, north(ms[x, below, :], tm[x, below, :]), m)
        mat_ref[0, cut, :] = time_step * l_ref[cut, :]
        mat_ref[1, cut, :] = (2.0 * time_step) * m
        mat_ref[2, cut, :] = (0.25 * time_step) * (m + m_e + m_n + m_en)
        mat_ref[3, cut, :] = (0.25 * time_step) * (m + m_e + m_z + m_ez)
        mat_ref[4, cut, :] = (0.25 * time_step) * (m + m_n + m_z + m_nz)
        buoy_ref[0, cut, :] = (0.5 * time_step) * (b + b_e)
        buoy_ref[1, cut, :] = (0.5 * time_step) * (b + b_n)
        buoy_ref[2, cut, :] = (0.5 * time_step) * (b + b_z)
        return carry

    lax.fori_loop(0, size_x, step, 0, unroll=4)


def extend(ext, rows, at, ok, layers):
    for row, c, x in rows:
        ext[c, x, PAD : PAD + layers, :] = jnp.where(ok, at(row), 0.0)


def stresses(layers, v_ref, old, ready, mat_ref, below, above, cols, out_ref, refs, ext, pack, slope):
    even_ref, odd_ref, col_ref = refs
    size_x = v_ref.shape[1] // layers
    west_ok, east_ok, _, _ = place()
    for c in range(3):
        fill(ext, c, v_ref, c, size_x, layers)
    extend(ext, ((0, 0, 0), (1, 0, 1), (2, 1, 1), (3, 2, 1)), below, west_ok, layers)
    over = size_x + 2
    rows = ((0, 0, over), (1, 1, over), (2, 1, over + 1), (3, 2, over), (4, 2, over + 1))
    extend(ext, rows, above, east_ok, layers)

    fields = (
        (lambda cut: v_ref[1, cut, :], False, 5),
        (lambda cut: v_ref[0, cut, :], True, 1),
        (lambda cut: v_ref[2, cut, :], True, 7),
    )
    slopes(fields, cols, slope)

    def step(x, carry):
        cut = pl.ds(pl.multiple_of(x * layers, layers), layers)
        dx = across(ext, 0, x, False, layers)
        dy = slope[0, cut, :]
        dz = down(ext, 2, x, False, layers)
        both = mat_ref[0, cut, :] * (dx + dy + dz)
        twice = mat_ref[1, cut, :]
        xx = old(0, x, cut) + (both + twice * dx)
        yy = old(1, x, cut) + (both + twice * dy)
        zz = old(2, x, cut) + (both + twice * dz)
        xy = old(3, x, cut) + mat_ref[2, cut, :] * (
            slope[1, cut, :] + across(ext, 1, x, True, layers)
        )
        xz = old(4, x, cut) + mat_ref[3, cut, :] * (
            down(ext, 0, x, True, layers) + across(ext, 2, x, True, layers)
        )
        yz = old(5, x, cut) + mat_ref[4, cut, :] * (
            down(ext, 1, x, True, layers) + slope[2, cut, :]
        )
        for c, value in enumerate((xx, yy, zz, xy, xz, yz)):
            out_ref[c, cut, :] = value
        pack[cut, :] = packed([(yy, 0, 3, 1), (xy, 3, 3, 5), (yz, 6, 3, 8)])
        return carry

    for strip in range(size_x // STRIP):
        ready(strip)
        lax.fori_loop(strip * STRIP, (strip + 1) * STRIP, step, 0, unroll=4)
    send_columns(pack, col_ref)

    def slab(c, x):
        return out_ref[c, x * layers : (x + 1) * layers, :]

    up = [slab(c, size_x - x) for c, x in ((0, 1), (3, 2), (3, 1), (4, 2), (4, 1))]
    two_ways(up, [slab(c, x) for c, x in ((0, 0), (0, 1), (3, 0), (4, 0))], even_ref, odd_ref)


def begin_kernel(
    layers,
    v_ref,
    b_ref,
    m_ref,
    s_ref,
    l_ref,
    stiff_hbm,
    x_even,
    x_odd,
    y_even,
    y_odd,
    table_ref,
    out_ref,
    even_ref,
    odd_ref,
    col_ref,
    mat_ref,
    buoy_ref,
    stiff_ref,
    bs,
    ms,
    tb,
    tm,
    ext,
    cols,
    pack,
    slope,
    sems,
):
    half = stiff_ref.shape[0]
    half = stiff_ref.shape[0]
    copies = fetch([stiff_hbm.at[pl.ds(0, half)]], [stiff_ref], sems)
    _, _, south_ok, north_ok = place()
    below, above = below_above("gx", x_even, x_odd)
    receive_columns(y_even, y_odd, (0, 3, 4, 6), south_ok, north_ok, cols)
    materials(layers, b_ref, l_ref, m_ref, above, cols, table_ref, mat_ref, buoy_ref, bs, ms, tb, tm)

    def ready(strip):
        pass

    def old(c, x, cut):
        return s_ref[c, cut, :]

    refs = (even_ref, odd_ref, col_ref)
    stresses(layers, v_ref, old, ready, mat_ref, below, above, cols, out_ref, refs, ext, pack, slope)
    copies[0].wait()


def stress_kernel(
    layers,
    v_ref,
    s_hbm,
    mat_hbm,
    x_even,
    x_odd,
    y_even,
    y_odd,
    out_ref,
    even_ref,
    odd_ref,
    col_ref,
    s_ref,
    mat_ref,
    ext,
    cols,
    pack,
    slope,
    sems,
):
    strips = v_ref.shape[1] // layers // STRIP
    cuts = [pl.ds(strip * STRIP * layers, STRIP * layers) for strip in range(strips)]
    sources, targets = [], []
    for cut in cuts:
        sources += [s_hbm.at[:, cut], mat_hbm.at[:, cut]]
        targets += [s_ref.at[:, cut], mat_ref.at[:, cut]]
    copies = fetch(sources, targets, sems)
    _, _, south_ok, north_ok = place()
    below, above = below_above("gx", x_even, x_odd)
    receive_columns(y_even, y_odd, (0, 3, 4, 6), south_ok, north_ok, cols)

    def ready(strip):
        copies[2 * strip].wait()
        copies[2 * strip + 1].wait()

    def old(c, x, cut):
        return s_ref[c, cut, :]

    refs = (even_ref, odd_ref, col_ref)
    stresses(layers, v_ref, old, ready, mat_ref, below, above, cols, out_ref, refs, ext, pack, slope)


def moving(layers, v_ref, s_ref, buoy_ref, halo, push_ref, ext, cols, slope):
    x_even, x_odd, y_even, y_odd = halo
    size_x = v_ref.shape[1] // layers
    west_ok, east_ok, south_ok, north_ok = place()
    below, above = below_above("gx", x_even, x_odd)
    receive_columns(y_even, y_odd, (0, 3, 4, 6, 7), south_ok, north_ok, cols)
    for c, src in enumerate((0, 3, 4, 5, 2)):
        fill(ext, c, s_ref, src, size_x, layers)
    rows = ((0, 0, 1), (1, 1, 0), (2, 1, 1), (3, 2, 0), (4, 2, 1))
    extend(ext, rows, below, west_ok, layers)
    over = size_x + 2
    extend(ext, ((0, 0, over), (1, 0, over + 1), (2, 1, over), (3, 2, over)), above, east_ok, layers)

    fields = (
        (lambda cut: s_ref[3, cut, :], False, 5),
        (lambda cut: s_ref[1, cut, :], True, 1),
        (lambda cut: s_ref[5, cut, :], False, 8),
    )
    slopes(fields, cols, slope)

    def fresh(x, cut):
        ax = across(ext, 0, x, True, layers) + slope[0, cut, :] + down(ext, 2, x, False, layers)
        ay = across(ext, 1, x, False, layers) + slope[1, cut, :] + down(ext, 3, x, False, layers)
        az = across(ext, 2, x, False, layers) + slope[2, cut, :] + down(ext, 4, x, True, layers)
        layer = lax.broadcasted_iota(jnp.int32, ax.shape, 0)
        result = []
        for c, accel in enumerate((ax, ay, az)):
            pushed = jnp.where(layer == 0, push_ref[c, pl.ds(x, 1), :], 0.0)
            result.append(v_ref[c, cut, :] + buoy_ref[c, cut, :] * accel + pushed)
        return result

    return fresh


def velocity_kernel(
    layers,
    v_ref,
    s_ref,
    buoy_ref,
    x_even,
    x_odd,
    y_even,
    y_odd,
    push_ref,
    out_ref,
    even_ref,
    odd_ref,
    col_ref,
    ext,
    cols,
    pack,
    slope,
):
    size_x = v_ref.shape[1] // layers
    halo = (x_even, x_odd, y_even, y_odd)
    fresh = moving(layers, v_ref, s_ref, buoy_ref, halo, push_ref, ext, cols, slope)

    def step(x, carry):
        cut = pl.ds(pl.multiple_of(x * layers, layers), layers)
        v = fresh(x, cut)
        for c in range(3):
            out_ref[c, cut, :] = v[c]
        pack[cut, :] = packed([(v[0], 0, 3, 1), (v[1], 3, 3, 5), (v[2], 6, 3, 7)])
        return carry

    lax.fori_loop(0, size_x, step, 0, unroll=4)
    send_columns(pack, col_ref)

    def slab(c, x):
        return out_ref[c, x * layers : (x + 1) * layers, :]

    up = [slab(c, size_x - x) for c, x in ((0, 2), (0, 1), (1, 1), (2, 1))]
    down_rows = [slab(c, x) for c, x in ((0, 0), (1, 0), (1, 1), (2, 0), (2, 1))]
    two_ways(up, down_rows, even_ref, odd_ref)


def third(value, e):
    d = lanes_of(value).astype(f32)
    return d - 3.0 * jnp.floor((d + 0.5) * (1.0 / 3.0)) == e


def column(row):
    n = row.shape[1]
    same = lax.broadcasted_iota(jnp.int32, (n, n), 0) == lax.broadcasted_iota(jnp.int32, (n, n), 1)
    return jnp.sum(jnp.where(same, row, 0.0), axis=1, keepdims=True)


def slot_table(owner_ref, slots):
    number = owner_ref.shape[1]
    owner = owner_ref[...].astype(f32)
    owner_col = column(owner)
    same = owner_col == owner
    i = lax.broadcasted_iota(jnp.int32, same.shape, 0)
    j = lax.broadcasted_iota(jnp.int32, same.shape, 1)
    slot_row = owner * CAP + jnp.sum(jnp.where(same & (i < j), 1.0, 0.0), axis=0, keepdims=True)
    slot_col = owner_col * CAP + jnp.sum(jnp.where(same & (j < i), 1.0, 0.0), axis=1, keepdims=True)
    to_slot = lax.broadcasted_iota(jnp.int32, (slots, number), 0).astype(f32) == slot_row
    of_slot = lax.broadcasted_iota(jnp.int32, (number, slots), 1).astype(f32) == slot_col
    return jnp.where(to_slot, 1.0, 0.0), jnp.where(of_slot, 1.0, 0.0)


def counted(counts_ref, shape):
    return lax.broadcasted_iota(jnp.int32, shape, 1).astype(f32) < column(
        counts_ref[...].astype(f32)
    )


def table(
    span,
    rate_ref,
    coupling_ref,
    contact_ref,
    counts_ref,
    owner_ref,
    corner_ref,
    out_ref,
):
    number, width = rate_ref.shape
    slots = out_ref.shape[0]
    mask = counted(counts_ref, (number, width))
    rate = jnp.where(mask, rate_ref[...], 0.0)
    coupling = jnp.where(mask, coupling_ref[...], 0.0)
    contact = contact_ref[...]
    weights = contact / jnp.sum(contact, axis=1, keepdims=True)
    corner = column(corner_ref[...].astype(f32))
    start_x = jnp.floor((corner + 0.5) * (1.0 / span))
    start_y = corner - start_x * span
    row = jnp.concatenate([weights, jnp.zeros((number, 128 - weights.shape[1]), f32)], axis=1)
    lane = lanes_of(row)
    row = jnp.where(lane == AT_X, start_x, row)
    row = jnp.where(lane == AT_Y, start_y, row)
    sums = (
        (AT_RATE, coupling * rate),
        (AT_COUPLING, coupling),
        (AT_SQUARE, time_step * coupling * coupling),
    )
    row = sums_by_third(row, sums)
    to_slot, _ = slot_table(owner_ref, slots)
    out_ref[...] = jnp.dot(to_slot, row, precision=exact, preferred_element_type=f32)


def first_kernel(layers, v_hbm, b_hbm, m_hbm, *refs):
    outs, near, pack, sems = refs[:6], refs[6:9], refs[9], refs[10]
    for copy in fetch((v_hbm, b_hbm, m_hbm), near, sems):
        copy.wait()
    edges(layers, *near, *outs, pack)


def table_kernel(span, layers, shear_ref, *refs):
    table(span, *refs)
    first = shear_ref[pl.ds(0, layers), 0:1]
    spot = lax.broadcasted_iota(jnp.int32, (layers, 128), 1) - AT_CORNER
    own = spot == lax.broadcasted_iota(jnp.int32, (layers, 128), 0)
    refs[-1][...] += jnp.sum(jnp.where(own, first, 0.0), axis=0, keepdims=True)


def sums_by_third(row, sums):
    lane = lanes_of(row)
    for at, value in sums:
        for e in range(3):
            total = jnp.sum(jnp.where(third(value, e), value, 0.0), axis=1, keepdims=True)
            row = jnp.where(lane == at + e, total, row)
    return row


def fetch_strips(stiff_hbm, begin, stiff_ref, sems):
    size = stiff_ref.shape[0] // sems.shape[0]
    strips = range(sems.shape[0])
    return fetch(
        [stiff_hbm.at[pl.ds(begin + c * size, size)] for c in strips],
        [stiff_ref.at[pl.ds(c * size, size)] for c in strips],
        sems,
    )


def products(stiff_ref, at, drift_ref, out_ref, begin, end):
    group = 16
    for g in range(begin // group * group, end, group):
        rounded = drift_ref[g : g + group, :].astype(jnp.bfloat16)
        row = lax.broadcasted_iota(jnp.int32, rounded.shape, 0)
        low, high = max(g, begin), min(g + group, end)
        total = out_ref[g : g + group, :]
        for b in range(low, high):
            part = lax.dot_general(
                rounded, stiff_ref[b - at], (((1,), (1,)), ((), ())), preferred_element_type=f32
            )
            total = jnp.where(row == b - g, part, total)
        out_ref[g : g + group, :] = total


def pull_kernel(
    stiff_ref,
    stiff_hbm,
    raw_ref,
    rate_ref,
    coupling_ref,
    counts_ref,
    owner_ref,
    base_ref,
    drift_out,
    next_ref,
    pull,
    rest_ref,
    sems,
):
    number, half = drift_out.shape[0], stiff_ref.shape[0]
    copies = fetch_strips(stiff_hbm, half, rest_ref, sems)
    mask = counted(counts_ref, drift_out.shape)
    drift_out[...] = jnp.where(mask, raw_ref[...], 0.0)
    pull[...] = jnp.zeros(pull.shape, f32)
    products(stiff_ref, 0, drift_out, pull, 0, half)
    size = (number - half) // len(copies)
    for c, copy in enumerate(copies):
        copy.wait()
        products(rest_ref, half, drift_out, pull, half + c * size, half + (c + 1) * size)
    rate = jnp.where(mask, rate_ref[...], 0.0)
    coupling = jnp.where(mask, coupling_ref[...], 0.0)
    base = rate - time_step * pull[...] - time_step * coupling * rate
    base = jnp.where(mask, base, 0.0)
    base_ref[...] = base
    row = sums_by_third(jnp.zeros((number, 128), f32), ((AT_NEXT, coupling * base),))
    to_slot, _ = slot_table(owner_ref, next_ref.shape[0])
    next_ref[...] = jnp.dot(to_slot, row, precision=exact, preferred_element_type=f32)


def motion(maps_ref, v_ref, layers):
    size_x, slots, size_y = maps_ref.shape
    total = [jnp.zeros((slots, size_y), f32) for _ in range(3)]
    for x in range(size_x):
        part = maps_ref[x]
        for c in range(3):
            total[c] = total[c] + part * v_ref[c, x * layers : x * layers + 1, :]
    return [jnp.sum(t, axis=1, keepdims=True) for t in total]


def spread(at, reaction, out_ref):
    for x in range(out_ref.shape[1]):
        part = at(x)
        for c in range(3):
            out_ref[c, x : x + 1, :] = jnp.sum(part * reaction[c], axis=0, keepdims=True)


def footprints(table):
    lane = lanes_of(table)
    off_y = lane - table[:, AT_Y : AT_Y + 1].astype(jnp.int32)
    start_x = jnp.broadcast_to(table[:, AT_X : AT_X + 1], table.shape)
    within = (off_y >= 0) & (off_y < FOOT)
    inside = jnp.where(within, off_y, 0)
    lines = []
    for a in range(FOOT):
        picked = jnp.take_along_axis(table, inside + a * FOOT, axis=1)
        lines.append(jnp.where(within, picked, 0.0))

    def at(x):
        value = jnp.zeros(table.shape, f32)
        for a in range(FOOT):
            value = jnp.where(start_x == float(x - a), lines[a], value)
        return value

    return at


def surface_kernel(layers, table_ref, v_ref, maps_ref, moved_ref, push_ref):
    table = table_ref[...]
    lane = lanes_of(table)
    at = footprints(table)
    for x in range(maps_ref.shape[0]):
        maps_ref[x] = at(x)
    moved = motion(maps_ref, v_ref, layers)
    reaction = []
    rows = jnp.zeros(table.shape, f32)
    for c in range(3):
        rest, slope = (table[:, at + c : at + c + 1] for at in (AT_RATE, AT_COUPLING))
        reaction.append(time_step * FOOT * (rest - slope * moved[c]))
        rows = jnp.where(lane == FIRST + c, moved[c], rows)
    moved_ref[...] = rows
    spread(lambda x: maps_ref[x], reaction, push_ref)


def spread_thirds(moved, at, value):
    result = jnp.zeros(value.shape, f32)
    for e in range(3):
        result = jnp.where(third(value, e), moved[:, at + e : at + e + 1], result)
    return result


def motion_again_kernel(layers, v_ref, maps_ref, before_ref, next_ref, out_ref):
    moved = motion(maps_ref, v_ref, layers)
    rows = before_ref[...] + next_ref[...]
    lane = lanes_of(rows)
    for c in range(3):
        rows = jnp.where(lane == SECOND + c, moved[c], rows)
    out_ref[...] = rows


def prepare_kernel(
    sent_ref,
    back_ref,
    table_ref,
    base_ref,
    drift_ref,
    coupling_ref,
    counts_ref,
    owner_ref,
    push_ref,
    drift_out,
    rate_out,
):
    table, sent, back = table_ref[...], sent_ref[...], back_ref[...]
    reaction = []
    for c in range(3):
        rest = back[:, AT_NEXT + c : AT_NEXT + c + 1]
        rest = rest + table[:, AT_SQUARE + c : AT_SQUARE + c + 1] * sent[:, FIRST + c : FIRST + c + 1]
        slope = table[:, AT_COUPLING + c : AT_COUPLING + c + 1]
        reaction.append(time_step * FOOT * (rest - slope * sent[:, SECOND + c : SECOND + c + 1]))
    spread(footprints(table), reaction, push_ref)
    _, of_slot = slot_table(owner_ref, back.shape[0])
    moved = jnp.dot(of_slot, back, precision=exact, preferred_element_type=f32)
    coupling = coupling_ref[...]
    mask = counted(counts_ref, coupling.shape)
    rate = base_ref[...] + time_step * coupling * spread_thirds(moved, FIRST, coupling)
    rate = jnp.where(mask, rate, 0.0)
    drift_out[...] = jnp.where(mask, drift_ref[...] + time_step * rate, 0.0)
    rate_out[...] = rate - time_step * coupling * (rate - spread_thirds(moved, SECOND, coupling))


def finish_kernel(
    layers,
    v_ref,
    s_ref,
    buoy_ref,
    x_even,
    x_odd,
    y_even,
    y_odd,
    push_ref,
    half,
    rate_ref,
    counts_ref,
    stiff_hbm,
    out_hbm,
    drift_out,
    rate_out,
    out_ref,
    ext,
    cols,
    slope,
    pull,
    stiff_ref,
    sems,
    out_sems,
):
    fetch_strips(stiff_hbm, 0, stiff_ref, sems)
    size_x = v_ref.shape[1] // layers
    halo = (x_even, x_odd, y_even, y_odd)
    fresh = moving(layers, v_ref, s_ref, buoy_ref, halo, push_ref, ext, cols, slope)
    strips = sems.shape[0]
    share = half.shape[0] // strips
    batch = size_x // strips

    def advance(strip):
        for i in range(batch):
            x = strip * batch + i
            v = fresh(x, pl.ds(pl.multiple_of(x * layers, layers), layers))
            for c in range(3):
                out_ref[x // TILE, c, :, lax.rem(x, TILE), :] = v[c]

    def multiply(strip):
        cut = pl.ds(pl.multiple_of(strip * share, share), share)
        pltpu.make_async_copy(stiff_hbm.at[cut], stiff_ref.at[cut], sems.at[strip]).wait()
        rounded = half[cut, :].astype(jnp.bfloat16)
        row = lax.broadcasted_iota(jnp.int32, rounded.shape, 0)
        total = jnp.zeros(rounded.shape, f32)
        for b in range(share):
            part = lax.dot_general(
                rounded,
                stiff_ref[strip * share + b],
                (((1,), (1,)), ((), ())),
                preferred_element_type=f32,
            )
            total = jnp.where(row == b, part, total)
        pull[cut, :] = total

    def leave(tile):
        return pltpu.make_async_copy(out_ref.at[tile], out_hbm.at[:, :, tile], out_sems.at[tile])

    def step(strip, carry):
        multiply(strip - 1)
        advance(strip)
        return carry

    tiles = size_x // TILE
    for tile in range(tiles):
        begin, end = tile * strips // tiles, (tile + 1) * strips // tiles
        if tile == 0:
            advance(0)
            begin = 1
        lax.fori_loop(begin, end, step, 0)
        leave(tile).start()
    multiply(strips - 1)
    mask = counted(counts_ref, half.shape)
    rate = jnp.where(mask, rate_ref[...] - time_step * pull[...], 0.0)
    rate_out[...] = rate
    drift_out[...] = jnp.where(mask, half[...] + time_step * rate, 0.0)
    for tile in range(tiles):
        leave(tile).wait()


def trade(rows):
    devices = lax.axis_size("gx") * lax.axis_size("gy")
    blocks = rows.reshape(devices, CAP, rows.shape[1])
    blocks = lax.all_to_all(blocks, ("gx", "gy"), split_axis=0, concat_axis=0, tiled=True)
    return blocks.reshape(rows.shape)


def body(
    soil_velocity,
    soil_stress,
    buoyancy,
    lame_first,
    shear_modulus,
    stiffness,
    storey_drift,
    drift_rate,
    coupling,
    contact,
    dof_counts,
    owner_tile,
    corner_cell,
):
    layers, size_x, size_y = buoyancy.shape
    cells = layers * size_x
    number, width = storey_drift.shape
    slots = lax.axis_size("gx") * lax.axis_size("gy") * CAP
    span = size_y - FOOT + 1
    counts, owner, corner = (a.reshape(1, number) for a in (dof_counts, owner_tile, corner_cell))

    def bind(kernel, *fixed):
        def bound(*refs):
            kernel(*fixed, *refs)

        return bound

    def vm(*dims):
        return pltpu.VMEM(dims, f32)

    field = vm(cells, size_y)
    tall = layers + 2 * PAD
    plane = near_by(number, width)
    dma = pltpu.SemaphoreType.DMA
    flat = [a.reshape(cells, size_y) for a in (buoyancy, shear_modulus, lame_first)]
    far = (soil_velocity.reshape(3, cells, size_y), *flat[:2])
    vt, bt, mt, one, two, col = call(
        bind(first_kernel, layers),
        "first",
        (
            near_by(3, cells, size_y),
            near_by(cells, size_y),
            near_by(cells, size_y),
            near_by(7, layers, size_y),
            near_by(7, layers, size_y),
            near_by(16, cells),
        ),
        [Far(a) for a in far],
        [pltpu.VMEM(a.shape, a.dtype) for a in far] + [field, dma((len(far),))],
    )
    (rows,) = call(
        bind(table_kernel, span, layers),
        "table",
        (near_by(slots, 128),),
        (mt, drift_rate, coupling, contact, counts, owner, corner),
    )

    def exchange(one, two, col):
        return swap(one, "gx", 0), swap(two, "gx", 1), swap(col, "gy", 0), swap(col, "gy", 1)

    halo = exchange(one, two, col)
    rows = trade(rows)
    st, lt = call(
        bind(load_kernel, layers),
        "load",
        (near_by(6, cells, size_y), near_by(cells, size_y)),
        (rows, Far(soil_stress.reshape(6, cells, size_y)), Far(flat[2])),
        [vm(6, cells, size_y), field, dma((7,))],
    )
    half = number // 2
    payload = (near_by(5, layers, size_y), near_by(5, layers, size_y), near_by(16, cells))
    ext = vm(3, size_x + 4, tall, size_y)
    stack = vm(size_x + 1, tall, size_y)
    st, one, two, col, means, buoys, stiff = call(
        bind(begin_kernel, layers),
        "begin",
        (
            near_by(6, cells, size_y),
            *payload,
            near_by(5, cells, size_y),
            near_by(3, cells, size_y),
            near_by(half, width, width, dtype=stiffness.dtype),
        ),
        (vt, bt, mt, st, lt, Far(stiffness), *halo, rows),
        [
            stack,
            stack,
            stack,
            stack,
            ext,
            field,
            field,
            vm(3, cells, size_y),
            dma((1,)),
        ],
    )

    halo = exchange(one, two, col)
    maps, moved, push = call(
        bind(surface_kernel, layers),
        "surface",
        (near_by(size_x, slots, size_y), near_by(slots, 128), near_by(3, size_x, size_y)),
        (rows, vt),
    )
    chunks = 4 if number % 8 == 0 else 1
    base, drift, following = call(
        pull_kernel,
        "pull",
        (plane, plane, near_by(slots, 128)),
        (stiff, Far(stiffness), storey_drift, drift_rate, coupling, counts, owner),
        [
            vm(number, width),
            pltpu.VMEM((number - half, width, width), stiffness.dtype),
            dma((chunks,)),
        ],
    )
    push, following = lax.optimization_barrier((push, following))
    bulk = vm(5, size_x + 4, tall, size_y)
    vt, one, two, col = call(
        bind(velocity_kernel, layers),
        "velocity",
        (near_by(3, cells, size_y), *payload),
        (vt, st, buoys, *halo, push),
        [bulk, field, field, vm(3, cells, size_y)],
    )
    halo = exchange(one, two, col)
    (sent,) = call(
        bind(motion_again_kernel, layers),
        "motion_again",
        (near_by(slots, 128),),
        (vt, maps, moved, following),
    )
    vt, sent = lax.optimization_barrier((vt, sent))
    back = trade(sent)
    strips = size_x // STRIP
    st, one, two, col = call(
        bind(stress_kernel, layers),
        "stress",
        (near_by(6, cells, size_y), *payload),
        (vt, Far(st), Far(means), *halo),
        [
            vm(6, cells, size_y),
            vm(5, cells, size_y),
            ext,
            field,
            field,
            vm(3, cells, size_y),
            dma((2 * strips,)),
        ],
    )
    halo = exchange(one, two, col)
    sent, st = lax.optimization_barrier((sent, st))
    push, drift, rate = call(
        prepare_kernel,
        "prepare",
        (near_by(3, size_x, size_y), plane, plane),
        (sent, back, rows, base, drift, coupling, counts, owner),
    )
    tiles = size_x // TILE
    v, drift, rate = call(
        bind(finish_kernel, layers),
        "finish",
        (
            pltpu.HBM((3, layers, tiles, TILE, size_y), f32),
            shape(number, width),
            shape(number, width),
        ),
        (
            vt,
            st,
            buoys,
            *halo,
            push,
            drift,
            rate,
            counts,
            Far(stiffness),
        ),
        [
            vm(tiles, 3, layers, TILE, size_y),
            bulk,
            field,
            vm(3, cells, size_y),
            vm(number, width),
            pltpu.VMEM(stiffness.shape, stiffness.dtype),
            dma((chunks,)),
            dma((tiles,)),
        ],
        far_outs=(0,),
    )
    return v.reshape(soil_velocity.shape), drift, rate


def solution(mesh):
    both = ("gx", "gy")
    soil = P(None, None, "gx", "gy")
    cell = P(None, "gx", "gy")
    placed = (
        soil,
        soil,
        cell,
        cell,
        cell,
        P(both, None, None),
        P(both, None),
        P(both, None),
        P(both, None),
        P(both, None),
        P(both),
        P(both, None),
        P(both),
    )
    return jax.shard_map(
        body,
        mesh=mesh,
        in_specs=placed,
        out_specs=(soil, P(both, None), P(both, None)),
        check_vma=False,
    )
```

```python
import jax
import jax.numpy as jnp
from jax import lax
from jax.experimental import pallas as pl
from jax.experimental.pallas import tpu as pltpu
from jax.sharding import PartitionSpec as P

FOOT = 8
CAP = 2
PAD = 8
STRIP = 4
TILE = 8

near = 9.0 / 8.0
far = 1.0 / 24.0
time_step = 0.3
exact = lax.Precision.HIGHEST
f32 = jnp.float32

AT_X, AT_Y, AT_RATE, AT_COUPLING, AT_SQUARE, AT_CORNER = 64, 65, 66, 69, 72, 75
FIRST, SECOND, AT_NEXT = 0, 3, 8


COSTS = {
    "first": 30_000_000,
    "load": 20_000_000,
    "begin": 40_000_000,
    "stress": 25_000_000,
    "surface": 10_000_000,
    "pull": 30_000_000,
    "velocity": 25_000_000,
    "motion_again": 10_000_000,
    "prepare": 60_000_000,
    "finish": 60_000_000,
}


class Far:
    def __init__(self, value):
        self.value = value


def call(kernel, name, outs, args, scratch=(), far_outs=()):
    cost = COSTS[name]
    specs, values = [], []
    for a in args:
        far = isinstance(a, Far)
        a = a.value if far else a
        values.append(pltpu.with_memory_space_constraint(a, pltpu.HBM if far else pltpu.VMEM))
        specs.append(pl.BlockSpec(memory_space=pl.ANY if far else pltpu.VMEM))
    return pl.pallas_call(
        kernel,
        name=name,
        out_shape=outs,
        in_specs=specs,
        out_specs=tuple(
            pl.BlockSpec(memory_space=pl.ANY if i in far_outs else pltpu.VMEM)
            for i in range(len(outs))
        ),
        scratch_shapes=list(scratch),
        cost_estimate=pl.CostEstimate(flops=1000*cost, bytes_accessed=cost, transcendentals=0),
        compiler_params=pltpu.CompilerParams(vmem_limit_bytes=16 * 2**20),
    )(*values)


def shape(*dims):
    return jax.ShapeDtypeStruct(dims, f32)


def near_by(*dims, dtype=f32):
    return pltpu.VMEM(dims, dtype)


def fetch(sources, targets, sems):
    copies = [
        pltpu.make_async_copy(source, target, sems.at[i])
        for i, (source, target) in enumerate(zip(sources, targets))
    ]
    for copy in copies:
        copy.start()
    return copies


def swap(block, axis, odd):
    size = lax.axis_size(axis)
    pairs = [(i % size, (i + 1) % size) for i in range(odd, size + odd, 2)]
    return lax.ppermute(block, axis, pairs + [(b, a) for a, b in pairs])


def even(axis):
    return lax.rem(lax.axis_index(axis), 2) == 0


def two_ways(up, down, even_ref, odd_ref):
    lead = even("gx")
    blank = jnp.zeros(even_ref.shape[1:], f32)
    for row in range(even_ref.shape[0]):
        a = up[row] if row < len(up) else blank
        b = down[row] if row < len(down) else blank
        even_ref[row] = jnp.where(lead, a, b)
        odd_ref[row] = jnp.where(lead, b, a)


def below_above(axis, even_ref, odd_ref):
    lead = even(axis)

    def below(index):
        return jnp.where(lead, odd_ref[index], even_ref[index])

    def above(index):
        return jnp.where(lead, even_ref[index], odd_ref[index])

    return below, above


def lanes_of(value):
    return lax.broadcasted_iota(jnp.int32, value.shape, len(value.shape) - 1)


def roll(value, amount):
    return pltpu.roll(value, amount % value.shape[-1], len(value.shape) - 1)


def packed(pieces):
    result = None
    for slab, first, count, amount in pieces:
        moved = roll(slab, amount) if amount else slab
        if result is None:
            result = moved
        else:
            lane = lanes_of(slab)
            result = jnp.where((lane >= first) & (lane < first + count), moved, result)
    return result


def send_columns(pack_ref, out_ref):
    rows, width = out_ref.shape
    for block in range(width // 128):
        part = pack_ref[block * 128 : (block + 1) * 128, :]
        out_ref[:, block * 128 : (block + 1) * 128] = part.T[:rows]


def receive_columns(even_ref, odd_ref, from_south, south_ok, north_ok, out_ref):
    rows, width = even_ref.shape
    below, above = below_above("gy", even_ref, odd_ref)
    for block in range(width // 128):
        cut = slice(block * 128, (block + 1) * 128)
        south = jnp.where(south_ok, below((slice(None), cut)), 0.0)
        north = jnp.where(north_ok, above((slice(None), cut)), 0.0)
        row = lax.broadcasted_iota(jnp.int32, south.shape, 0)
        taken = row == from_south[0]
        for other in from_south[1:]:
            taken = taken | (row == other)
        part = jnp.where(taken, south, north)
        whole = jnp.concatenate([part, jnp.zeros((128 - rows, 128), f32)], axis=0)
        out_ref[cut, :] = whole.T


def bands(forward, amount):
    row = lax.broadcasted_iota(jnp.int32, (256, 128), 0)
    lane = row - 128
    beyond = jnp.where(lane < amount, lane - amount, 128 + lane - amount)
    shift = jnp.where(row < 128, row, beyond) - lax.broadcasted_iota(jnp.int32, (256, 128), 1)
    first, last = (amount - 1, amount + 1) if forward else (amount - 2, amount)
    valid = (row < 128) | ((lane >= first) & (lane <= last))
    value = jnp.zeros((256, 128), f32)
    at = 0 if forward else -1
    for step, entry in ((at + 1, 27.0), (at, -27.0), (at + 2, -1.0), (at - 1, 1.0)):
        value = jnp.where(shift == step, entry, value)
    return jnp.where(valid, value, 0.0).astype(jnp.bfloat16)


def parted(value):
    large = value.astype(jnp.bfloat16)
    return large, (value - large.astype(f32)).astype(jnp.bfloat16)


def slopes(fields, cols, out_ref):
    matrices = [bands(forward, amount) for _, forward, amount in fields]
    size = 256
    for begin in range(0, cols.shape[0], size):
        cut = slice(begin, begin + size)
        ghost = parted(cols[cut, :])
        for i, (read, _, _) in enumerate(fields):
            total = None
            for own, other in zip(parted(read(cut)), ghost):
                both = jnp.concatenate([own, other], axis=1)
                part = jnp.dot(both, matrices[i], preferred_element_type=f32)
                total = part if total is None else total + part
            out_ref[i, cut, :] = total * (1.0 / 24.0)


def across(ext, c, x, forward, layers):
    def at(d):
        return ext[c, x + 2 + d, PAD : PAD + layers, :]

    if forward:
        return near * (at(1) - at(0)) - far * (at(2) - at(-1))
    return near * (at(0) - at(-1)) - far * (at(1) - at(-2))


def down(ext, c, x, forward, layers):
    def at(d):
        return ext[c, x + 2, PAD + d : PAD + layers + d, :]

    if forward:
        return near * (at(1) - at(0)) - far * (at(2) - at(-1))
    return near * (at(0) - at(-1)) - far * (at(1) - at(-2))


def place():
    gx, gy = lax.axis_index("gx"), lax.axis_index("gy")
    nx, ny = lax.axis_size("gx"), lax.axis_size("gy")
    return gx > 0, gx < nx - 1, gy > 0, gy < ny - 1


def fill(ext, c, source, src, size_x, layers):
    for x in range(size_x):
        ext[c, x + 2, 0:PAD, :] = jnp.zeros((PAD, 128), f32)
        ext[c, x + 2, PAD : PAD + layers, :] = source[src, x * layers : (x + 1) * layers, :]
        ext[c, x + 2, PAD + layers : PAD + layers + PAD, :] = jnp.zeros((PAD, 128), f32)


def edges(layers, v_ref, b_ref, m_ref, vt_ref, bt_ref, mt_ref, even_ref, odd_ref, col_ref, pack):
    size_x = vt_ref.shape[1] // layers

    def slab(ref, x):
        return ref[x * layers : (x + 1) * layers, :]

    for x in range(size_x):
        cut = pl.ds(x * layers, layers)
        turned = pl.ds(x, layers, stride=size_x)
        v = [v_ref[c, turned, :] for c in range(3)]
        buoy, shear = b_ref[turned, :], m_ref[turned, :]
        for c in range(3):
            vt_ref[c, cut, :] = v[c]
        bt_ref[cut, :] = buoy
        mt_ref[cut, :] = shear
        pack[cut, :] = packed(
            [(v[0], 0, 3, 1), (v[1], 3, 3, 5), (v[2], 6, 3, 7), (buoy, 9, 1, 9), (shear, 10, 1, 10)]
        )
    last = size_x - 1
    up = [slab(vt_ref.at[c], x) for c, x in ((0, last - 1), (0, last), (1, last), (2, last))]
    down = [slab(vt_ref.at[c], x) for c, x in ((0, 0), (1, 0), (1, 1), (2, 0), (2, 1))]
    two_ways(up, down + [slab(bt_ref, 0), slab(mt_ref, 0)], even_ref, odd_ref)
    send_columns(pack, col_ref)


def load_kernel(layers, after_ref, s_hbm, l_hbm, st_ref, lt_ref, s_ref, l_ref, sems):
    del after_ref
    size_x = l_ref.shape[0] // layers
    copies = fetch(
        [l_hbm] + [s_hbm.at[c] for c in range(6)], [l_ref] + [s_ref.at[c] for c in range(6)], sems
    )
    for c, copy in enumerate(copies):
        copy.wait()
        for x in range(size_x):
            cut, turned = pl.ds(x * layers, layers), pl.ds(x, layers, stride=size_x)
            if c == 0:
                lt_ref[cut, :] = l_ref[turned, :]
            else:
                st_ref[c - 1, cut, :] = s_ref[c - 1, turned, :]


def materials(layers, b_ref, l_ref, m_ref, above, cols, table_ref, mat_ref, buoy_ref, bs, ms, tb, tm):
    size_x = b_ref.shape[0] // layers
    _, east_ok, _, north_ok = place()
    nx, ny = lax.axis_size("gx"), lax.axis_size("gy")
    beyond = lax.rem(lax.axis_index("gx") + 1, nx) * ny + lax.rem(lax.axis_index("gy") + 1, ny)
    inner = slice(PAD, PAD + layers)
    for x in range(size_x):
        cut = slice(x * layers, (x + 1) * layers)
        bs[x, inner, :] = b_ref[cut, :]
        ms[x, inner, :] = m_ref[cut, :]
        part = cols[cut, :]
        tb[x, inner, :] = roll(part, -9)
        tm[x, inner, :] = roll(part, -10)
    bs[size_x, inner, :] = above(5)
    ms[size_x, inner, :] = above(6)
    line = jnp.broadcast_to(table_ref[pl.ds(beyond * CAP, 1), :], (layers, 128))
    own = lanes_of(line) - AT_CORNER == lax.broadcasted_iota(jnp.int32, line.shape, 0)
    corner = jnp.sum(jnp.where(own, line, 0.0), axis=1, keepdims=True)
    tm[size_x, inner, :] = jnp.broadcast_to(corner, line.shape)
    zero = jnp.zeros((PAD, 128), f32)
    for x in range(size_x + 1):
        bs[x, PAD + layers : PAD + layers + PAD, :] = zero
        ms[x, PAD + layers : PAD + layers + PAD, :] = zero
        tm[x, PAD + layers : PAD + layers + PAD, :] = zero
    below = slice(PAD + 1, PAD + layers + 1)

    def step(x, carry):
        cut = pl.ds(pl.multiple_of(x * layers, layers), layers)
        b, m = bs[x, inner, :], ms[x, inner, :]
        lane = lanes_of(b)
        layer = lax.broadcasted_iota(jnp.int32, b.shape, 0)
        in_x = (x < size_x - 1) | east_ok
        in_y = (lane < 127) | north_ok
        in_z = layer < layers - 1

        def north(value, ghost):
            return roll(jnp.where(lane == 0, ghost, value), -1)

        b_e = jnp.where(in_x, bs[x + 1, inner, :], b)
        b_n = jnp.where(in_y, north(b, tb[x, inner, :]), b)
        b_z = jnp.where(in_z, bs[x, below, :], b)
        m_e = jnp.where(in_x, ms[x + 1, inner, :], m)
        m_n = jnp.where(in_y, north(m, tm[x, inner, :]), m)
        m_z = jnp.where(in_z, ms[x, below, :], m)
        m_en = jnp.where(in_y & in_x, north(ms[x + 1, inner, :], tm[x + 1, inner, :]), m)
        m_ez = jnp.where(in_z & in_x, ms[x + 1, below, :], m)
        m_nz = jnp.where(in_z & in_y, north(ms[x, below, :], tm[x, below, :]), m)
        mat_ref[0, cut, :] = time_step * l_ref[cut, :]
        mat_ref[1, cut, :] = (2.0 * time_step) * m
        mat_ref[2, cut, :] = (0.25 * time_step) * (m + m_e + m_n + m_en)
        mat_ref[3, cut, :] = (0.25 * time_step) * (m + m_e + m_z + m_ez)
        mat_ref[4, cut, :] = (0.25 * time_step) * (m + m_n + m_z + m_nz)
        buoy_ref[0, cut, :] = (0.5 * time_step) * (b + b_e)
        buoy_ref[1, cut, :] = (0.5 * time_step) * (b + b_n)
        buoy_ref[2, cut, :] = (0.5 * time_step) * (b + b_z)
        return carry

    lax.fori_loop(0, size_x, step, 0, unroll=4)


def extend(ext, rows, at, ok, layers):
    for row, c, x in rows:
        ext[c, x, PAD : PAD + layers, :] = jnp.where(ok, at(row), 0.0)


def stresses(layers, v_ref, old, ready, mat_ref, below, above, cols, out_ref, refs, ext, pack, slope):
    even_ref, odd_ref, col_ref = refs
    size_x = v_ref.shape[1] // layers
    west_ok, east_ok, _, _ = place()
    for c in range(3):
        fill(ext, c, v_ref, c, size_x, layers)
    extend(ext, ((0, 0, 0), (1, 0, 1), (2, 1, 1), (3, 2, 1)), below, west_ok, layers)
    over = size_x + 2
    rows = ((0, 0, over), (1, 1, over), (2, 1, over + 1), (3, 2, over), (4, 2, over + 1))
    extend(ext, rows, above, east_ok, layers)

    fields = (
        (lambda cut: v_ref[1, cut, :], False, 5),
        (lambda cut: v_ref[0, cut, :], True, 1),
        (lambda cut: v_ref[2, cut, :], True, 7),
    )
    slopes(fields, cols, slope)

    def step(x, carry):
        cut = pl.ds(pl.multiple_of(x * layers, layers), layers)
        dx = across(ext, 0, x, False, layers)
        dy = slope[0, cut, :]
        dz = down(ext, 2, x, False, layers)
        both = mat_ref[0, cut, :] * (dx + dy + dz)
        twice = mat_ref[1, cut, :]
        xx = old(0, x, cut) + (both + twice * dx)
        yy = old(1, x, cut) + (both + twice * dy)
        zz = old(2, x, cut) + (both + twice * dz)
        xy = old(3, x, cut) + mat_ref[2, cut, :] * (
            slope[1, cut, :] + across(ext, 1, x, True, layers)
        )
        xz = old(4, x, cut) + mat_ref[3, cut, :] * (
            down(ext, 0, x, True, layers) + across(ext, 2, x, True, layers)
        )
        yz = old(5, x, cut) + mat_ref[4, cut, :] * (
            down(ext, 1, x, True, layers) + slope[2, cut, :]
        )
        for c, value in enumerate((xx, yy, zz, xy, xz, yz)):
            out_ref[c, cut, :] = value
        pack[cut, :] = packed([(yy, 0, 3, 1), (xy, 3, 3, 5), (yz, 6, 3, 8)])
        return carry

    for strip in range(size_x // STRIP):
        ready(strip)
        lax.fori_loop(strip * STRIP, (strip + 1) * STRIP, step, 0, unroll=4)
    send_columns(pack, col_ref)

    def slab(c, x):
        return out_ref[c, x * layers : (x + 1) * layers, :]

    up = [slab(c, size_x - x) for c, x in ((0, 1), (3, 2), (3, 1), (4, 2), (4, 1))]
    two_ways(up, [slab(c, x) for c, x in ((0, 0), (0, 1), (3, 0), (4, 0))], even_ref, odd_ref)


def begin_kernel(
    layers,
    v_ref,
    b_ref,
    m_ref,
    s_ref,
    l_ref,
    stiff_hbm,
    x_even,
    x_odd,
    y_even,
    y_odd,
    table_ref,
    out_ref,
    even_ref,
    odd_ref,
    col_ref,
    mat_ref,
    buoy_ref,
    stiff_ref,
    bs,
    ms,
    tb,
    tm,
    ext,
    cols,
    pack,
    slope,
    sems,
):
    half = stiff_ref.shape[0]
    half = stiff_ref.shape[0]
    copies = fetch([stiff_hbm.at[pl.ds(0, half)]], [stiff_ref], sems)
    _, _, south_ok, north_ok = place()
    below, above = below_above("gx", x_even, x_odd)
    receive_columns(y_even, y_odd, (0, 3, 4, 6), south_ok, north_ok, cols)
    materials(layers, b_ref, l_ref, m_ref, above, cols, table_ref, mat_ref, buoy_ref, bs, ms, tb, tm)

    def ready(strip):
        pass

    def old(c, x, cut):
        return s_ref[c, cut, :]

    refs = (even_ref, odd_ref, col_ref)
    stresses(layers, v_ref, old, ready, mat_ref, below, above, cols, out_ref, refs, ext, pack, slope)
    copies[0].wait()


def stress_kernel(
    layers,
    v_ref,
    s_hbm,
    mat_hbm,
    x_even,
    x_odd,
    y_even,
    y_odd,
    out_ref,
    even_ref,
    odd_ref,
    col_ref,
    s_ref,
    mat_ref,
    ext,
    cols,
    pack,
    slope,
    sems,
):
    strips = v_ref.shape[1] // layers // STRIP
    cuts = [pl.ds(strip * STRIP * layers, STRIP * layers) for strip in range(strips)]
    sources, targets = [], []
    for cut in cuts:
        sources += [s_hbm.at[:, cut], mat_hbm.at[:, cut]]
        targets += [s_ref.at[:, cut], mat_ref.at[:, cut]]
    copies = fetch(sources, targets, sems)
    _, _, south_ok, north_ok = place()
    below, above = below_above("gx", x_even, x_odd)
    receive_columns(y_even, y_odd, (0, 3, 4, 6), south_ok, north_ok, cols)

    def ready(strip):
        copies[2 * strip].wait()
        copies[2 * strip + 1].wait()

    def old(c, x, cut):
        return s_ref[c, cut, :]

    refs = (even_ref, odd_ref, col_ref)
    stresses(layers, v_ref, old, ready, mat_ref, below, above, cols, out_ref, refs, ext, pack, slope)


def moving(layers, v_ref, s_ref, buoy_ref, halo, push_ref, ext, cols, slope):
    x_even, x_odd, y_even, y_odd = halo
    size_x = v_ref.shape[1] // layers
    west_ok, east_ok, south_ok, north_ok = place()
    below, above = below_above("gx", x_even, x_odd)
    receive_columns(y_even, y_odd, (0, 3, 4, 6, 7), south_ok, north_ok, cols)
    for c, src in enumerate((0, 3, 4, 5, 2)):
        fill(ext, c, s_ref, src, size_x, layers)
    rows = ((0, 0, 1), (1, 1, 0), (2, 1, 1), (3, 2, 0), (4, 2, 1))
    extend(ext, rows, below, west_ok, layers)
    over = size_x + 2
    extend(ext, ((0, 0, over), (1, 0, over + 1), (2, 1, over), (3, 2, over)), above, east_ok, layers)

    fields = (
        (lambda cut: s_ref[3, cut, :], False, 5),
        (lambda cut: s_ref[1, cut, :], True, 1),
        (lambda cut: s_ref[5, cut, :], False, 8),
    )
    slopes(fields, cols, slope)

    def fresh(x, cut):
        ax = across(ext, 0, x, True, layers) + slope[0, cut, :] + down(ext, 2, x, False, layers)
        ay = across(ext, 1, x, False, layers) + slope[1, cut, :] + down(ext, 3, x, False, layers)
        az = across(ext, 2, x, False, layers) + slope[2, cut, :] + down(ext, 4, x, True, layers)
        layer = lax.broadcasted_iota(jnp.int32, ax.shape, 0)
        result = []
        for c, accel in enumerate((ax, ay, az)):
            pushed = jnp.where(layer == 0, push_ref[c, pl.ds(x, 1), :], 0.0)
            result.append(v_ref[c, cut, :] + buoy_ref[c, cut, :] * accel + pushed)
        return result

    return fresh


def velocity_kernel(
    layers,
    v_ref,
    s_ref,
    buoy_ref,
    x_even,
    x_odd,
    y_even,
    y_odd,
    push_ref,
    out_ref,
    even_ref,
    odd_ref,
    col_ref,
    ext,
    cols,
    pack,
    slope,
):
    size_x = v_ref.shape[1] // layers
    halo = (x_even, x_odd, y_even, y_odd)
    fresh = moving(layers, v_ref, s_ref, buoy_ref, halo, push_ref, ext, cols, slope)

    def step(x, carry):
        cut = pl.ds(pl.multiple_of(x * layers, layers), layers)
        v = fresh(x, cut)
        for c in range(3):
            out_ref[c, cut, :] = v[c]
        pack[cut, :] = packed([(v[0], 0, 3, 1), (v[1], 3, 3, 5), (v[2], 6, 3, 7)])
        return carry

    lax.fori_loop(0, size_x, step, 0, unroll=8)
    send_columns(pack, col_ref)

    def slab(c, x):
        return out_ref[c, x * layers : (x + 1) * layers, :]

    up = [slab(c, size_x - x) for c, x in ((0, 2), (0, 1), (1, 1), (2, 1))]
    down_rows = [slab(c, x) for c, x in ((0, 0), (1, 0), (1, 1), (2, 0), (2, 1))]
    two_ways(up, down_rows, even_ref, odd_ref)


def third(value, e):
    d = lanes_of(value).astype(f32)
    return d - 3.0 * jnp.floor((d + 0.5) * (1.0 / 3.0)) == e


def column(row):
    n = row.shape[1]
    same = lax.broadcasted_iota(jnp.int32, (n, n), 0) == lax.broadcasted_iota(jnp.int32, (n, n), 1)
    return jnp.sum(jnp.where(same, row, 0.0), axis=1, keepdims=True)


def slot_table(owner_ref, slots):
    number = owner_ref.shape[1]
    owner = owner_ref[...].astype(f32)
    owner_col = column(owner)
    same = owner_col == owner
    i = lax.broadcasted_iota(jnp.int32, same.shape, 0)
    j = lax.broadcasted_iota(jnp.int32, same.shape, 1)
    slot_row = owner * CAP + jnp.sum(jnp.where(same & (i < j), 1.0, 0.0), axis=0, keepdims=True)
    slot_col = owner_col * CAP + jnp.sum(jnp.where(same & (j < i), 1.0, 0.0), axis=1, keepdims=True)
    to_slot = lax.broadcasted_iota(jnp.int32, (slots, number), 0).astype(f32) == slot_row
    of_slot = lax.broadcasted_iota(jnp.int32, (number, slots), 1).astype(f32) == slot_col
    return jnp.where(to_slot, 1.0, 0.0), jnp.where(of_slot, 1.0, 0.0)


def counted(counts_ref, shape):
    return lax.broadcasted_iota(jnp.int32, shape, 1).astype(f32) < column(
        counts_ref[...].astype(f32)
    )


def table(
    span,
    rate_ref,
    coupling_ref,
    contact_ref,
    counts_ref,
    owner_ref,
    corner_ref,
    out_ref,
):
    number, width = rate_ref.shape
    slots = out_ref.shape[0]
    mask = counted(counts_ref, (number, width))
    rate = jnp.where(mask, rate_ref[...], 0.0)
    coupling = jnp.where(mask, coupling_ref[...], 0.0)
    contact = contact_ref[...]
    weights = contact / jnp.sum(contact, axis=1, keepdims=True)
    corner = column(corner_ref[...].astype(f32))
    start_x = jnp.floor((corner + 0.5) * (1.0 / span))
    start_y = corner - start_x * span
    row = jnp.concatenate([weights, jnp.zeros((number, 128 - weights.shape[1]), f32)], axis=1)
    lane = lanes_of(row)
    row = jnp.where(lane == AT_X, start_x, row)
    row = jnp.where(lane == AT_Y, start_y, row)
    sums = (
        (AT_RATE, coupling * rate),
        (AT_COUPLING, coupling),
        (AT_SQUARE, time_step * coupling * coupling),
    )
    row = sums_by_third(row, sums)
    to_slot, _ = slot_table(owner_ref, slots)
    out_ref[...] = jnp.dot(to_slot, row, precision=exact, preferred_element_type=f32)


def first_kernel(layers, span, *refs):
    far, outs, near, pack, sems = refs[:9], refs[9:16], refs[16:25], refs[25], refs[26]
    rows_ref, shear_ref = outs[6], outs[2]
    order = list(range(3, 9)) + list(range(3))
    copies = fetch([far[i] for i in order], [near[i] for i in order], sems)
    for copy in copies[:6]:
        copy.wait()
    table(span, *near[3:], rows_ref)
    for copy in copies[6:]:
        copy.wait()
    edges(layers, *near[:3], *outs[:6], pack)
    first = shear_ref[pl.ds(0, layers), 0:1]
    spot = lax.broadcasted_iota(jnp.int32, (layers, 128), 1) - AT_CORNER
    own = spot == lax.broadcasted_iota(jnp.int32, (layers, 128), 0)
    rows_ref[...] += jnp.sum(jnp.where(own, first, 0.0), axis=0, keepdims=True)


def sums_by_third(row, sums):
    lane = lanes_of(row)
    for at, value in sums:
        for e in range(3):
            total = jnp.sum(jnp.where(third(value, e), value, 0.0), axis=1, keepdims=True)
            row = jnp.where(lane == at + e, total, row)
    return row


def fetch_strips(stiff_hbm, begin, stiff_ref, sems):
    size = stiff_ref.shape[0] // sems.shape[0]
    strips = range(sems.shape[0])
    return fetch(
        [stiff_hbm.at[pl.ds(begin + c * size, size)] for c in strips],
        [stiff_ref.at[pl.ds(c * size, size)] for c in strips],
        sems,
    )


def products(stiff_ref, at, drift_ref, out_ref, begin, end):
    group = 16
    for g in range(begin // group * group, end, group):
        rounded = drift_ref[g : g + group, :].astype(jnp.bfloat16)
        row = lax.broadcasted_iota(jnp.int32, rounded.shape, 0)
        low, high = max(g, begin), min(g + group, end)
        total = out_ref[g : g + group, :]
        for b in range(low, high):
            part = lax.dot_general(
                rounded, stiff_ref[b - at], (((1,), (1,)), ((), ())), preferred_element_type=f32
            )
            total = jnp.where(row == b - g, part, total)
        out_ref[g : g + group, :] = total


def pull_kernel(
    stiff_ref,
    stiff_hbm,
    raw_ref,
    rate_ref,
    coupling_ref,
    counts_ref,
    owner_ref,
    base_ref,
    drift_out,
    next_ref,
    pull,
    rest_ref,
    sems,
):
    number, half = drift_out.shape[0], stiff_ref.shape[0]
    copies = fetch_strips(stiff_hbm, half, rest_ref, sems)
    mask = counted(counts_ref, drift_out.shape)
    drift_out[...] = jnp.where(mask, raw_ref[...], 0.0)
    pull[...] = jnp.zeros(pull.shape, f32)
    products(stiff_ref, 0, drift_out, pull, 0, half)
    size = (number - half) // len(copies)
    for c, copy in enumerate(copies):
        copy.wait()
        products(rest_ref, half, drift_out, pull, half + c * size, half + (c + 1) * size)
    rate = jnp.where(mask, rate_ref[...], 0.0)
    coupling = jnp.where(mask, coupling_ref[...], 0.0)
    base = rate - time_step * pull[...] - time_step * coupling * rate
    base = jnp.where(mask, base, 0.0)
    base_ref[...] = base
    row = sums_by_third(jnp.zeros((number, 128), f32), ((AT_NEXT, coupling * base),))
    to_slot, _ = slot_table(owner_ref, next_ref.shape[0])
    next_ref[...] = jnp.dot(to_slot, row, precision=exact, preferred_element_type=f32)


def motion(maps_ref, v_ref, layers):
    size_x, slots, size_y = maps_ref.shape
    total = [jnp.zeros((slots, size_y), f32) for _ in range(3)]
    for x in range(size_x):
        part = maps_ref[x]
        for c in range(3):
            total[c] = total[c] + part * v_ref[c, x * layers : x * layers + 1, :]
    return [jnp.sum(t, axis=1, keepdims=True) for t in total]


def spread(at, reaction, out_ref):
    for x in range(out_ref.shape[1]):
        part = at(x)
        for c in range(3):
            out_ref[c, x : x + 1, :] = jnp.sum(part * reaction[c], axis=0, keepdims=True)


def footprints(table):
    lane = lanes_of(table)
    off_y = lane - table[:, AT_Y : AT_Y + 1].astype(jnp.int32)
    start_x = jnp.broadcast_to(table[:, AT_X : AT_X + 1], table.shape)
    within = (off_y >= 0) & (off_y < FOOT)
    inside = jnp.where(within, off_y, 0)
    lines = []
    for a in range(FOOT):
        picked = jnp.take_along_axis(table, inside + a * FOOT, axis=1)
        lines.append(jnp.where(within, picked, 0.0))

    def at(x):
        value = jnp.zeros(table.shape, f32)
        for a in range(FOOT):
            value = jnp.where(start_x == float(x - a), lines[a], value)
        return value

    return at


def surface_kernel(layers, table_ref, v_ref, maps_ref, moved_ref, push_ref):
    table = table_ref[...]
    lane = lanes_of(table)
    at = footprints(table)
    for x in range(maps_ref.shape[0]):
        maps_ref[x] = at(x)
    moved = motion(maps_ref, v_ref, layers)
    reaction = []
    rows = jnp.zeros(table.shape, f32)
    for c in range(3):
        rest, slope = (table[:, at + c : at + c + 1] for at in (AT_RATE, AT_COUPLING))
        reaction.append(time_step * FOOT * (rest - slope * moved[c]))
        rows = jnp.where(lane == FIRST + c, moved[c], rows)
    moved_ref[...] = rows
    spread(lambda x: maps_ref[x], reaction, push_ref)


def spread_thirds(moved, at, value):
    result = jnp.zeros(value.shape, f32)
    for e in range(3):
        result = jnp.where(third(value, e), moved[:, at + e : at + e + 1], result)
    return result


def motion_again_kernel(layers, v_ref, maps_ref, before_ref, next_ref, out_ref):
    moved = motion(maps_ref, v_ref, layers)
    rows = before_ref[...] + next_ref[...]
    lane = lanes_of(rows)
    for c in range(3):
        rows = jnp.where(lane == SECOND + c, moved[c], rows)
    out_ref[...] = rows


def prepare_kernel(
    sent_ref,
    back_ref,
    table_ref,
    base_ref,
    drift_ref,
    coupling_ref,
    counts_ref,
    owner_ref,
    stiff_hbm,
    push_ref,
    drift_out,
    rate_out,
    stiff_ref,
    sems,
):
    copies = fetch_strips(stiff_hbm, 0, stiff_ref, sems)
    table, sent, back = table_ref[...], sent_ref[...], back_ref[...]
    reaction = []
    for c in range(3):
        rest = back[:, AT_NEXT + c : AT_NEXT + c + 1]
        rest = rest + table[:, AT_SQUARE + c : AT_SQUARE + c + 1] * sent[:, FIRST + c : FIRST + c + 1]
        slope = table[:, AT_COUPLING + c : AT_COUPLING + c + 1]
        reaction.append(time_step * FOOT * (rest - slope * sent[:, SECOND + c : SECOND + c + 1]))
    spread(footprints(table), reaction, push_ref)
    _, of_slot = slot_table(owner_ref, back.shape[0])
    moved = jnp.dot(of_slot, back, precision=exact, preferred_element_type=f32)
    coupling = coupling_ref[...]
    mask = counted(counts_ref, coupling.shape)
    rate = base_ref[...] + time_step * coupling * spread_thirds(moved, FIRST, coupling)
    rate = jnp.where(mask, rate, 0.0)
    drift_out[...] = jnp.where(mask, drift_ref[...] + time_step * rate, 0.0)
    rate_out[...] = rate - time_step * coupling * (rate - spread_thirds(moved, SECOND, coupling))
    for copy in copies:
        copy.wait()


def finish_kernel(
    layers,
    v_ref,
    s_ref,
    buoy_ref,
    x_even,
    x_odd,
    y_even,
    y_odd,
    push_ref,
    half,
    rate_ref,
    counts_ref,
    early_ref,
    stiff_hbm,
    out_hbm,
    drift_out,
    rate_out,
    out_ref,
    ext,
    cols,
    slope,
    pull,
    late_ref,
    sems,
    out_sems,
):
    early = early_ref.shape[0]
    fetch_strips(stiff_hbm, early, late_ref, sems)
    size_x = v_ref.shape[1] // layers
    halo = (x_even, x_odd, y_even, y_odd)
    fresh = moving(layers, v_ref, s_ref, buoy_ref, halo, push_ref, ext, cols, slope)
    share = late_ref.shape[0] // sems.shape[0]
    strips = half.shape[0] // share
    sooner = early // share
    batch = size_x // strips

    def advance(strip):
        for i in range(batch):
            x = strip * batch + i
            v = fresh(x, pl.ds(pl.multiple_of(x * layers, layers), layers))
            for c in range(3):
                out_ref[x // TILE, c, :, lax.rem(x, TILE), :] = v[c]

    def multiply(stiff_ref, at, strip):
        cut = pl.ds(pl.multiple_of(strip * share, share), share)
        rounded = half[cut, :].astype(jnp.bfloat16)
        row = lax.broadcasted_iota(jnp.int32, rounded.shape, 0)
        total = jnp.zeros(rounded.shape, f32)
        for b in range(share):
            part = lax.dot_general(
                rounded,
                stiff_ref[strip * share + b - at],
                (((1,), (1,)), ((), ())),
                preferred_element_type=f32,
            )
            total = jnp.where(row == b, part, total)
        pull[cut, :] = total

    def leave(tile):
        return pltpu.make_async_copy(out_ref.at[tile], out_hbm.at[:, :, tile], out_sems.at[tile])

    def step(strip, carry):
        multiply(early_ref, 0, strip)
        advance(strip)
        return carry

    def late_step(strip, carry):
        begin = pl.multiple_of(strip * share - early, share)
        pltpu.make_async_copy(
            stiff_hbm.at[pl.ds(strip * share, share)],
            late_ref.at[pl.ds(begin, share)],
            sems.at[strip - sooner],
        ).wait()
        multiply(late_ref, early, strip)
        advance(strip)
        return carry

    tiles = size_x // TILE
    for tile in range(tiles):
        begin, end = tile * strips // tiles, (tile + 1) * strips // tiles
        middle = min(max(begin, sooner), end)
        lax.fori_loop(begin, middle, step, 0)
        lax.fori_loop(middle, end, late_step, 0)
        leave(tile).start()
    mask = counted(counts_ref, half.shape)
    rate = jnp.where(mask, rate_ref[...] - time_step * pull[...], 0.0)
    rate_out[...] = rate
    drift_out[...] = jnp.where(mask, half[...] + time_step * rate, 0.0)
    for tile in range(tiles):
        leave(tile).wait()


def trade(rows):
    devices = lax.axis_size("gx") * lax.axis_size("gy")
    blocks = rows.reshape(devices, CAP, rows.shape[1])
    blocks = lax.all_to_all(blocks, ("gx", "gy"), split_axis=0, concat_axis=0, tiled=True)
    return blocks.reshape(rows.shape)


def body(
    soil_velocity,
    soil_stress,
    buoyancy,
    lame_first,
    shear_modulus,
    stiffness,
    storey_drift,
    drift_rate,
    coupling,
    contact,
    dof_counts,
    owner_tile,
    corner_cell,
):
    layers, size_x, size_y = buoyancy.shape
    cells = layers * size_x
    number, width = storey_drift.shape
    slots = lax.axis_size("gx") * lax.axis_size("gy") * CAP
    span = size_y - FOOT + 1
    counts, owner, corner = (a.reshape(1, number) for a in (dof_counts, owner_tile, corner_cell))

    def bind(kernel, *fixed):
        def bound(*refs):
            kernel(*fixed, *refs)

        return bound

    def vm(*dims):
        return pltpu.VMEM(dims, f32)

    field = vm(cells, size_y)
    tall = layers + 2 * PAD
    plane = near_by(number, width)
    dma = pltpu.SemaphoreType.DMA
    flat = [a.reshape(cells, size_y) for a in (buoyancy, shear_modulus, lame_first)]
    far = (soil_velocity.reshape(3, cells, size_y), *flat[:2])
    far += (drift_rate, coupling, contact, counts, owner, corner)
    vt, bt, mt, one, two, col, rows = call(
        bind(first_kernel, layers, span),
        "first",
        (
            near_by(3, cells, size_y),
            near_by(cells, size_y),
            near_by(cells, size_y),
            near_by(7, layers, size_y),
            near_by(7, layers, size_y),
            near_by(16, cells),
            near_by(slots, 128),
        ),
        [Far(a) for a in far],
        [pltpu.VMEM(a.shape, a.dtype) for a in far] + [field, dma((len(far),))],
    )

    def exchange(one, two, col):
        return swap(one, "gx", 0), swap(two, "gx", 1), swap(col, "gy", 0), swap(col, "gy", 1)

    halo = exchange(one, two, col)
    rows = trade(rows)
    st, lt = call(
        bind(load_kernel, layers),
        "load",
        (near_by(6, cells, size_y), near_by(cells, size_y)),
        (rows, Far(soil_stress.reshape(6, cells, size_y)), Far(flat[2])),
        [vm(6, cells, size_y), field, dma((7,))],
    )
    half = number // 2
    payload = (near_by(5, layers, size_y), near_by(5, layers, size_y), near_by(16, cells))
    ext = vm(3, size_x + 4, tall, size_y)
    stack = vm(size_x + 1, tall, size_y)
    st, one, two, col, means, buoys, stiff = call(
        bind(begin_kernel, layers),
        "begin",
        (
            near_by(6, cells, size_y),
            *payload,
            near_by(5, cells, size_y),
            near_by(3, cells, size_y),
            near_by(half, width, width, dtype=stiffness.dtype),
        ),
        (vt, bt, mt, st, lt, Far(stiffness), *halo, rows),
        [
            stack,
            stack,
            stack,
            stack,
            ext,
            field,
            field,
            vm(3, cells, size_y),
            dma((1,)),
        ],
    )

    halo = exchange(one, two, col)
    maps, moved, push = call(
        bind(surface_kernel, layers),
        "surface",
        (near_by(size_x, slots, size_y), near_by(slots, 128), near_by(3, size_x, size_y)),
        (rows, vt),
    )
    chunks = 4 if number % 8 == 0 else 1
    base, drift, following = call(
        pull_kernel,
        "pull",
        (plane, plane, near_by(slots, 128)),
        (stiff, Far(stiffness), storey_drift, drift_rate, coupling, counts, owner),
        [
            vm(number, width),
            pltpu.VMEM((number - half, width, width), stiffness.dtype),
            dma((chunks,)),
        ],
    )
    push, following = lax.optimization_barrier((push, following))
    bulk = vm(5, size_x + 4, tall, size_y)
    vt, one, two, col = call(
        bind(velocity_kernel, layers),
        "velocity",
        (near_by(3, cells, size_y), *payload),
        (vt, st, buoys, *halo, push),
        [bulk, field, field, vm(3, cells, size_y)],
    )
    halo = exchange(one, two, col)
    (sent,) = call(
        bind(motion_again_kernel, layers),
        "motion_again",
        (near_by(slots, 128),),
        (vt, maps, moved, following),
    )
    vt, sent = lax.optimization_barrier((vt, sent))
    back = trade(sent)
    strips = size_x // STRIP
    st, one, two, col = call(
        bind(stress_kernel, layers),
        "stress",
        (near_by(6, cells, size_y), *payload),
        (vt, Far(st), Far(means), *halo),
        [
            vm(6, cells, size_y),
            vm(5, cells, size_y),
            ext,
            field,
            field,
            vm(3, cells, size_y),
            dma((2 * strips,)),
        ],
    )
    halo = exchange(one, two, col)
    sent, st = lax.optimization_barrier((sent, st))
    early = number // 4
    push, drift, rate, stiff = call(
        prepare_kernel,
        "prepare",
        (
            near_by(3, size_x, size_y),
            plane,
            plane,
            near_by(early, width, width, dtype=stiffness.dtype),
        ),
        (sent, back, rows, base, drift, coupling, counts, owner, Far(stiffness)),
        [dma((1,))],
    )
    tiles = size_x // TILE
    v, drift, rate = call(
        bind(finish_kernel, layers),
        "finish",
        (
            pltpu.HBM((3, layers, tiles, TILE, size_y), f32),
            shape(number, width),
            shape(number, width),
        ),
        (
            vt,
            st,
            buoys,
            *halo,
            push,
            drift,
            rate,
            counts,
            stiff,
            Far(stiffness),
        ),
        [
            vm(tiles, 3, layers, TILE, size_y),
            bulk,
            field,
            vm(3, cells, size_y),
            vm(number, width),
            pltpu.VMEM((number - early, width, width), stiffness.dtype),
            dma((3,)),
            dma((tiles,)),
        ],
        far_outs=(0,),
    )
    return v.reshape(soil_velocity.shape), drift, rate


def solution(mesh):
    both = ("gx", "gy")
    soil = P(None, None, "gx", "gy")
    cell = P(None, "gx", "gy")
    placed = (
        soil,
        soil,
        cell,
        cell,
        cell,
        P(both, None, None),
        P(both, None),
        P(both, None),
        P(both, None),
        P(both, None),
        P(both),
        P(both, None),
        P(both),
    )
    return jax.shard_map(
        body,
        mesh=mesh,
        in_specs=placed,
        out_specs=(soil, P(both, None), P(both, None)),
        check_vma=False,
    )
```

```python
import jax
import jax.numpy as jnp
from jax import lax
from jax.experimental import pallas as pl
from jax.experimental.pallas import tpu as pltpu
from jax.sharding import PartitionSpec as P

FOOT = 8
CAP = 2
PAD = 8
STRIP = 4
TILE = 8

near = 9.0 / 8.0
far = 1.0 / 24.0
time_step = 0.3
exact = lax.Precision.HIGHEST
f32 = jnp.float32

AT_X, AT_Y, AT_RATE, AT_COUPLING, AT_SQUARE, AT_CORNER = 64, 65, 66, 69, 72, 75
FIRST, SECOND, AT_NEXT = 0, 3, 8


COSTS = {
    "first": 30_000_000,
    "load": 20_000_000,
    "begin": 40_000_000,
    "stress": 25_000_000,
    "surface": 10_000_000,
    "pull": 30_000_000,
    "velocity": 25_000_000,
    "motion_again": 10_000_000,
    "prepare": 60_000_000,
    "finish": 60_000_000,
}


class Far:
    def __init__(self, value):
        self.value = value


def call(kernel, name, outs, args, scratch=(), far_outs=()):
    cost = COSTS[name]
    specs, values = [], []
    for a in args:
        far = isinstance(a, Far)
        a = a.value if far else a
        values.append(pltpu.with_memory_space_constraint(a, pltpu.HBM if far else pltpu.VMEM))
        specs.append(pl.BlockSpec(memory_space=pl.ANY if far else pltpu.VMEM))
    return pl.pallas_call(
        kernel,
        name=name,
        out_shape=outs,
        in_specs=specs,
        out_specs=tuple(
            pl.BlockSpec(memory_space=pl.ANY if i in far_outs else pltpu.VMEM)
            for i in range(len(outs))
        ),
        scratch_shapes=list(scratch),
        cost_estimate=pl.CostEstimate(flops=1000*cost, bytes_accessed=cost, transcendentals=0),
        compiler_params=pltpu.CompilerParams(vmem_limit_bytes=16 * 2**20),
    )(*values)


def shape(*dims):
    return jax.ShapeDtypeStruct(dims, f32)


def near_by(*dims, dtype=f32):
    return pltpu.VMEM(dims, dtype)


def fetch(sources, targets, sems):
    copies = [
        pltpu.make_async_copy(source, target, sems.at[i])
        for i, (source, target) in enumerate(zip(sources, targets))
    ]
    for copy in copies:
        copy.start()
    return copies


def swap(block, axis, odd):
    size = lax.axis_size(axis)
    pairs = [(i % size, (i + 1) % size) for i in range(odd, size + odd, 2)]
    return lax.ppermute(block, axis, pairs + [(b, a) for a, b in pairs])


def even(axis):
    return lax.rem(lax.axis_index(axis), 2) == 0


def two_ways(up, down, even_ref, odd_ref):
    lead = even("gx")
    blank = jnp.zeros(even_ref.shape[1:], f32)
    for row in range(even_ref.shape[0]):
        a = up[row] if row < len(up) else blank
        b = down[row] if row < len(down) else blank
        even_ref[row] = jnp.where(lead, a, b)
        odd_ref[row] = jnp.where(lead, b, a)


def below_above(axis, even_ref, odd_ref):
    lead = even(axis)

    def below(index):
        return jnp.where(lead, odd_ref[index], even_ref[index])

    def above(index):
        return jnp.where(lead, even_ref[index], odd_ref[index])

    return below, above


def lanes_of(value):
    return lax.broadcasted_iota(jnp.int32, value.shape, len(value.shape) - 1)


def roll(value, amount):
    return pltpu.roll(value, amount % value.shape[-1], len(value.shape) - 1)


def packed(pieces):
    result = None
    for slab, first, count, amount in pieces:
        moved = roll(slab, amount) if amount else slab
        if result is None:
            result = moved
        else:
            lane = lanes_of(slab)
            result = jnp.where((lane >= first) & (lane < first + count), moved, result)
    return result


def send_columns(pack_ref, out_ref):
    rows, width = out_ref.shape
    for block in range(width // 128):
        part = pack_ref[block * 128 : (block + 1) * 128, :]
        out_ref[:, block * 128 : (block + 1) * 128] = part.T[:rows]


def receive_columns(even_ref, odd_ref, from_south, south_ok, north_ok, out_ref):
    rows, width = even_ref.shape
    below, above = below_above("gy", even_ref, odd_ref)
    for block in range(width // 128):
        cut = slice(block * 128, (block + 1) * 128)
        south = jnp.where(south_ok, below((slice(None), cut)), 0.0)
        north = jnp.where(north_ok, above((slice(None), cut)), 0.0)
        row = lax.broadcasted_iota(jnp.int32, south.shape, 0)
        taken = row == from_south[0]
        for other in from_south[1:]:
            taken = taken | (row == other)
        part = jnp.where(taken, south, north)
        whole = jnp.concatenate([part, jnp.zeros((128 - rows, 128), f32)], axis=0)
        out_ref[cut, :] = whole.T


def bands(forward, amount):
    row = lax.broadcasted_iota(jnp.int32, (256, 128), 0)
    lane = row - 128
    beyond = jnp.where(lane < amount, lane - amount, 128 + lane - amount)
    shift = jnp.where(row < 128, row, beyond) - lax.broadcasted_iota(jnp.int32, (256, 128), 1)
    first, last = (amount - 1, amount + 1) if forward else (amount - 2, amount)
    valid = (row < 128) | ((lane >= first) & (lane <= last))
    value = jnp.zeros((256, 128), f32)
    at = 0 if forward else -1
    for step, entry in ((at + 1, 27.0), (at, -27.0), (at + 2, -1.0), (at - 1, 1.0)):
        value = jnp.where(shift == step, entry, value)
    return jnp.where(valid, value, 0.0).astype(jnp.bfloat16)


def parted(value):
    large = value.astype(jnp.bfloat16)
    return large, (value - large.astype(f32)).astype(jnp.bfloat16)


def slopes(fields, cols, out_ref):
    matrices = [bands(forward, amount) for _, forward, amount in fields]
    size = 512
    for begin in range(0, cols.shape[0], size):
        cut = slice(begin, begin + size)
        ghost = parted(cols[cut, :])
        for i, (read, _, _) in enumerate(fields):
            total = None
            for own, other in zip(parted(read(cut)), ghost):
                both = jnp.concatenate([own, other], axis=1)
                part = jnp.dot(both, matrices[i], preferred_element_type=f32)
                total = part if total is None else total + part
            out_ref[i, cut, :] = total * (1.0 / 24.0)


def across(ext, c, x, forward, layers):
    def at(d):
        return ext[c, x + 2 + d, PAD : PAD + layers, :]

    if forward:
        return near * (at(1) - at(0)) - far * (at(2) - at(-1))
    return near * (at(0) - at(-1)) - far * (at(1) - at(-2))


def down(ext, c, x, forward, layers):
    def at(d):
        return ext[c, x + 2, PAD + d : PAD + layers + d, :]

    if forward:
        return near * (at(1) - at(0)) - far * (at(2) - at(-1))
    return near * (at(0) - at(-1)) - far * (at(1) - at(-2))


def place():
    gx, gy = lax.axis_index("gx"), lax.axis_index("gy")
    nx, ny = lax.axis_size("gx"), lax.axis_size("gy")
    return gx > 0, gx < nx - 1, gy > 0, gy < ny - 1


def fill(ext, c, source, src, size_x, layers):
    for x in range(size_x):
        ext[c, x + 2, 0:PAD, :] = jnp.zeros((PAD, 128), f32)
        ext[c, x + 2, PAD : PAD + layers, :] = source[src, x * layers : (x + 1) * layers, :]
        ext[c, x + 2, PAD + layers : PAD + layers + PAD, :] = jnp.zeros((PAD, 128), f32)


def edges(layers, v_ref, b_ref, m_ref, vt_ref, bt_ref, mt_ref, even_ref, odd_ref, col_ref, pack):
    size_x = vt_ref.shape[1] // layers

    def slab(ref, x):
        return ref[x * layers : (x + 1) * layers, :]

    for x in range(size_x):
        cut = pl.ds(x * layers, layers)
        turned = pl.ds(x, layers, stride=size_x)
        v = [v_ref[c, turned, :] for c in range(3)]
        buoy, shear = b_ref[turned, :], m_ref[turned, :]
        for c in range(3):
            vt_ref[c, cut, :] = v[c]
        bt_ref[cut, :] = buoy
        mt_ref[cut, :] = shear
        pack[cut, :] = packed(
            [(v[0], 0, 3, 1), (v[1], 3, 3, 5), (v[2], 6, 3, 7), (buoy, 9, 1, 9), (shear, 10, 1, 10)]
        )
    last = size_x - 1
    up = [slab(vt_ref.at[c], x) for c, x in ((0, last - 1), (0, last), (1, last), (2, last))]
    down = [slab(vt_ref.at[c], x) for c, x in ((0, 0), (1, 0), (1, 1), (2, 0), (2, 1))]
    two_ways(up, down + [slab(bt_ref, 0), slab(mt_ref, 0)], even_ref, odd_ref)
    send_columns(pack, col_ref)


def load_kernel(layers, after_ref, s_hbm, l_hbm, st_ref, lt_ref, s_ref, l_ref, sems):
    del after_ref
    size_x = l_ref.shape[0] // layers
    copies = fetch(
        [l_hbm] + [s_hbm.at[c] for c in range(6)], [l_ref] + [s_ref.at[c] for c in range(6)], sems
    )
    for c, copy in enumerate(copies):
        copy.wait()
        for x in range(size_x):
            cut, turned = pl.ds(x * layers, layers), pl.ds(x, layers, stride=size_x)
            if c == 0:
                lt_ref[cut, :] = l_ref[turned, :]
            else:
                st_ref[c - 1, cut, :] = s_ref[c - 1, turned, :]


def materials(layers, b_ref, l_ref, m_ref, above, cols, table_ref, mat_ref, buoy_ref, bs, ms, tb, tm):
    size_x = b_ref.shape[0] // layers
    _, east_ok, _, north_ok = place()
    nx, ny = lax.axis_size("gx"), lax.axis_size("gy")
    beyond = lax.rem(lax.axis_index("gx") + 1, nx) * ny + lax.rem(lax.axis_index("gy") + 1, ny)
    inner = slice(PAD, PAD + layers)
    for x in range(size_x):
        cut = slice(x * layers, (x + 1) * layers)
        bs[x, inner, :] = b_ref[cut, :]
        ms[x, inner, :] = m_ref[cut, :]
        part = cols[cut, :]
        tb[x, inner, :] = roll(part, -9)
        tm[x, inner, :] = roll(part, -10)
    bs[size_x, inner, :] = above(5)
    ms[size_x, inner, :] = above(6)
    line = jnp.broadcast_to(table_ref[pl.ds(beyond * CAP, 1), :], (layers, 128))
    own = lanes_of(line) - AT_CORNER == lax.broadcasted_iota(jnp.int32, line.shape, 0)
    corner = jnp.sum(jnp.where(own, line, 0.0), axis=1, keepdims=True)
    tm[size_x, inner, :] = jnp.broadcast_to(corner, line.shape)
    zero = jnp.zeros((PAD, 128), f32)
    for x in range(size_x + 1):
        bs[x, PAD + layers : PAD + layers + PAD, :] = zero
        ms[x, PAD + layers : PAD + layers + PAD, :] = zero
        tm[x, PAD + layers : PAD + layers + PAD, :] = zero
    below = slice(PAD + 1, PAD + layers + 1)

    def step(x, carry):
        cut = pl.ds(pl.multiple_of(x * layers, layers), layers)
        b, m = bs[x, inner, :], ms[x, inner, :]
        lane = lanes_of(b)
        layer = lax.broadcasted_iota(jnp.int32, b.shape, 0)
        in_x = (x < size_x - 1) | east_ok
        in_y = (lane < 127) | north_ok
        in_z = layer < layers - 1

        def north(value, ghost):
            return roll(jnp.where(lane == 0, ghost, value), -1)

        b_e = jnp.where(in_x, bs[x + 1, inner, :], b)
        b_n = jnp.where(in_y, north(b, tb[x, inner, :]), b)
        b_z = jnp.where(in_z, bs[x, below, :], b)
        m_e = jnp.where(in_x, ms[x + 1, inner, :], m)
        m_n = jnp.where(in_y, north(m, tm[x, inner, :]), m)
        m_z = jnp.where(in_z, ms[x, below, :], m)
        m_en = jnp.where(in_y & in_x, north(ms[x + 1, inner, :], tm[x + 1, inner, :]), m)
        m_ez = jnp.where(in_z & in_x, ms[x + 1, below, :], m)
        m_nz = jnp.where(in_z & in_y, north(ms[x, below, :], tm[x, below, :]), m)
        mat_ref[0, cut, :] = time_step * l_ref[cut, :]
        mat_ref[1, cut, :] = (2.0 * time_step) * m
        mat_ref[2, cut, :] = (0.25 * time_step) * (m + m_e + m_n + m_en)
        mat_ref[3, cut, :] = (0.25 * time_step) * (m + m_e + m_z + m_ez)
        mat_ref[4, cut, :] = (0.25 * time_step) * (m + m_n + m_z + m_nz)
        buoy_ref[0, cut, :] = (0.5 * time_step) * (b + b_e)
        buoy_ref[1, cut, :] = (0.5 * time_step) * (b + b_n)
        buoy_ref[2, cut, :] = (0.5 * time_step) * (b + b_z)
        return carry

    lax.fori_loop(0, size_x, step, 0, unroll=4)


def extend(ext, rows, at, ok, layers):
    for row, c, x in rows:
        ext[c, x, PAD : PAD + layers, :] = jnp.where(ok, at(row), 0.0)


def stresses(layers, v_ref, old, ready, mat_ref, below, above, cols, out_ref, refs, ext, pack, slope):
    even_ref, odd_ref, col_ref = refs
    size_x = v_ref.shape[1] // layers
    west_ok, east_ok, _, _ = place()
    for c in range(3):
        fill(ext, c, v_ref, c, size_x, layers)
    extend(ext, ((0, 0, 0), (1, 0, 1), (2, 1, 1), (3, 2, 1)), below, west_ok, layers)
    over = size_x + 2
    rows = ((0, 0, over), (1, 1, over), (2, 1, over + 1), (3, 2, over), (4, 2, over + 1))
    extend(ext, rows, above, east_ok, layers)

    fields = (
        (lambda cut: v_ref[1, cut, :], False, 5),
        (lambda cut: v_ref[0, cut, :], True, 1),
        (lambda cut: v_ref[2, cut, :], True, 7),
    )
    slopes(fields, cols, slope)

    def step(x, carry):
        cut = pl.ds(pl.multiple_of(x * layers, layers), layers)
        dx = across(ext, 0, x, False, layers)
        dy = slope[0, cut, :]
        dz = down(ext, 2, x, False, layers)
        both = mat_ref[0, cut, :] * (dx + dy + dz)
        twice = mat_ref[1, cut, :]
        xx = old(0, x, cut) + (both + twice * dx)
        yy = old(1, x, cut) + (both + twice * dy)
        zz = old(2, x, cut) + (both + twice * dz)
        xy = old(3, x, cut) + mat_ref[2, cut, :] * (
            slope[1, cut, :] + across(ext, 1, x, True, layers)
        )
        xz = old(4, x, cut) + mat_ref[3, cut, :] * (
            down(ext, 0, x, True, layers) + across(ext, 2, x, True, layers)
        )
        yz = old(5, x, cut) + mat_ref[4, cut, :] * (
            down(ext, 1, x, True, layers) + slope[2, cut, :]
        )
        for c, value in enumerate((xx, yy, zz, xy, xz, yz)):
            out_ref[c, cut, :] = value
        pack[cut, :] = packed([(yy, 0, 3, 1), (xy, 3, 3, 5), (yz, 6, 3, 8)])
        return carry

    for strip in range(size_x // STRIP):
        ready(strip)
        lax.fori_loop(strip * STRIP, (strip + 1) * STRIP, step, 0, unroll=4)
    send_columns(pack, col_ref)

    def slab(c, x):
        return out_ref[c, x * layers : (x + 1) * layers, :]

    up = [slab(c, size_x - x) for c, x in ((0, 1), (3, 2), (3, 1), (4, 2), (4, 1))]
    two_ways(up, [slab(c, x) for c, x in ((0, 0), (0, 1), (3, 0), (4, 0))], even_ref, odd_ref)


def begin_kernel(
    layers,
    v_ref,
    b_ref,
    m_ref,
    s_ref,
    l_ref,
    stiff_hbm,
    x_even,
    x_odd,
    y_even,
    y_odd,
    table_ref,
    out_ref,
    even_ref,
    odd_ref,
    col_ref,
    mat_ref,
    buoy_ref,
    stiff_ref,
    bs,
    ms,
    tb,
    tm,
    ext,
    cols,
    pack,
    slope,
    sems,
):
    half = stiff_ref.shape[0]
    half = stiff_ref.shape[0]
    copies = fetch([stiff_hbm.at[pl.ds(0, half)]], [stiff_ref], sems)
    _, _, south_ok, north_ok = place()
    below, above = below_above("gx", x_even, x_odd)
    receive_columns(y_even, y_odd, (0, 3, 4, 6), south_ok, north_ok, cols)
    materials(layers, b_ref, l_ref, m_ref, above, cols, table_ref, mat_ref, buoy_ref, bs, ms, tb, tm)

    def ready(strip):
        pass

    def old(c, x, cut):
        return s_ref[c, cut, :]

    refs = (even_ref, odd_ref, col_ref)
    stresses(layers, v_ref, old, ready, mat_ref, below, above, cols, out_ref, refs, ext, pack, slope)
    copies[0].wait()


def stress_kernel(
    layers,
    v_ref,
    s_hbm,
    mat_hbm,
    x_even,
    x_odd,
    y_even,
    y_odd,
    out_ref,
    even_ref,
    odd_ref,
    col_ref,
    s_ref,
    mat_ref,
    ext,
    cols,
    pack,
    slope,
    sems,
):
    strips = v_ref.shape[1] // layers // STRIP
    cuts = [pl.ds(strip * STRIP * layers, STRIP * layers) for strip in range(strips)]
    sources, targets = [], []
    for cut in cuts:
        sources += [s_hbm.at[:, cut], mat_hbm.at[:, cut]]
        targets += [s_ref.at[:, cut], mat_ref.at[:, cut]]
    copies = fetch(sources, targets, sems)
    _, _, south_ok, north_ok = place()
    below, above = below_above("gx", x_even, x_odd)
    receive_columns(y_even, y_odd, (0, 3, 4, 6), south_ok, north_ok, cols)

    def ready(strip):
        copies[2 * strip].wait()
        copies[2 * strip + 1].wait()

    def old(c, x, cut):
        return s_ref[c, cut, :]

    refs = (even_ref, odd_ref, col_ref)
    stresses(layers, v_ref, old, ready, mat_ref, below, above, cols, out_ref, refs, ext, pack, slope)


def moving(layers, v_ref, s_ref, buoy_ref, halo, push_ref, ext, cols, slope):
    x_even, x_odd, y_even, y_odd = halo
    size_x = v_ref.shape[1] // layers
    west_ok, east_ok, south_ok, north_ok = place()
    below, above = below_above("gx", x_even, x_odd)
    receive_columns(y_even, y_odd, (0, 3, 4, 6, 7), south_ok, north_ok, cols)
    for c, src in enumerate((0, 3, 4, 5, 2)):
        fill(ext, c, s_ref, src, size_x, layers)
    rows = ((0, 0, 1), (1, 1, 0), (2, 1, 1), (3, 2, 0), (4, 2, 1))
    extend(ext, rows, below, west_ok, layers)
    over = size_x + 2
    extend(ext, ((0, 0, over), (1, 0, over + 1), (2, 1, over), (3, 2, over)), above, east_ok, layers)

    fields = (
        (lambda cut: s_ref[3, cut, :], False, 5),
        (lambda cut: s_ref[1, cut, :], True, 1),
        (lambda cut: s_ref[5, cut, :], False, 8),
    )
    slopes(fields, cols, slope)

    def fresh(x, cut):
        ax = across(ext, 0, x, True, layers) + slope[0, cut, :] + down(ext, 2, x, False, layers)
        ay = across(ext, 1, x, False, layers) + slope[1, cut, :] + down(ext, 3, x, False, layers)
        az = across(ext, 2, x, False, layers) + slope[2, cut, :] + down(ext, 4, x, True, layers)
        layer = lax.broadcasted_iota(jnp.int32, ax.shape, 0)
        result = []
        for c, accel in enumerate((ax, ay, az)):
            pushed = jnp.where(layer == 0, push_ref[c, pl.ds(x, 1), :], 0.0)
            result.append(v_ref[c, cut, :] + buoy_ref[c, cut, :] * accel + pushed)
        return result

    return fresh


def velocity_kernel(
    layers,
    v_ref,
    s_ref,
    buoy_ref,
    x_even,
    x_odd,
    y_even,
    y_odd,
    push_ref,
    out_ref,
    even_ref,
    odd_ref,
    col_ref,
    ext,
    cols,
    pack,
    slope,
):
    size_x = v_ref.shape[1] // layers
    halo = (x_even, x_odd, y_even, y_odd)
    fresh = moving(layers, v_ref, s_ref, buoy_ref, halo, push_ref, ext, cols, slope)

    def step(x, carry):
        cut = pl.ds(pl.multiple_of(x * layers, layers), layers)
        v = fresh(x, cut)
        for c in range(3):
            out_ref[c, cut, :] = v[c]
        pack[cut, :] = packed([(v[0], 0, 3, 1), (v[1], 3, 3, 5), (v[2], 6, 3, 7)])
        return carry

    lax.fori_loop(0, size_x, step, 0, unroll=8)
    send_columns(pack, col_ref)

    def slab(c, x):
        return out_ref[c, x * layers : (x + 1) * layers, :]

    up = [slab(c, size_x - x) for c, x in ((0, 2), (0, 1), (1, 1), (2, 1))]
    down_rows = [slab(c, x) for c, x in ((0, 0), (1, 0), (1, 1), (2, 0), (2, 1))]
    two_ways(up, down_rows, even_ref, odd_ref)


def third(value, e):
    d = lanes_of(value).astype(f32)
    return d - 3.0 * jnp.floor((d + 0.5) * (1.0 / 3.0)) == e


def column(row):
    n = row.shape[1]
    same = lax.broadcasted_iota(jnp.int32, (n, n), 0) == lax.broadcasted_iota(jnp.int32, (n, n), 1)
    return jnp.sum(jnp.where(same, row, 0.0), axis=1, keepdims=True)


def slot_table(owner_ref, slots):
    number = owner_ref.shape[1]
    owner = owner_ref[...].astype(f32)
    owner_col = column(owner)
    same = owner_col == owner
    i = lax.broadcasted_iota(jnp.int32, same.shape, 0)
    j = lax.broadcasted_iota(jnp.int32, same.shape, 1)
    slot_row = owner * CAP + jnp.sum(jnp.where(same & (i < j), 1.0, 0.0), axis=0, keepdims=True)
    slot_col = owner_col * CAP + jnp.sum(jnp.where(same & (j < i), 1.0, 0.0), axis=1, keepdims=True)
    to_slot = lax.broadcasted_iota(jnp.int32, (slots, number), 0).astype(f32) == slot_row
    of_slot = lax.broadcasted_iota(jnp.int32, (number, slots), 1).astype(f32) == slot_col
    return jnp.where(to_slot, 1.0, 0.0), jnp.where(of_slot, 1.0, 0.0)


def counted(counts_ref, shape):
    return lax.broadcasted_iota(jnp.int32, shape, 1).astype(f32) < column(
        counts_ref[...].astype(f32)
    )


def table(
    span,
    rate_ref,
    coupling_ref,
    contact_ref,
    counts_ref,
    owner_ref,
    corner_ref,
    out_ref,
):
    number, width = rate_ref.shape
    slots = out_ref.shape[0]
    mask = counted(counts_ref, (number, width))
    rate = jnp.where(mask, rate_ref[...], 0.0)
    coupling = jnp.where(mask, coupling_ref[...], 0.0)
    contact = contact_ref[...]
    weights = contact / jnp.sum(contact, axis=1, keepdims=True)
    corner = column(corner_ref[...].astype(f32))
    start_x = jnp.floor((corner + 0.5) * (1.0 / span))
    start_y = corner - start_x * span
    row = jnp.concatenate([weights, jnp.zeros((number, 128 - weights.shape[1]), f32)], axis=1)
    lane = lanes_of(row)
    row = jnp.where(lane == AT_X, start_x, row)
    row = jnp.where(lane == AT_Y, start_y, row)
    sums = (
        (AT_RATE, coupling * rate),
        (AT_COUPLING, coupling),
        (AT_SQUARE, time_step * coupling * coupling),
    )
    row = sums_by_third(row, sums)
    to_slot, _ = slot_table(owner_ref, slots)
    out_ref[...] = jnp.dot(to_slot, row, precision=exact, preferred_element_type=f32)


def first_kernel(layers, span, *refs):
    far, outs, near, pack, sems = refs[:9], refs[9:16], refs[16:25], refs[25], refs[26]
    rows_ref, shear_ref = outs[6], outs[2]
    order = list(range(3, 9)) + list(range(3))
    copies = fetch([far[i] for i in order], [near[i] for i in order], sems)
    for copy in copies[:6]:
        copy.wait()
    table(span, *near[3:], rows_ref)
    for copy in copies[6:]:
        copy.wait()
    edges(layers, *near[:3], *outs[:6], pack)
    first = shear_ref[pl.ds(0, layers), 0:1]
    spot = lax.broadcasted_iota(jnp.int32, (layers, 128), 1) - AT_CORNER
    own = spot == lax.broadcasted_iota(jnp.int32, (layers, 128), 0)
    rows_ref[...] += jnp.sum(jnp.where(own, first, 0.0), axis=0, keepdims=True)


def sums_by_third(row, sums):
    lane = lanes_of(row)
    for at, value in sums:
        for e in range(3):
            total = jnp.sum(jnp.where(third(value, e), value, 0.0), axis=1, keepdims=True)
            row = jnp.where(lane == at + e, total, row)
    return row


def fetch_strips(stiff_hbm, begin, stiff_ref, sems):
    size = stiff_ref.shape[0] // sems.shape[0]
    strips = range(sems.shape[0])
    return fetch(
        [stiff_hbm.at[pl.ds(begin + c * size, size)] for c in strips],
        [stiff_ref.at[pl.ds(c * size, size)] for c in strips],
        sems,
    )


def products(stiff_ref, at, drift_ref, out_ref, begin, end):
    group = 16
    for g in range(begin // group * group, end, group):
        rounded = drift_ref[g : g + group, :].astype(jnp.bfloat16)
        row = lax.broadcasted_iota(jnp.int32, rounded.shape, 0)
        low, high = max(g, begin), min(g + group, end)
        total = out_ref[g : g + group, :]
        for b in range(low, high):
            part = lax.dot_general(
                rounded, stiff_ref[b - at], (((1,), (1,)), ((), ())), preferred_element_type=f32
            )
            total = jnp.where(row == b - g, part, total)
        out_ref[g : g + group, :] = total


def pull_kernel(
    stiff_ref,
    stiff_hbm,
    raw_ref,
    rate_ref,
    coupling_ref,
    counts_ref,
    owner_ref,
    base_ref,
    drift_out,
    next_ref,
    pull,
    rest_ref,
    sems,
):
    number, half = drift_out.shape[0], stiff_ref.shape[0]
    copies = fetch_strips(stiff_hbm, half, rest_ref, sems)
    mask = counted(counts_ref, drift_out.shape)
    drift_out[...] = jnp.where(mask, raw_ref[...], 0.0)
    pull[...] = jnp.zeros(pull.shape, f32)
    products(stiff_ref, 0, drift_out, pull, 0, half)
    size = (number - half) // len(copies)
    for c, copy in enumerate(copies):
        copy.wait()
        products(rest_ref, half, drift_out, pull, half + c * size, half + (c + 1) * size)
    rate = jnp.where(mask, rate_ref[...], 0.0)
    coupling = jnp.where(mask, coupling_ref[...], 0.0)
    base = rate - time_step * pull[...] - time_step * coupling * rate
    base = jnp.where(mask, base, 0.0)
    base_ref[...] = base
    row = sums_by_third(jnp.zeros((number, 128), f32), ((AT_NEXT, coupling * base),))
    to_slot, _ = slot_table(owner_ref, next_ref.shape[0])
    next_ref[...] = jnp.dot(to_slot, row, precision=exact, preferred_element_type=f32)


def motion(maps_ref, v_ref, layers):
    size_x, slots, size_y = maps_ref.shape
    total = [jnp.zeros((slots, size_y), f32) for _ in range(3)]
    for x in range(size_x):
        part = maps_ref[x]
        for c in range(3):
            total[c] = total[c] + part * v_ref[c, x * layers : x * layers + 1, :]
    return [jnp.sum(t, axis=1, keepdims=True) for t in total]


def spread(at, reaction, out_ref):
    for x in range(out_ref.shape[1]):
        part = at(x)
        for c in range(3):
            out_ref[c, x : x + 1, :] = jnp.sum(part * reaction[c], axis=0, keepdims=True)


def footprints(table):
    lane = lanes_of(table)
    off_y = lane - table[:, AT_Y : AT_Y + 1].astype(jnp.int32)
    start_x = jnp.broadcast_to(table[:, AT_X : AT_X + 1], table.shape)
    within = (off_y >= 0) & (off_y < FOOT)
    inside = jnp.where(within, off_y, 0)
    lines = []
    for a in range(FOOT):
        picked = jnp.take_along_axis(table, inside + a * FOOT, axis=1)
        lines.append(jnp.where(within, picked, 0.0))

    def at(x):
        value = jnp.zeros(table.shape, f32)
        for a in range(FOOT):
            value = jnp.where(start_x == float(x - a), lines[a], value)
        return value

    return at


def surface_kernel(layers, table_ref, v_ref, maps_ref, moved_ref, push_ref):
    table = table_ref[...]
    lane = lanes_of(table)
    at = footprints(table)
    for x in range(maps_ref.shape[0]):
        maps_ref[x] = at(x)
    moved = motion(maps_ref, v_ref, layers)
    reaction = []
    rows = jnp.zeros(table.shape, f32)
    for c in range(3):
        rest, slope = (table[:, at + c : at + c + 1] for at in (AT_RATE, AT_COUPLING))
        reaction.append(time_step * FOOT * (rest - slope * moved[c]))
        rows = jnp.where(lane == FIRST + c, moved[c], rows)
    moved_ref[...] = rows
    spread(lambda x: maps_ref[x], reaction, push_ref)


def spread_thirds(moved, at, value):
    result = jnp.zeros(value.shape, f32)
    for e in range(3):
        result = jnp.where(third(value, e), moved[:, at + e : at + e + 1], result)
    return result


def motion_again_kernel(layers, v_ref, maps_ref, before_ref, next_ref, out_ref):
    moved = motion(maps_ref, v_ref, layers)
    rows = before_ref[...] + next_ref[...]
    lane = lanes_of(rows)
    for c in range(3):
        rows = jnp.where(lane == SECOND + c, moved[c], rows)
    out_ref[...] = rows


def prepare_kernel(
    sent_ref,
    back_ref,
    table_ref,
    base_ref,
    drift_ref,
    coupling_ref,
    counts_ref,
    owner_ref,
    stiff_hbm,
    push_ref,
    drift_out,
    rate_out,
    stiff_ref,
    sems,
):
    copies = fetch_strips(stiff_hbm, 0, stiff_ref, sems)
    table, sent, back = table_ref[...], sent_ref[...], back_ref[...]
    reaction = []
    for c in range(3):
        rest = back[:, AT_NEXT + c : AT_NEXT + c + 1]
        rest = rest + table[:, AT_SQUARE + c : AT_SQUARE + c + 1] * sent[:, FIRST + c : FIRST + c + 1]
        slope = table[:, AT_COUPLING + c : AT_COUPLING + c + 1]
        reaction.append(time_step * FOOT * (rest - slope * sent[:, SECOND + c : SECOND + c + 1]))
    spread(footprints(table), reaction, push_ref)
    _, of_slot = slot_table(owner_ref, back.shape[0])
    moved = jnp.dot(of_slot, back, precision=exact, preferred_element_type=f32)
    coupling = coupling_ref[...]
    mask = counted(counts_ref, coupling.shape)
    rate = base_ref[...] + time_step * coupling * spread_thirds(moved, FIRST, coupling)
    rate = jnp.where(mask, rate, 0.0)
    drift_out[...] = jnp.where(mask, drift_ref[...] + time_step * rate, 0.0)
    rate_out[...] = rate - time_step * coupling * (rate - spread_thirds(moved, SECOND, coupling))
    for copy in copies:
        copy.wait()


def finish_kernel(
    layers,
    v_ref,
    s_ref,
    buoy_ref,
    x_even,
    x_odd,
    y_even,
    y_odd,
    push_ref,
    half,
    rate_ref,
    counts_ref,
    early_ref,
    stiff_hbm,
    out_hbm,
    drift_out,
    rate_out,
    out_ref,
    ext,
    cols,
    slope,
    pull,
    late_ref,
    sems,
    out_sems,
):
    early = early_ref.shape[0]
    fetch_strips(stiff_hbm, early, late_ref, sems)
    size_x = v_ref.shape[1] // layers
    halo = (x_even, x_odd, y_even, y_odd)
    fresh = moving(layers, v_ref, s_ref, buoy_ref, halo, push_ref, ext, cols, slope)
    share = late_ref.shape[0] // sems.shape[0]
    strips = half.shape[0] // share
    sooner = early // share
    batch = size_x // strips

    def advance(strip):
        for i in range(batch):
            x = strip * batch + i
            v = fresh(x, pl.ds(pl.multiple_of(x * layers, layers), layers))
            for c in range(3):
                out_ref[x // TILE, c, :, lax.rem(x, TILE), :] = v[c]

    def multiply(stiff_ref, at, strip):
        cut = pl.ds(pl.multiple_of(strip * share, share), share)
        rounded = half[cut, :].astype(jnp.bfloat16)
        row = lax.broadcasted_iota(jnp.int32, rounded.shape, 0)
        total = jnp.zeros(rounded.shape, f32)
        for b in range(share):
            part = lax.dot_general(
                rounded,
                stiff_ref[strip * share + b - at],
                (((1,), (1,)), ((), ())),
                preferred_element_type=f32,
            )
            total = jnp.where(row == b, part, total)
        pull[cut, :] = total

    def leave(tile):
        return pltpu.make_async_copy(out_ref.at[tile], out_hbm.at[:, :, tile], out_sems.at[tile])

    def step(strip, carry):
        multiply(early_ref, 0, strip)
        advance(strip)
        return carry

    def late_step(strip, carry):
        begin = pl.multiple_of(strip * share - early, share)
        pltpu.make_async_copy(
            stiff_hbm.at[pl.ds(strip * share, share)],
            late_ref.at[pl.ds(begin, share)],
            sems.at[strip - sooner],
        ).wait()
        multiply(late_ref, early, strip)
        advance(strip)
        return carry

    tiles = size_x // TILE
    for tile in range(tiles):
        begin, end = tile * strips // tiles, (tile + 1) * strips // tiles
        middle = min(max(begin, sooner), end)
        lax.fori_loop(begin, middle, step, 0)
        lax.fori_loop(middle, end, late_step, 0)
        leave(tile).start()
    mask = counted(counts_ref, half.shape)
    rate = jnp.where(mask, rate_ref[...] - time_step * pull[...], 0.0)
    rate_out[...] = rate
    drift_out[...] = jnp.where(mask, half[...] + time_step * rate, 0.0)
    for tile in range(tiles):
        leave(tile).wait()


def trade(rows):
    devices = lax.axis_size("gx") * lax.axis_size("gy")
    blocks = rows.reshape(devices, CAP, rows.shape[1])
    blocks = lax.all_to_all(blocks, ("gx", "gy"), split_axis=0, concat_axis=0, tiled=True)
    return blocks.reshape(rows.shape)


def body(
    soil_velocity,
    soil_stress,
    buoyancy,
    lame_first,
    shear_modulus,
    stiffness,
    storey_drift,
    drift_rate,
    coupling,
    contact,
    dof_counts,
    owner_tile,
    corner_cell,
):
    layers, size_x, size_y = buoyancy.shape
    cells = layers * size_x
    number, width = storey_drift.shape
    slots = lax.axis_size("gx") * lax.axis_size("gy") * CAP
    span = size_y - FOOT + 1
    counts, owner, corner = (a.reshape(1, number) for a in (dof_counts, owner_tile, corner_cell))

    def bind(kernel, *fixed):
        def bound(*refs):
            kernel(*fixed, *refs)

        return bound

    def vm(*dims):
        return pltpu.VMEM(dims, f32)

    field = vm(cells, size_y)
    tall = layers + 2 * PAD
    plane = near_by(number, width)
    dma = pltpu.SemaphoreType.DMA
    flat = [a.reshape(cells, size_y) for a in (buoyancy, shear_modulus, lame_first)]
    far = (soil_velocity.reshape(3, cells, size_y), *flat[:2])
    far += (drift_rate, coupling, contact, counts, owner, corner)
    vt, bt, mt, one, two, col, rows = call(
        bind(first_kernel, layers, span),
        "first",
        (
            near_by(3, cells, size_y),
            near_by(cells, size_y),
            near_by(cells, size_y),
            near_by(7, layers, size_y),
            near_by(7, layers, size_y),
            near_by(16, cells),
            near_by(slots, 128),
        ),
        [Far(a) for a in far],
        [pltpu.VMEM(a.shape, a.dtype) for a in far] + [field, dma((len(far),))],
    )

    def exchange(one, two, col):
        return swap(one, "gx", 0), swap(two, "gx", 1), swap(col, "gy", 0), swap(col, "gy", 1)

    halo = exchange(one, two, col)
    rows = trade(rows)
    st, lt = call(
        bind(load_kernel, layers),
        "load",
        (near_by(6, cells, size_y), near_by(cells, size_y)),
        (rows, Far(soil_stress.reshape(6, cells, size_y)), Far(flat[2])),
        [vm(6, cells, size_y), field, dma((7,))],
    )
    half = number // 2
    payload = (near_by(5, layers, size_y), near_by(5, layers, size_y), near_by(16, cells))
    ext = vm(3, size_x + 4, tall, size_y)
    stack = vm(size_x + 1, tall, size_y)
    st, one, two, col, means, buoys, stiff = call(
        bind(begin_kernel, layers),
        "begin",
        (
            near_by(6, cells, size_y),
            *payload,
            near_by(5, cells, size_y),
            near_by(3, cells, size_y),
            near_by(half, width, width, dtype=stiffness.dtype),
        ),
        (vt, bt, mt, st, lt, Far(stiffness), *halo, rows),
        [
            stack,
            stack,
            stack,
            stack,
            ext,
            field,
            field,
            vm(3, cells, size_y),
            dma((1,)),
        ],
    )

    halo = exchange(one, two, col)
    maps, moved, push = call(
        bind(surface_kernel, layers),
        "surface",
        (near_by(size_x, slots, size_y), near_by(slots, 128), near_by(3, size_x, size_y)),
        (rows, vt),
    )
    chunks = 4 if number % 8 == 0 else 1
    base, drift, following = call(
        pull_kernel,
        "pull",
        (plane, plane, near_by(slots, 128)),
        (stiff, Far(stiffness), storey_drift, drift_rate, coupling, counts, owner),
        [
            vm(number, width),
            pltpu.VMEM((number - half, width, width), stiffness.dtype),
            dma((chunks,)),
        ],
    )
    push, following = lax.optimization_barrier((push, following))
    bulk = vm(5, size_x + 4, tall, size_y)
    vt, one, two, col = call(
        bind(velocity_kernel, layers),
        "velocity",
        (near_by(3, cells, size_y), *payload),
        (vt, st, buoys, *halo, push),
        [bulk, field, field, vm(3, cells, size_y)],
    )
    halo = exchange(one, two, col)
    (sent,) = call(
        bind(motion_again_kernel, layers),
        "motion_again",
        (near_by(slots, 128),),
        (vt, maps, moved, following),
    )
    vt, sent = lax.optimization_barrier((vt, sent))
    back = trade(sent)
    strips = size_x // STRIP
    st, one, two, col = call(
        bind(stress_kernel, layers),
        "stress",
        (near_by(6, cells, size_y), *payload),
        (vt, Far(st), Far(means), *halo),
        [
            vm(6, cells, size_y),
            vm(5, cells, size_y),
            ext,
            field,
            field,
            vm(3, cells, size_y),
            dma((2 * strips,)),
        ],
    )
    halo = exchange(one, two, col)
    sent, st = lax.optimization_barrier((sent, st))
    early = number // 4
    push, drift, rate, stiff = call(
        prepare_kernel,
        "prepare",
        (
            near_by(3, size_x, size_y),
            plane,
            plane,
            near_by(early, width, width, dtype=stiffness.dtype),
        ),
        (sent, back, rows, base, drift, coupling, counts, owner, Far(stiffness)),
        [dma((1,))],
    )
    tiles = size_x // TILE
    v, drift, rate = call(
        bind(finish_kernel, layers),
        "finish",
        (
            pltpu.HBM((3, layers, tiles, TILE, size_y), f32),
            shape(number, width),
            shape(number, width),
        ),
        (
            vt,
            st,
            buoys,
            *halo,
            push,
            drift,
            rate,
            counts,
            stiff,
            Far(stiffness),
        ),
        [
            vm(tiles, 3, layers, TILE, size_y),
            bulk,
            field,
            vm(3, cells, size_y),
            vm(number, width),
            pltpu.VMEM((number - early, width, width), stiffness.dtype),
            dma((3,)),
            dma((tiles,)),
        ],
        far_outs=(0,),
    )
    return v.reshape(soil_velocity.shape), drift, rate


def solution(mesh):
    both = ("gx", "gy")
    soil = P(None, None, "gx", "gy")
    cell = P(None, "gx", "gy")
    placed = (
        soil,
        soil,
        cell,
        cell,
        cell,
        P(both, None, None),
        P(both, None),
        P(both, None),
        P(both, None),
        P(both, None),
        P(both),
        P(both, None),
        P(both),
    )
    return jax.shard_map(
        body,
        mesh=mesh,
        in_specs=placed,
        out_specs=(soil, P(both, None), P(both, None)),
        check_vma=False,
    )
```
